32 devices in a mesh: dp: 16 (over z, y, core), tensor: 2 (over x).
Axes of the slice: x: 2, y: 2, z: 4, core: 2. Of those that a mesh axis runs over, the one named last changes fastest.
Arguments:
- token_codes: int32 [96, 196], P('dp'), may hold values from 0 to 8191
- mask_slots: int32 [96, 78], P('dp'), may hold values from 0 to 195, as said below
- mask_counts: int32 [96], P('dp'), may hold values from 1 to 78, as said below
- embedding: float32 [8192, 768], P('tensor', 'dp'), may hold values from -6 to 6
- emb_first: float32 [8192, 768], P('tensor', 'dp'), may hold values from -0.001953125 to 0.001953125
- emb_second: float32 [8192, 768], P('tensor', 'dp'), may hold values from 1.6302126e-08 to 6.52085e-08
- readout: float32 [8192, 768], P('tensor', 'dp')
- read_first: float32 [8192, 768], P('tensor', 'dp'), may hold values from -0.001953125 to 0.001953125
- read_second: float32 [8192, 768], P('tensor', 'dp'), may hold values from 1.6302126e-08 to 6.52085e-08
- in_proj: float32 [2, 768, 3, 768], P(None, 'dp', None, 'tensor'), may hold values from -0.21875 to 0.21875
- in_first: float32 [2, 768, 3, 768], P(None, 'dp', None, 'tensor'), may hold values from -0.005859375 to 0.005859375
- in_second: float32 [2, 768, 3, 768], P(None, 'dp', None, 'tensor'), may hold values from 1.7388933e-07 to 6.9555733e-07
- out_proj: float32 [2, 768, 768], P(None, 'dp', 'tensor'), may hold values from -0.875 to 0.875
- out_first: float32 [2, 768, 768], P(None, 'dp', 'tensor'), may hold values from -0.005859375 to 0.005859375
- out_second: float32 [2, 768, 768], P(None, 'dp', 'tensor'), may hold values from 1.7388933e-07 to 6.9555733e-07
- up_proj: float32 [2, 768, 3072], P(None, 'dp', 'tensor'), may hold values from -0.21875 to 0.21875
- up_first: float32 [2, 768, 3072], P(None, 'dp', 'tensor'), may hold values from -0.005859375 to 0.005859375
- up_second: float32 [2, 768, 3072], P(None, 'dp', 'tensor'), may hold values from 1.7388933e-07 to 6.9555733e-07
- down_proj: float32 [2, 768, 3072], P(None, 'dp', 'tensor'), may hold values from -0.109375 to 0.109375
- down_first: float32 [2, 768, 3072], P(None, 'dp', 'tensor'), may hold values from -0.005859375 to 0.005859375
- down_second: float32 [2, 768, 3072], P(None, 'dp', 'tensor'), may hold values from 1.7388933e-07 to 6.9555733e-07
- vectors: float32 [32, 768], replicated
- vec_first: float32 [32, 768], replicated, may hold values from -0.01953125 to 0.01953125
- vec_second: float32 [32, 768], replicated, may hold values from 1.565004e-06 to 6.260016e-06
- position: float32 [2, 12, 732], replicated, may hold values from -3 to 3
- pos_first: float32 [2, 12, 732], replicated, may hold values from -0.01953125 to 0.01953125
- pos_second: float32 [2, 12, 732], replicated, may hold values from 1.565004e-06 to 6.260016e-06
Outputs:
- loss_sum: float32 [], replicated
- mask_total: float32 [], replicated
- emb_master: float32 [8192, 768], P('tensor', 'dp')
- emb_mean: float32 [8192, 768], P('tensor', 'dp')
- emb_square: float32 [8192, 768], P('tensor', 'dp')
- read_master: float32 [8192, 768], P('tensor', 'dp')
- read_mean: float32 [8192, 768], P('tensor', 'dp')
- read_square: float32 [8192, 768], P('tensor', 'dp')
- in_master: float32 [2, 768, 3, 768], P(None, 'dp', None, 'tensor')
- in_mean: float32 [2, 768, 3, 768], P(None, 'dp', None, 'tensor')
- in_square: float32 [2, 768, 3, 768], P(None, 'dp', None, 'tensor')
- out_master: float32 [2, 768, 768], P(None, 'dp', 'tensor')
- out_mean: float32 [2, 768, 768], P(None, 'dp', 'tensor')
- out_square: float32 [2, 768, 768], P(None, 'dp', 'tensor')
- up_master: float32 [2, 768, 3072], P(None, 'dp', 'tensor')
- up_mean: float32 [2, 768, 3072], P(None, 'dp', 'tensor')
- up_square: float32 [2, 768, 3072], P(None, 'dp', 'tensor')
- down_master: float32 [2, 768, 3072], P(None, 'dp', 'tensor')
- down_mean: float32 [2, 768, 3072], P(None, 'dp', 'tensor')
- down_square: float32 [2, 768, 3072], P(None, 'dp', 'tensor')
- vec_master: float32 [32, 768], replicated
- vec_mean: float32 [32, 768], replicated
- vec_square: float32 [32, 768], replicated
- pos_master: float32 [2, 12, 732], replicated
- pos_mean: float32 [2, 12, 732], replicated
- pos_square: float32 [2, 12, 732], replicated
- in_copy: bfloat16 [2, 768, 3, 768], P(None, 'dp', None, 'tensor')
- out_copy: bfloat16 [2, 768, 768], P(None, 'dp', 'tensor')
- up_copy: bfloat16 [2, 768, 3072], P(None, 'dp', 'tensor')
- down_copy: bfloat16 [2, 768, 3072], P(None, 'dp', 'tensor')
The draws below stay inside these ranges and needn't reach their ends.
Inputs may be any that keep to these rules, and one draw needn't show every extreme that they name: `mask_slots`: each row names 78 different patch indices; the first mask_counts entries of a row are that sequence's masked patches, the others are unused. `mask_counts`: some sequence uses all 78 slots.
All inputs are finite; a program needn't handle non-finite values.
Results may differ from the reference program's by a relative error of at most 0.007.
The reference program's roundings to bfloat16 on the way count: a program that leaves them out, or rounds other values in their place, can miss the bound.
Values may be sent and summed in bfloat16 or wider, within the bound.
A program may use at most 256 MiB of HBM per device.

```python
import math
import jax
import jax.numpy as jnp
import numpy as np
from jax import lax

D = 768
HEADS = 12
HD = 64
FF = 3072
V = 8192
GRID = 14
LAYERS = 2
STEP = 5
SEQ_DEV = 6
NPATCH = 196
L = 197
NUM_REL = 732
MASK_MOST = 78
NVEC = 32
SEQS = 96


def draw_mask_slots(key, part):
    key = jax.random.fold_in(key, 7)
    seq_keys = jax.random.split(key, SEQS)

    def permute_one(seq_key):
        return jax.random.permutation(seq_key, NPATCH)[:MASK_MOST]
    chosen_rows = jax.vmap(permute_one)(seq_keys)
    return chosen_rows.astype(jnp.int32)


def draw_mask_counts(key, part):
    key = jax.random.fold_in(key, 11)
    lowest = (MASK_MOST + 2) // 3
    seq_order = jnp.arange(SEQS, dtype=jnp.int32)
    rising = lowest + (MASK_MOST - lowest) * seq_order // max(SEQS - 1, 1)
    spread_max = max(1, MASK_MOST // 8)
    jitter = jax.random.randint(key, (SEQS,), -spread_max, spread_max + 1)
    counts = jnp.clip(rising + jitter, 1, MASK_MOST)
    return counts.at[SEQS - 1].set(MASK_MOST).astype(jnp.int32)


def draw_readout(key, part):
    key = jax.random.fold_in(key, 5)
    row_at = jnp.arange(V, dtype=jnp.float32)[:, None] / (V - 1)
    normal_part = jax.random.normal(key, (V, D), jnp.float32)
    growth = 1.0 + 2.0 * row_at
    return normal_part * growth * D ** (-0.5)


def draw_vectors(key, part):
    key = jax.random.fold_in(key, 9)
    gain_key, noise_key = jax.random.split(key)
    row_at = jnp.arange(NVEC)[:, None]
    row_kind = row_at % 14
    tail_at = row_at - 14 * LAYERS
    inside = row_at < 14 * LAYERS
    is_gain = inside & ((row_kind == 0) | (row_kind == 5) | (row_kind == 6) | (row_kind == 9)) | (tail_at == 2)
    is_token = (tail_at == 0) | (tail_at == 1)
    gains = jnp.exp(jax.random.uniform(gain_key, (NVEC, D), jnp.float32, -0.5, 0.5))
    noise = jax.random.normal(noise_key, (NVEC, D), jnp.float32)
    return jnp.where(is_gain, gains, jnp.where(is_token, noise, 0.3 * noise))


def touch_ends(values, stream_key, smallest, high):
    index_at = [jax.random.randint(jax.random.fold_in(stream_key, axis), (), 0, length) for axis, length in enumerate(values.shape)]
    widest = values.shape.index(max(values.shape))
    beside = index_at[:widest] + [(index_at[widest] + 1) % values.shape[widest]] + index_at[widest + 1:]
    return values.at[tuple(index_at)].set(smallest).at[tuple(beside)].set(high)


def level_of(own_key, dims, cuts, low, top_value):
    def one(dim, parts):
        heights = jax.random.uniform(jax.random.fold_in(jax.random.fold_in(own_key, 6), dim), (parts,), jnp.float32, low / len(cuts), top_value / len(cuts))
        return jnp.repeat(jnp.exp(heights), dims[dim] // parts).reshape((-1,) + (1,) * (len(dims) - dim - 1))

    factor_of = one(*cuts[0])
    for cut in cuts[1:]:
        factor_of = factor_of * one(*cut)
    return factor_of


def rank_bounds(amount, skew):
    loads = [(1 << 20) // math.isqrt(standing ** skew) + 1 for standing in range(1, amount + 1)]
    width = 1 + sum(loads) // (1 << 30)
    return np.cumsum(np.array([max(1, weight // width) for weight in loads]))


def ranked_ids(key, dims, number_of, lean):
    listing = rank_bounds(number_of, lean)
    lot = jax.random.randint(jax.random.fold_in(key, 1), dims, 0, int(listing[number_of - 1]))
    grade = jnp.searchsorted(jnp.asarray(listing, jnp.int32), lot, side="right")
    return jax.random.permutation(jax.random.fold_in(key, 2), number_of)[grade].astype(jnp.int32)


def normal_values(key, extent, deviation, bound, cuts=(), held_as=jnp.bfloat16):
    level = level_of(key, extent, cuts, -0.22, 0.18) if cuts else 1.0
    values = jax.random.normal(key, extent, jnp.float32) * deviation * level
    return jnp.minimum(jnp.maximum(values, -bound), bound).astype(held_as)


def setup_inputs(seed: int = 0) -> dict:
    key_list = jax.random.split(jax.random.key(seed), 28)
    token_codes = touch_ends(ranked_ids(key_list[0], (SEQS, NPATCH), V, 2), jax.random.fold_in(key_list[0], 3), 0, V - 1).astype(jnp.int32)
    mask_slots = draw_mask_slots(jax.random.fold_in(key_list[27], 71), 0)
    mask_counts = draw_mask_counts(jax.random.fold_in(key_list[27], 71), 0)
    embedding = normal_values(key_list[3], (V, D), 1.0, 6.0, ((0, 2), (1, 16)), jnp.float32)
    emb_first = normal_values(key_list[4], (V, D), ((SEQS * MASK_MOST * V) ** -0.5), 0.001953125, ((0, 2), (1, 16)), jnp.float32)
    emb_second = jnp.clip(jnp.exp(math.log(6.520850348579188e-08) - 1.3862944 * jax.random.uniform(key_list[5], (V, D), jnp.float32) ** level_of(key_list[5], (V, D), ((0, 2), (1, 16)), -0.2, 0.2)), 1.630212587144797e-08, 6.520850348579188e-08)
    readout = draw_readout(jax.random.fold_in(key_list[27], 71), 0)
    read_first = normal_values(key_list[7], (V, D), ((SEQS * MASK_MOST * V) ** -0.5), 0.001953125, ((0, 2), (1, 16)), jnp.float32)
    read_second = jnp.clip(jnp.exp(math.log(6.520850348579188e-08) - 1.3862944 * jax.random.uniform(key_list[8], (V, D), jnp.float32) ** level_of(key_list[8], (V, D), ((0, 2), (1, 16)), -0.2, 0.2)), 1.630212587144797e-08, 6.520850348579188e-08)
    in_proj = normal_values(key_list[9], (LAYERS, D, 3, D), D ** -0.5, 0.21875, ((1, 16), (3, 2)), jnp.float32)
    in_first = normal_values(key_list[10], (LAYERS, D, 3, D), ((SEQS * MASK_MOST * D) ** -0.5), 0.005859375, ((1, 16), (3, 2)), jnp.float32)
    in_second = jnp.clip(jnp.exp(math.log(6.955573326195008e-07) - 1.3862944 * jax.random.uniform(key_list[11], (LAYERS, D, 3, D), jnp.float32) ** level_of(key_list[11], (LAYERS, D, 3, D), ((1, 16), (3, 2)), -0.2, 0.2)), 1.738893331548752e-07, 6.955573326195008e-07)
    out_proj = normal_values(key_list[12], (LAYERS, D, D), (D // 16) ** -0.5, 0.875, ((1, 16), (2, 2)), jnp.float32)
    out_first = normal_values(key_list[13], (LAYERS, D, D), ((SEQS * MASK_MOST * D) ** -0.5), 0.005859375, ((1, 16), (2, 2)), jnp.float32)
    out_second = jnp.clip(jnp.exp(math.log(6.955573326195008e-07) - 1.3862944 * jax.random.uniform(key_list[14], (LAYERS, D, D), jnp.float32) ** level_of(key_list[14], (LAYERS, D, D), ((1, 16), (2, 2)), -0.2, 0.2)), 1.738893331548752e-07, 6.955573326195008e-07)
    up_proj = normal_values(key_list[15], (LAYERS, D, FF), D ** -0.5, 0.21875, ((1, 16), (2, 2)), jnp.float32)
    up_first = normal_values(key_list[16], (LAYERS, D, FF), ((SEQS * MASK_MOST * D) ** -0.5), 0.005859375, ((1, 16), (2, 2)), jnp.float32)
    up_second = jnp.clip(jnp.exp(math.log(6.955573326195008e-07) - 1.3862944 * jax.random.uniform(key_list[17], (LAYERS, D, FF), jnp.float32) ** level_of(key_list[17], (LAYERS, D, FF), ((1, 16), (2, 2)), -0.2, 0.2)), 1.738893331548752e-07, 6.955573326195008e-07)
    down_proj = normal_values(key_list[18], (LAYERS, D, FF), FF ** -0.5, 0.109375, ((1, 16), (2, 2)), jnp.float32)
    down_first = normal_values(key_list[19], (LAYERS, D, FF), ((SEQS * MASK_MOST * D) ** -0.5), 0.005859375, ((1, 16), (2, 2)), jnp.float32)
    down_second = jnp.clip(jnp.exp(math.log(6.955573326195008e-07) - 1.3862944 * jax.random.uniform(key_list[20], (LAYERS, D, FF), jnp.float32) ** level_of(key_list[20], (LAYERS, D, FF), ((1, 16), (2, 2)), -0.2, 0.2)), 1.738893331548752e-07, 6.955573326195008e-07)
    vectors = draw_vectors(jax.random.fold_in(key_list[27], 71), 0)
    vec_first = normal_values(key_list[22], (NVEC, D), (3 * (SEQS * MASK_MOST * D) ** -0.5), 0.01953125, (), jnp.float32)
    vec_second = jnp.clip(jnp.exp(jax.random.uniform(key_list[23], (NVEC, D), jnp.float32, math.log(1.5650040268155863e-06), math.log(6.260016107262345e-06))), 1.5650040268155863e-06, 6.260016107262345e-06)
    position = normal_values(key_list[24], (LAYERS, HEADS, NUM_REL), 0.5, 3.0, (), jnp.float32)
    pos_first = normal_values(key_list[25], (LAYERS, HEADS, NUM_REL), (3 * (SEQS * MASK_MOST * D) ** -0.5), 0.01953125, (), jnp.float32)
    pos_second = jnp.clip(jnp.exp(jax.random.uniform(key_list[26], (LAYERS, HEADS, NUM_REL), jnp.float32, math.log(1.5650040268155863e-06), math.log(6.260016107262345e-06))), 1.5650040268155863e-06, 6.260016107262345e-06)
    return dict(token_codes=token_codes, mask_slots=mask_slots, mask_counts=mask_counts, embedding=embedding, emb_first=emb_first, emb_second=emb_second, readout=readout, read_first=read_first, read_second=read_second, in_proj=in_proj, in_first=in_first, in_second=in_second, out_proj=out_proj, out_first=out_first, out_second=out_second, up_proj=up_proj, up_first=up_first, up_second=up_second, down_proj=down_proj, down_first=down_first, down_second=down_second, vectors=vectors, vec_first=vec_first, vec_second=vec_second, position=position, pos_first=pos_first, pos_second=pos_second)


beta_one = 0.5
beta_two = 0.5
adam_eps = 1e-08
rate_matrix = 0.05
rate_vector = 0.3
rate_table = 0.5
decay_matrix = 0.05
norm_eps = 1e-06
highest = lax.Precision.HIGHEST

@jax.custom_vjp
def low(v):
    return lax.optimization_barrier(v.astype(jnp.bfloat16)).astype(jnp.float32)

@jax.custom_vjp
def low_back(v):
    return v

def low_keep(v):
    return (low(v), None)

def low_pass(kept, grad):
    return (grad,)

def back_keep(v):
    return (v, None)

def back_low(kept, grad):
    return (low(grad),)
low.defvjp(low_keep, low_pass)
low_back.defvjp(back_keep, back_low)

def rounded(value):
    return low(low_back(value))

def layer_norm(values, gain_row, shift_row):
    center = values - lax.optimization_barrier(jnp.mean(values, axis=-1, keepdims=True))
    spread_sq = lax.optimization_barrier(jnp.mean(center * center, axis=-1, keepdims=True))
    return center * lax.rsqrt(spread_sq + norm_eps) * gain_row + shift_row

def gelu_exact(values):
    return jax.nn.gelu(values, approximate=False)

def relative_table(grid_side):
    coords = np.stack(np.meshgrid(np.arange(grid_side), np.arange(grid_side), indexing='ij')).reshape(2, -1)
    offsets = coords[:, :, None] - coords[:, None, :] + grid_side - 1
    inner_idx = offsets[0] * (2 * grid_side - 1) + offsets[1]
    cell_count = (2 * grid_side - 1) ** 2
    result = np.zeros((grid_side * grid_side + 1, grid_side * grid_side + 1), np.int32)
    result[1:, 1:] = inner_idx
    result[0, 1:] = cell_count
    result[1:, 0] = cell_count + 1
    result[0, 0] = cell_count + 2
    return result

def layer_step(stream, matrices, vectors, position, layer_at, lookup):
    w_in, w_out, w_up, w_down = matrices
    first_row = layer_at * 14
    row_count = stream.shape[0]
    seq_count = row_count // L
    normed = low(layer_norm(stream, vectors[first_row], vectors[first_row + 1]))
    mixed_in = jnp.dot(normed, w_in.reshape(D, 3 * D), precision=highest).reshape(row_count, 3, D)
    offset = jnp.stack([vectors[first_row + 2], jnp.zeros((D,), jnp.float32), vectors[first_row + 3]])
    triple = rounded(mixed_in + offset).reshape(seq_count, L, 3, HEADS, HD)
    queries, key_rows, values = (triple[:, :, 0], triple[:, :, 1], triple[:, :, 2])
    scores = jnp.einsum('bqhe,bkhe->bhqk', queries, key_rows, precision=highest) * HD ** (-0.5)
    scores = low_back(scores + position[layer_at][:, lookup])
    weights = low(jax.nn.softmax(scores, axis=-1))
    attended = rounded(jnp.einsum('bhqk,bkhe->bqhe', weights, values, precision=highest).reshape(row_count, D))
    branch = low_back(jnp.dot(attended, w_out.T, precision=highest))
    stream = stream + vectors[first_row + 5] * (branch + vectors[first_row + 4])
    normed = low(layer_norm(stream, vectors[first_row + 6], vectors[first_row + 7]))
    hidden_pre = low_back(jnp.dot(normed, w_up, precision=highest) + vectors[first_row + 10:first_row + 14].reshape(FF))
    hidden = low(gelu_exact(hidden_pre))
    branch = low_back(jnp.dot(hidden, w_down.T, precision=highest))
    return stream + vectors[first_row + 9] * (branch + vectors[first_row + 8])

def block_loss(params, codes_block, slots_block, counts_block, lookup):
    embedding, readout, w_in, w_out, w_up, w_down, vectors, position = params
    seq_count = codes_block.shape[0]
    live_slot = jnp.arange(MASK_MOST)[None, :] < counts_block[:, None]
    masked = jnp.any((slots_block[:, :, None] == jnp.arange(NPATCH)[None, None, :]) & live_slot[:, :, None], axis=1)
    tail_row = LAYERS * 14
    looked = low(embedding)[codes_block]
    patches = jnp.where(masked[:, :, None], vectors[tail_row + 1], looked)
    leading = jnp.broadcast_to(vectors[tail_row], (seq_count, 1, D))
    stream = low_back(jnp.concatenate([leading, patches], axis=1).reshape(seq_count * L, D))
    for layer_at in range(LAYERS):
        matrices = (low(w_in[layer_at]), low(w_out[layer_at]), low(w_up[layer_at]), low(w_down[layer_at]))
        stream = layer_step(stream, matrices, vectors, position, layer_at, lookup)
    pick_rows = (jnp.arange(seq_count)[:, None] * L + 1 + slots_block).reshape(-1)
    final_rows = low(layer_norm(stream[pick_rows], vectors[tail_row + 2], vectors[tail_row + 3]))
    logits = low_back(jnp.dot(final_rows, low(readout).T, precision=highest))
    target = jnp.take_along_axis(codes_block, slots_block, axis=1).reshape(-1)
    picked = jnp.take_along_axis(logits, target[:, None], axis=1)[:, 0]
    losses = jax.nn.logsumexp(logits, axis=-1) - picked
    return jnp.sum(losses * live_slot.reshape(-1).astype(jnp.float32))

def adamw_update(master, gradient, first_mom, second_mom, step_rate, decay_rate):
    first_mom = beta_one * first_mom + (1.0 - beta_one) * gradient
    second_mom = beta_two * second_mom + (1.0 - beta_two) * gradient * gradient
    step_dir = first_mom / (1.0 - beta_one ** STEP) / (jnp.sqrt(second_mom / (1.0 - beta_two ** STEP)) + adam_eps)
    return (master - step_rate * (step_dir + decay_rate * master), first_mom, second_mom)

def reference(token_codes, mask_slots, mask_counts, embedding, emb_first, emb_second, readout, read_first, read_second, in_proj, in_first, in_second, out_proj, out_first, out_second, up_proj, up_first, up_second, down_proj, down_first, down_second, vectors, vec_first, vec_second, position, pos_first, pos_second):
    lookup = jnp.asarray(relative_table(GRID)).astype(jnp.int32)
    mask_total = jnp.sum(mask_counts.astype(jnp.float32))
    blocks = SEQS // SEQ_DEV
    stacked = (token_codes.reshape(blocks, SEQ_DEV, NPATCH), mask_slots.reshape(blocks, SEQ_DEV, MASK_MOST), mask_counts.reshape(blocks, SEQ_DEV))

    def whole_loss(params):

        def one_block(params_in, codes_block, slots_block, counts_block):
            return block_loss(params_in, codes_block, slots_block, counts_block, lookup)
        checked = jax.checkpoint(one_block)

        def scan_step(carried, block_item):
            return (carried + checked(params, block_item[0], block_item[1], block_item[2]), None)
        summed, _unused = lax.scan(scan_step, jnp.zeros((), jnp.float32), stacked)
        return summed
    params = (embedding, readout, in_proj, out_proj, up_proj, down_proj, vectors, position)
    loss_sum, pull_back = jax.vjp(whole_loss, params)
    grads_all = pull_back(jnp.ones((), jnp.float32) / mask_total)[0]
    emb_new = adamw_update(embedding, grads_all[0], emb_first, emb_second, rate_table, decay_matrix)
    read_new = adamw_update(readout, grads_all[1], read_first, read_second, rate_matrix, decay_matrix)
    in_new = adamw_update(in_proj, grads_all[2], in_first, in_second, rate_matrix, decay_matrix)
    out_new = adamw_update(out_proj, grads_all[3], out_first, out_second, rate_matrix, decay_matrix)
    up_new = adamw_update(up_proj, grads_all[4], up_first, up_second, rate_matrix, decay_matrix)
    down_new = adamw_update(down_proj, grads_all[5], down_first, down_second, rate_matrix, decay_matrix)
    vec_new = adamw_update(vectors, grads_all[6], vec_first, vec_second, rate_vector, 0.0)
    pos_new = adamw_update(position, grads_all[7], pos_first, pos_second, rate_vector, 0.0)
    return (loss_sum, mask_total, emb_new[0], emb_new[1], emb_new[2], read_new[0], read_new[1], read_new[2], in_new[0], in_new[1], in_new[2], out_new[0], out_new[1], out_new[2], up_new[0], up_new[1], up_new[2], down_new[0], down_new[1], down_new[2], vec_new[0], vec_new[1], vec_new[2], pos_new[0], pos_new[1], pos_new[2], in_new[0].astype(jnp.bfloat16), out_new[0].astype(jnp.bfloat16), up_new[0].astype(jnp.bfloat16), down_new[0].astype(jnp.bfloat16))
```

```python
import functools
import math

import jax
import jax.numpy as jnp
import numpy as np
from jax import lax
from jax.experimental import pallas as pl
from jax.experimental.pallas import tpu as pltpu
from jax.sharding import PartitionSpec as P

HEADS = 12
HD = 64
STEP = 5

beta_one = 0.5
beta_two = 0.5
adam_eps = 1e-08
rate_matrix = 0.05
rate_vector = 0.3
rate_table = 0.5
decay_matrix = 0.05
norm_eps = 1e-06
F32 = jnp.float32
BF16 = jnp.bfloat16
BIG = -1e30
ROOT_HALF = 0.5**0.5


def dot_nn(a, b):
    return lax.dot_general(a, b, (((1,), (0,)), ((), ())), preferred_element_type=F32)


def dot_nt(a, b):
    return lax.dot_general(a, b, (((1,), (1,)), ((), ())), preferred_element_type=F32)


def dot_tn(a, b):
    return lax.dot_general(a, b, (((0,), (0,)), ((), ())), preferred_element_type=F32)


def norm_parts(values):
    center = values - jnp.mean(values, axis=-1, keepdims=True)
    spread_sq = jnp.mean(center * center, axis=-1, keepdims=True)
    scale = lax.rsqrt(spread_sq + norm_eps)
    return center * scale, scale


def norm_back(grad, values, gain):
    unit, scale = norm_parts(values)
    inner = grad * gain
    back = scale * (
        inner
        - jnp.mean(inner, axis=-1, keepdims=True)
        - unit * jnp.mean(inner * unit, axis=-1, keepdims=True)
    )
    return back, jnp.sum(grad * unit, axis=0), jnp.sum(grad, axis=0)


def norm_back(grad, values, gain):
    unit, scale = norm_parts(values)
    inner = grad * gain
    back = scale * (
        inner
        - jnp.mean(inner, axis=-1, keepdims=True)
        - unit * jnp.mean(inner * unit, axis=-1, keepdims=True)
    )
    return back, jnp.sum(grad * unit, axis=0), jnp.sum(grad, axis=0)


ROWS = 48


def row_loop(rows, body):
    def step(i, _):
        body(pl.ds(pl.multiple_of(i * ROWS, ROWS), ROWS))
        return 0

    lax.fori_loop(0, rows // ROWS, step, 0)


def lane_low():
    return lax.broadcasted_iota(jnp.int32, (1, 2 * HD), 1) < HD


def halves(pair):
    low = lane_low()
    zero = jnp.zeros_like(pair)
    return jnp.where(low, pair, zero), jnp.where(low, zero, pair)


def softmax_rows(scores):
    e = jnp.exp(scores - jnp.max(scores, axis=-1, keepdims=True))
    return e * (1.0 / jnp.sum(e, axis=-1, keepdims=True))


def attention_loop(seqs, lp, half, body):
    pairs = half // (2 * HD)
    for t in range(2):

        def step(s, _):
            rows = pl.ds(pl.multiple_of(s * lp, 16), lp)
            for hp in range(pairs):
                body(t, s, rows, hp * 2 * HD, t * 2 * pairs + 2 * hp)
            return 0

        lax.fori_loop(0, seqs, step, 0)


def forward_kernel(
    seqs, x, w_attn, w_up, w_down, vec, bias, out, y1, qkv, att, r, middle, y2, pre, hid, z
):
    rows, d = x.shape
    half = d // 2
    lp = rows // seqs
    ff = w_up.shape[-1]
    tile = ff // 3

    def first_norm(at):
        unit, _ = norm_parts(x[at, :])
        y1[at, :] = (unit * vec[0:1, :] + vec[1:2, :]).astype(BF16)

    row_loop(rows, first_norm)
    for t in range(2):
        for w in range(3):
            mixed = dot_nn(y1[...], w_attn[t, :, w * half : (w + 1) * half])
            if w != 1:
                row = 2 if w == 0 else 3
                mixed = mixed + vec[row : row + 1, t * half : (t + 1) * half]
            qkv[t, :, w * half : (w + 1) * half] = mixed.astype(BF16)

    def attend(t, s, at, col, head):
        q = qkv[t, at, pl.ds(col, 2 * HD)]
        k = qkv[t, at, pl.ds(half + col, 2 * HD)]
        v = qkv[t, at, pl.ds(2 * half + col, 2 * HD)]
        found = []
        for i, part in enumerate(halves(q)):
            scores = dot_nt(part, k) * HD**-0.5 + bias[head + i]
            found.append(dot_nn(softmax_rows(scores).astype(BF16), v))
        att[t, at, pl.ds(col, 2 * HD)] = jnp.where(lane_low(), found[0], found[1]).astype(BF16)

    attention_loop(seqs, lp, half, attend)
    r[...] = dot_nt(att[0], w_attn[0, :, 3 * half :])
    r[...] += dot_nt(att[1], w_attn[1, :, 3 * half :])

    def second_norm(at):
        here = x[at, :] + vec[5:6, :] * (r[at, :] + vec[4:5, :])
        middle[at, :] = here
        unit, _ = norm_parts(here)
        y2[at, :] = (unit * vec[6:7, :] + vec[7:8, :]).astype(BF16)

    row_loop(rows, second_norm)
    per = 2 * ff // d
    for t in range(2):
        for j in range(3):
            cols = slice(j * tile, (j + 1) * tile)
            a = dot_nn(y2[...], w_up[t, :, cols])
            off = t * ff + j * tile
            shift = jnp.concatenate(
                [
                    vec[10 + o // d : 11 + o // d, o % d : o % d + half // 3]
                    for o in range(off, off + tile, half // 3)
                ],
                axis=1,
            )
            a = a + shift
            pre[t, :, cols] = a
            h = (0.5 * a * (1.0 + lax.erf(a * ROOT_HALF))).astype(BF16)
            hid[t, :, cols] = h
            part = dot_nt(h, w_down[t, :, cols])
            if t == 0 and j == 0:
                z[...] = part
            else:
                z[...] += part

    def finish(at):
        out[at, :] = middle[at, :] + vec[9:10, :] * (z[at, :] + vec[8:9, :])

    row_loop(rows, finish)


def whole():
    return pl.BlockSpec(memory_space=pltpu.VMEM)


def third(shape, k):
    return pl.BlockSpec((shape[0], shape[1], shape[2] // 3), lambda *_: (0, 0, k))


def big_call(kernel, ins, specs, outs, scratch, name, flops):
    return pl.pallas_call(
        kernel,
        out_shape=outs,
        grid=(1,),
        in_specs=specs,
        out_specs=[
            pl.BlockSpec(o.shape, functools.partial(lambda n, *_: (0,) * n, len(o.shape)))
            for o in outs
        ],
        scratch_shapes=scratch,
        compiler_params=pltpu.CompilerParams(vmem_limit_bytes=60 * 2**20),
        cost_estimate=pl.CostEstimate(flops=flops, bytes_accessed=4 * 10**7, transcendentals=0),
        name=name,
    )(*ins)


def full(a):
    return pl.BlockSpec(a.shape, functools.partial(lambda n, *_: (0,) * n, len(a.shape)))


def forward_layer(x, weights, vec, bias, seqs):
    rows, d = x.shape
    half, ff = d // 2, weights.shape[2] // 3
    s = jax.ShapeDtypeStruct
    outs = [
        s((rows, d), F32),
        s((rows, d), BF16),
        s((2, rows, 3 * half), BF16),
        s((2, rows, half), BF16),
        s((rows, d), F32),
        s((rows, d), F32),
        s((rows, d), BF16),
        s((2, rows, ff), F32),
        s((2, rows, ff), BF16),
        s((rows, d), F32),
    ]
    specs = [full(x)] + [third(weights.shape, k) for k in range(3)] + [full(vec), full(bias)]
    ins = [x, weights, weights, weights, vec, bias]
    found = big_call(
        functools.partial(forward_kernel, seqs), ins, specs, outs, [], "forward", 10**10
    )
    return found[0], (x,) + tuple(found[1:])


def norm_back_rows(grad, values, gain):
    unit, scale = norm_parts(values)
    inner = grad * gain
    back = scale * (
        inner
        - jnp.mean(inner, axis=-1, keepdims=True)
        - unit * jnp.mean(inner * unit, axis=-1, keepdims=True)
    )
    return back, unit


def col_sum(v):
    return jnp.sum(v, axis=0, keepdims=True)


def feed_back_kernel(
    g, z, hid, pre, middle, y2, vec, w_up, w_down, gm, g_up, g_down, sums, upb, dz, dy2
):
    rows, d = g.shape
    ff = w_up.shape[-1]
    tile = ff // 3
    sums[...] = jnp.zeros_like(sums)

    def first(at):
        here = g[at, :]
        scaled = here * vec[9:10, :]
        dz[at, :] = scaled.astype(BF16)
        sums[0:1, :] += col_sum(scaled)
        sums[1:2, :] += col_sum(here * (z[at, :] + vec[8:9, :]))

    row_loop(rows, first)
    for t in range(2):
        for j in range(3):
            cols = slice(j * tile, (j + 1) * tile)
            dh = dot_nn(dz[...], w_down[t, :, cols])
            a = pre[t, :, cols]
            slope = 0.5 * (1.0 + lax.erf(a * ROOT_HALF))
            slope = slope + a * (jnp.exp(-0.5 * a * a) * (2 * math.pi) ** -0.5)
            da = (dh * slope).astype(BF16)
            upb[t : t + 1, cols] = col_sum(da.astype(F32))
            g_down[t, :, cols] = dot_tn(dz[...], hid[t, :, cols]).astype(BF16)
            g_up[t, :, cols] = dot_tn(y2[...], da).astype(BF16)
            part = dot_nt(da, w_up[t, :, cols])
            if t == 0 and j == 0:
                dy2[...] = part
            else:
                dy2[...] += part

    def last(at):
        grad = dy2[at, :]
        back, unit = norm_back_rows(grad, middle[at, :], vec[6:7, :])
        gm[at, :] = g[at, :] + back
        sums[2:3, :] += col_sum(grad * unit)
        sums[3:4, :] += col_sum(grad)

    row_loop(rows, last)


def attn_back_kernel(
    seqs, gm, r, x, y1, qkv, att, bias, vec, w_attn, g, g_attn, sums, rel, dr, do, dqkv, dy1
):
    rows, d = gm.shape
    half = d // 2
    lp = rows // seqs
    sums[...] = jnp.zeros_like(sums)

    def first(at):
        here = gm[at, :]
        scaled = here * vec[5:6, :]
        dr[at, :] = scaled.astype(BF16)
        sums[0:1, :] += col_sum(scaled)
        sums[1:2, :] += col_sum(here * (r[at, :] + vec[4:5, :]))

    row_loop(rows, first)
    for t in range(2):
        g_attn[t, :, 3 * half :] = dot_tn(dr[...], att[t]).astype(BF16)
        do[t] = dot_nn(dr[...], w_attn[t, :, 3 * half :]).astype(BF16)

    def attend(t, s, at, col, head):
        q = qkv[t, at, pl.ds(col, 2 * HD)]
        k = qkv[t, at, pl.ds(half + col, 2 * HD)]
        v = qkv[t, at, pl.ds(2 * half + col, 2 * HD)]
        o = do[t, at, pl.ds(col, 2 * HD)]
        dq, dk, dv = [], [], []
        for i, (q_part, o_part) in enumerate(zip(halves(q), halves(o))):
            p = softmax_rows(dot_nt(q_part, k) * HD**-0.5 + bias[head + i])
            dp = dot_nt(o_part, v)
            ds = (p * (dp - jnp.sum(p * dp, axis=-1, keepdims=True))).astype(BF16)
            wide = ds.astype(F32)
            rel[head + i] = jnp.where(s == 0, wide, rel[head + i] + wide)
            dq.append(dot_nn(ds, k))
            dk.append(dot_tn(ds, q))
            dv.append(dot_tn(p.astype(BF16), o))
        low = lane_low()
        for w, pair in enumerate((dq, dk, dv)):
            value = jnp.where(low, pair[0], pair[1])
            if w < 2:
                value = value * HD**-0.5
            dqkv[t, at, pl.ds(w * half + col, 2 * HD)] = value.astype(BF16)

    attention_loop(seqs, lp, half, attend)
    for t in range(2):
        for w in range(3):
            cols = slice(w * half, (w + 1) * half)
            part = dqkv[t, :, cols]
            if w != 1:
                row = 2 if w == 0 else 3
                sums[row : row + 1, t * half : (t + 1) * half] = col_sum(part.astype(F32))
            g_attn[t, :, cols] = dot_tn(y1[...], part).astype(BF16)
            more = dot_nt(part, w_attn[t, :, cols])
            if t == 0 and w == 0:
                dy1[...] = more
            else:
                dy1[...] += more

    def last(at):
        grad = dy1[at, :]
        back, unit = norm_back_rows(grad, x[at, :], vec[0:1, :])
        g[at, :] = gm[at, :] + back
        sums[4:5, :] += col_sum(grad * unit)
        sums[5:6, :] += col_sum(grad)

    row_loop(rows, last)


def backward_layer(g, saved, weights, vec, bias, seqs):
    x, y1, qkv, att, r, middle, y2, pre, hid, z = saved
    rows, d = x.shape
    half, ff = d // 2, weights.shape[2] // 3
    s = jax.ShapeDtypeStruct
    part = s((2, d, ff), BF16)
    ins = [g, z, hid, pre, middle, y2, vec, weights, weights]
    gm, g_up, g_down, low_sums, upb = big_call(
        feed_back_kernel,
        ins,
        [full(a) for a in ins[:7]] + [third(weights.shape, 1), third(weights.shape, 2)],
        [s((rows, d), F32), part, part, s((8, d), F32), s((8, ff), F32)],
        [pltpu.VMEM((rows, d), BF16), pltpu.VMEM((rows, d), F32)],
        "feed_back",
        12 * 10**9,
    )
    ins = [gm, r, x, y1, qkv, att, bias, vec, weights]
    g, g_attn, top_sums, rel = big_call(
        functools.partial(attn_back_kernel, seqs),
        ins,
        [full(a) for a in ins[:8]] + [third(weights.shape, 0)],
        [s((rows, d), F32), part, s((8, d), F32), s(bias.shape, F32)],
        [
            pltpu.VMEM((rows, d), BF16),
            pltpu.VMEM((2, rows, half), BF16),
            pltpu.VMEM((2, rows, 3 * half), BF16),
            pltpu.VMEM((rows, d), F32),
        ],
        "attn_back",
        6 * 10**9,
    )
    vec_grad = jnp.concatenate(
        [
            top_sums[4:6],
            top_sums[2:4],
            top_sums[0:2],
            low_sums[2:4],
            low_sums[0:2],
            upb[:2].reshape(4, d),
        ],
        axis=0,
    )
    return g, (g_attn, g_up, g_down), vec_grad, rel


def strip_constant(side):
    width = 2 * side - 1
    wide = -(-(width * side) // 128) * 128
    out = np.zeros((width * width, 16, wide), np.float32)
    for c in range(side):
        for k in range(width):
            for e in range(side):
                out[width * k + side - 1 - c + e, c, k * side + e] = 1.0
    return out.reshape(width * width, 16 * wide), wide


def split_three(v):
    high = lax.reduce_precision(v, 8, 7)
    rest = v - high
    mid = lax.reduce_precision(rest, 8, 7)
    return jnp.concatenate([high, mid, rest - mid], axis=0).astype(BF16)


def add_three(v):
    n = v.shape[0] // 3
    return v[:n] + v[n : 2 * n] + v[2 * n :]


def expand_kernel(side, strips, ends, out):
    lp = out.shape[1]
    wide = strips.shape[2]
    tokens = side * side + 1
    a = strips[0]
    lane = lax.broadcasted_iota(jnp.int32, (1, lp), 1)
    row_end, col_end, corner = ends[0, 0:1, 0:1], ends[0, 0:1, 1:2], ends[0, 0:1, 2:3]
    top = jnp.where(lane == 0, corner, row_end)
    out[0, 0:1, :] = jnp.where(lane < tokens, top, BIG)
    for r in range(side):
        shift = (side - 1 - r) * side - 1
        moved = pltpu.roll(a, (wide - shift) % wide, 1)[:side, :lp]
        moved = jnp.where(lane == 0, col_end, moved)
        out[0, 1 + r * side : 1 + (r + 1) * side, :] = jnp.where(lane < tokens, moved, BIG)
    tail = jnp.where(lane < tokens, 0.0, BIG)
    out[0, tokens:, :] = jnp.broadcast_to(tail, (lp - tokens, lp))


def expand_bias(position, side, lp):
    layers, heads, entries = position.shape
    flat = position.reshape(layers * heads, entries)
    hot, wide = strip_constant(side)
    cells = hot.shape[0]
    strips = add_three(dot_nn(split_three(flat[:, :cells][:, ::-1]), jnp.asarray(hot, BF16)))
    strips = strips.reshape(layers * heads, 16, wide)
    ends = jnp.pad(flat[:, cells:], ((0, 0), (0, 125)))[:, None, :]
    out = pl.pallas_call(
        functools.partial(expand_kernel, side),
        out_shape=jax.ShapeDtypeStruct((layers * heads, lp, lp), F32),
        grid=(layers * heads,),
        in_specs=[
            pl.BlockSpec((1, 16, wide), lambda i: (i, 0, 0)),
            pl.BlockSpec((1, 1, 128), lambda i: (i, 0, 0)),
        ],
        out_specs=pl.BlockSpec((1, lp, lp), lambda i: (i, 0, 0)),
        name="expand",
    )(strips, ends)
    return out.reshape(layers, heads, lp, lp)


def fold_kernel(side, grads, strips, ends):
    lp = grads.shape[1]
    wide = strips.shape[2]
    tokens = side * side + 1
    lane = lax.broadcasted_iota(jnp.int32, (1, lp), 1)
    total = jnp.zeros((16, wide), F32)
    for r in range(side):
        shift = (side - 1 - r) * side - 1
        part = jnp.where(lane == 0, 0.0, grads[0, 1 + r * side : 1 + (r + 1) * side, :])
        part = jnp.concatenate([part, jnp.zeros((16 - side, lp), F32)], axis=0)
        part = jnp.concatenate([part, jnp.zeros((16, wide - lp), F32)], axis=1)
        total = total + pltpu.roll(part, shift % wide, 1)
    strips[0] = total
    corner = grads[0, 0:1, 0:1]
    row_end = jnp.sum(grads[0, 0:1, :], axis=1, keepdims=True) - corner
    col_end = jnp.sum(grads[0, 1:tokens, 0:1], axis=0, keepdims=True)
    out_lane = lax.broadcasted_iota(jnp.int32, (1, 128), 1)
    ends[0] = jnp.where(
        out_lane == 0, row_end, jnp.where(out_lane == 1, col_end, jnp.where(out_lane == 2, corner, 0.0))
    )


def fold_bias(grads, side):
    layers, heads, lp, _ = grads.shape
    hot, wide = strip_constant(side)
    n = layers * heads
    strips, ends = pl.pallas_call(
        functools.partial(fold_kernel, side),
        out_shape=[
            jax.ShapeDtypeStruct((n, 16, wide), F32),
            jax.ShapeDtypeStruct((n, 1, 128), F32),
        ],
        grid=(n,),
        in_specs=[pl.BlockSpec((1, lp, lp), lambda i: (i, 0, 0))],
        out_specs=[
            pl.BlockSpec((1, 16, wide), lambda i: (i, 0, 0)),
            pl.BlockSpec((1, 1, 128), lambda i: (i, 0, 0)),
        ],
        name="fold",
    )(grads.reshape(n, lp, lp))
    cells = add_three(dot_nt(split_three(strips.reshape(n, 16 * wide)), jnp.asarray(hot, BF16)))
    flat = jnp.concatenate([cells[:, ::-1], ends[:, 0, :3]], axis=1)
    return flat.reshape(layers, heads, -1)


def adamw_update(master, gradient, first_mom, second_mom, step_rate, decay_rate):
    first_mom = beta_one * first_mom + (1.0 - beta_one) * gradient
    second_mom = beta_two * second_mom + (1.0 - beta_two) * gradient * gradient
    step_dir = (
        first_mom
        / (1.0 - beta_one**STEP)
        / (jnp.sqrt(second_mom / (1.0 - beta_two**STEP)) + adam_eps)
    )
    return (master - step_rate * (step_dir + decay_rate * master), first_mom, second_mom)


def pack_layer(in_proj, out_proj, up_proj, down_proj):
    return jnp.concatenate(
        [in_proj[:, 0], in_proj[:, 1], in_proj[:, 2], out_proj, up_proj, down_proj], axis=1
    )


MESH = pl.DeviceIdType.MESH


def place():
    dp = lax.axis_index("dp")
    return lax.axis_index("tensor"), dp // 4, lax.rem(dp // 2, 2), lax.rem(dp, 2)


def at(x, z, y, c):
    return ((z * 2 + y) * 2 + c, x)


def near(v, step, size):
    return lax.rem(v + step, size)


def greet(peers):
    barrier = pltpu.get_barrier_semaphore()
    for peer in peers:
        pl.semaphore_signal(barrier, inc=1, device_id=peer, device_id_type=MESH)
    pl.semaphore_wait(barrier, len(peers))


def gather_kernel(wide, *refs):
    n = len(wide)
    srcs, dsts = refs[:n], refs[n : 2 * n]
    own_sem, send_sem, recv_sem = refs[2 * n :]
    x, z, y, c = place()
    peer_x, peer_y, peer_c = at(1 - x, z, y, c), at(x, z, 1 - y, c), at(x, z, y, 1 - c)
    up, down = at(x, jnp.minimum(z + 1, 3), y, c), at(x, jnp.maximum(z - 1, 0), y, c)
    barrier = pltpu.get_barrier_semaphore()
    for peer in (peer_x, peer_y, peer_c):
        pl.semaphore_signal(barrier, inc=1, device_id=peer, device_id_type=MESH)

    @pl.when(z < 3)
    def _():
        pl.semaphore_signal(barrier, inc=1, device_id=up, device_id_type=MESH)

    @pl.when(z > 0)
    def _():
        pl.semaphore_signal(barrier, inc=1, device_id=down, device_id_type=MESH)

    pl.semaphore_wait(barrier, 3 + jnp.where(z < 3, 1, 0) + jnp.where(z > 0, 1, 0))

    def slot(i, ox, oz, oy, oc):
        ref = dsts[i]
        dp = (oz * 2 + oy) * 2 + oc
        return ref.at[ox, dp] if wide[i] else ref.at[dp]

    Z, Y, X, C, Z2 = 0, 4, 8, 16, 32

    def make(i, src, origin, way, peer, two=False):
        ox, oz, oy, oc = origin
        if way == Z:
            k = Z + oz
        elif way == Y:
            k = Y + oz
        elif way == X:
            k = X + oy * 4 + oz
        else:
            k = C + (ox * 2 + oy) * 4 + oz
        return pltpu.make_async_remote_copy(
            src_ref=src,
            dst_ref=slot(i, *origin),
            send_sem=send_sem.at[i, Z2 if two else k],
            recv_sem=recv_sem.at[i, k],
            device_id=peer,
            device_id_type=MESH,
        )

    own = (x, z, y, c)
    locals_ = []
    for i in range(n):
        copy = pltpu.make_async_copy(srcs[i], slot(i, *own), own_sem.at[i])
        copy.start()
        locals_.append(copy)

    def spread(i, src, origin, ways):
        for way, peer in ((Y, peer_y), (X, peer_x), (C, peer_c)):
            if way in ways and (wide[i] or way != X):
                make(i, src, origin, way, peer).start()

    def begin(i):
        src = srcs[i]

        @pl.when(z < 3)
        def _():
            make(i, src, own, Z, up).start()

        @pl.when(z > 0)
        def _():
            make(i, src, own, Z, down, True).start()

        spread(i, src, own, (Y, X, C))

    def each_z(fn):
        for k in (1, 2, 3):
            pl.when(z - k >= 0)(functools.partial(fn, z - k, True))
            pl.when(z + k <= 3)(functools.partial(fn, z + k, False))

    def landed(i, origin, way, peer):
        ref = slot(i, *origin)
        make(i, ref, origin, way, peer).wait_recv()
        return ref

    def after_z(i):
        def one(oz, rising):
            origin = (x, oz, y, c)
            ref = landed(i, origin, Z, up)
            if rising:

                @pl.when(z < 3)
                def _():
                    make(i, ref, origin, Z, up).start()
            else:

                @pl.when(z > 0)
                def _():
                    make(i, ref, origin, Z, down).start()

            spread(i, ref, origin, (Y, X, C))

        each_z(one)

    def after_y(i):
        def one(oz, rising):
            origin = (x, oz, 1 - y, c)
            spread(i, landed(i, origin, Y, peer_y), origin, (X, C))

        one(z, True)
        each_z(one)

    def after_x(i):
        for oy in (y, 1 - y):

            def one(oz, rising):
                origin = (1 - x, oz, oy, c)
                spread(i, landed(i, origin, X, peer_x), origin, (C,))

            one(z, True)
            each_z(one)

    AHEAD = 1
    for i in range(min(AHEAD, n)):
        begin(i)
    for i in range(n + 2):
        if i + AHEAD < n:
            begin(i + AHEAD)
        if i < n:
            after_z(i)
        if 0 <= i - 1 < n:
            after_y(i - 1)
        if 0 <= i - 2 < n and wide[i - 2]:
            after_x(i - 2)
    for i in range(n):
        for ox in (0, 1) if wide[i] else (x,):
            for oy in (0, 1):
                for oz in range(4):
                    landed(i, (ox, oz, oy, 1 - c), C, peer_c)
                    make(i, slot(i, ox, oz, oy, c), (ox, oz, oy, c), C, peer_c).wait_send()
        for oz in range(4):
            make(i, slot(i, x, oz, y, c), (x, oz, y, c), Y, peer_y).wait_send()
        if wide[i]:
            for oy in (0, 1):
                for oz in range(4):
                    make(i, slot(i, x, oz, oy, c), (x, oz, oy, c), X, peer_x).wait_send()

        def sent(oz, rising):
            origin = (x, oz, y, c)
            pl.when(z < 3 if rising else z > 0)(
                lambda: make(i, slot(i, *origin), origin, Z, up).wait_send()
            )

        each_z(sent)
        pl.when(z < 3)(lambda: make(i, srcs[i], own, Z, up).wait_send())
        pl.when(z > 0)(lambda: make(i, srcs[i], own, Z, down, True).wait_send())
        locals_[i].wait()


def gather_all(shards, wide, cid):
    n = len(shards)
    outs = [
        jax.ShapeDtypeStruct(((2, 16) if w else (16,)) + s.shape, s.dtype)
        for s, w in zip(shards, wide)
    ]
    any_ = pl.BlockSpec(memory_space=pl.ANY)
    return pl.pallas_call(
        functools.partial(gather_kernel, wide),
        out_shape=outs,
        in_specs=[any_] * n,
        out_specs=[any_] * n,
        scratch_shapes=[
            pltpu.SemaphoreType.DMA((n,)),
            pltpu.SemaphoreType.DMA((n, 33)),
            pltpu.SemaphoreType.DMA((n, 33)),
        ],
        compiler_params=pltpu.CompilerParams(collective_id=cid, has_side_effects=True),
        name="gather",
    )(*shards)


RING = 3


def reduce_kernel(nw, nt, *refs):
    srcs, small = refs[: nw + nt], refs[nw + nt]
    outs, small_out = refs[nw + nt + 1 : 2 * (nw + nt) + 1], refs[2 * (nw + nt) + 1]
    accw, rcw, rxw, ryw, rzw, acct, rct, ryt, rzt, tot, rsm = refs[2 * (nw + nt) + 2 : -3]
    send_sem, recv_sem, free_sem = refs[-3:]
    x, z, y, c = place()
    zs = [near(z, k, 4) for k in (1, 2, 3)]
    peer_x, peer_y, peer_c = at(1 - x, z, y, c), at(x, z, 1 - y, c), at(x, z, y, 1 - c)
    greet([at(x, k, y, c) for k in zs] + [peer_x, peer_y, peer_c])
    counts = [0]

    def remote(src, dst, peer):
        k = counts[0]
        counts[0] += 1
        copy = pltpu.make_async_remote_copy(
            src_ref=src,
            dst_ref=dst,
            send_sem=send_sem.at[k],
            recv_sem=recv_sem.at[k],
            device_id=peer,
            device_id_type=MESH,
        )
        copy.start()
        return copy

    def local(src, dst):
        k = counts[0]
        counts[0] += 1
        copy = pltpu.make_async_copy(src, dst, send_sem.at[k])
        copy.start()
        return copy

    rw, rt = accw.shape[-2], acct.shape[-2]
    wide = [(i, j) for i in range(nw) for j in range(0, srcs[0].shape[-2], rw)]
    slim = [(nw + i, j) for i in range(nt) for j in range(0, srcs[nw].shape[-2], rt)]

    def group(kind, chunk, gx, gy, gc):
        i, j = chunk
        rows = pl.ds(j, rw if kind == "w" else rt)
        if kind == "w":
            return srcs[i].at[gx, :, gy, gc, rows, :]
        return srcs[i].at[:, gy, gc, rows, :]

    def groups(kind):
        if kind == "w":
            return [(1 - x, 1 - y), (1 - x, y), (x, 1 - y), (x, y)]
        return [(0, 1 - y), (0, y)]

    bufs = {"w": (accw, rcw, rxw, ryw, rzw), "t": (acct, rct, None, ryt, rzt)}
    chunks = {"w": wide, "t": slim}
    state = {}
    pending = []

    def add_into(dst, other):
        def body(k, _):
            dst[k] = dst[k] + other[k]
            return 0

        lax.fori_loop(0, dst.shape[0], body, 0)

    def fetch(kind, k):
        acc, rc = bufs[kind][:2]
        items = []
        if k >= RING:
            pl.semaphore_wait(free_sem.at[0 if kind == "w" else 1], 1)
        for g, (gx, gy) in enumerate(groups(kind)):
            mine = local(group(kind, chunks[kind][k], gx, gy, c), acc.at[k, g])
            other = remote(group(kind, chunks[kind][k], gx, gy, 1 - c), rc.at[k % RING, g], peer_c)
            items.append((mine, other))
        state[kind, k] = items

    def core_sum(kind, k):
        acc, rc, rx, ry, _ = bufs[kind]
        sent = []
        for g, (mine, other) in enumerate(state[kind, k]):
            mine.wait()
            other.wait_recv()
            pending.append(other)
            add_into(acc.at[k, g], rc.at[k % RING, g])
            if kind == "w" and g < 2:
                sent.append(remote(acc.at[k, g], rx.at[k, g], peer_x))
            if kind == "t" and g == 0:
                sent.append(remote(acc.at[k, g], ry.at[k], peer_y))
        if k + RING < len(chunks[kind]):
            pl.semaphore_signal(
                free_sem.at[0 if kind == "w" else 1], inc=1, device_id=peer_c, device_id_type=MESH
            )
        state[kind, k] = sent

    def after_x(k):
        sent = state["w", k]
        for g in range(2):
            sent[g].wait_recv()
            pending.append(sent[g])
            add_into(accw.at[k, 2 + g], rxw.at[k, g])
            if g == 0:
                state["w", k] = [remote(accw.at[k, 2], ryw.at[k], peer_y)]

    def after_y(kind, k):
        acc, _, _, ry, rz = bufs[kind]
        last = 3 if kind == "w" else 1
        copy = state[kind, k][0]
        copy.wait_recv()
        pending.append(copy)
        add_into(acc.at[k, last], ry.at[k])
        state[kind, k] = [
            remote(acc.at[k, last, zs[s]], rz.at[k, 2 - s], at(x, zs[s], y, c)) for s in range(3)
        ]

    def after_z(kind, k):
        acc, _, _, _, rz = bufs[kind]
        last = 3 if kind == "w" else 1
        total = acc[k, last, z].astype(F32)
        for s in range(3):
            state[kind, k][s].wait_recv()
            pending.append(state[kind, k][s])
        for s in range(3):
            total = total + rz[k, s].astype(F32)
        i, j = chunks[kind][k]
        outs[i][j : j + total.shape[0], :] = total

    tot[0] = small[...]
    flips = [peer_c, peer_x, peer_y]
    flips += [at(x, z + 1 - 2 * lax.rem(z, 2), y, c), at(x, lax.rem(z + 2, 4), y, c)]
    small_state = []

    def small_step(s):
        if s > 0:
            copy = small_state[-1]
            copy.wait_recv()
            pending.append(copy)
            tot[s] = tot[s - 1] + rsm[s - 1]
        if s < len(flips):
            small_state.append(remote(tot.at[s], rsm.at[s], flips[s]))

    n, m = len(wide), len(slim)
    fetch("w", 0)
    fetch("t", 0)
    for k in range(max(n, m) + 4):
        if k + 1 < n:
            fetch("w", k + 1)
        if k < n:
            core_sum("w", k)
        if k + 1 < m:
            fetch("t", k + 1)
        if k < m:
            core_sum("t", k)
        if k <= len(flips):
            small_step(k)
        if 0 <= k - 1 < n:
            after_x(k - 1)
        if 0 <= k - 1 < m:
            after_y("t", k - 1)
        if 0 <= k - 2 < n:
            after_y("w", k - 2)
        if 0 <= k - 2 < m:
            after_z("t", k - 2)
        if 0 <= k - 3 < n:
            after_z("w", k - 3)
    small_out[...] = tot[len(flips)]
    for copy in pending:
        copy.wait_send()


def reduce_all(wide, slim, small, cid):
    nw, nt = len(wide), len(slim)
    rows, cw = wide[0].shape[-2:]
    ct = slim[0].shape[-1]
    kw, kt = nw, nt * rows // 16
    outs = [jax.ShapeDtypeStruct((rows, a.shape[-1]), F32) for a in wide + slim]
    outs.append(jax.ShapeDtypeStruct(small.shape, F32))
    copies = kw * (8 + 2 + 1 + 3) + kt * (4 + 1 + 3) + 5
    any_ = pl.BlockSpec(memory_space=pl.ANY)
    vm = pl.BlockSpec(memory_space=pltpu.VMEM)
    return pl.pallas_call(
        functools.partial(reduce_kernel, nw, nt),
        out_shape=outs,
        in_specs=[any_] * (nw + nt) + [vm],
        out_specs=[vm] * (nw + nt + 1),
        scratch_shapes=[
            pltpu.VMEM((kw, 4, 4, rows, cw), BF16),
            pltpu.VMEM((RING, 4, 4, rows, cw), BF16),
            pltpu.VMEM((kw, 2, 4, rows, cw), BF16),
            pltpu.VMEM((kw, 4, rows, cw), BF16),
            pltpu.VMEM((kw, 3, rows, cw), BF16),
            pltpu.VMEM((kt, 2, 4, 16, ct), BF16),
            pltpu.VMEM((RING, 2, 4, 16, ct), BF16),
            pltpu.VMEM((kt, 4, 16, ct), BF16),
            pltpu.VMEM((kt, 3, 16, ct), BF16),
            pltpu.VMEM((6,) + small.shape, F32),
            pltpu.VMEM((5,) + small.shape, F32),
            pltpu.SemaphoreType.DMA((copies,)),
            pltpu.SemaphoreType.DMA((copies,)),
            pltpu.SemaphoreType.REGULAR((2,)),
        ],
        compiler_params=pltpu.CompilerParams(
            collective_id=cid, has_side_effects=True, vmem_limit_bytes=62 * 2**20
        ),
        name="reduce",
    )(*wide, *slim, small)


def gather_plain(shards, wide):
    full = [lax.all_gather(s, "dp") for s in shards]
    return [lax.all_gather(f, "tensor") if w else f for f, w in zip(full, wide)]


def reduce_plain(wide, slim, small):
    outs = []
    for grads in wide:
        part = lax.psum_scatter(grads, "tensor", scatter_dimension=0, tiled=False)
        outs.append(lax.psum_scatter(part, "dp", scatter_dimension=0, tiled=False).astype(F32))
    for grads in slim:
        outs.append(lax.psum_scatter(grads, "dp", scatter_dimension=0, tiled=False).astype(F32))
    outs.append(lax.psum(small, ("dp", "tensor")))
    return outs


def local(
    token_codes,
    mask_slots,
    mask_counts,
    embedding,
    emb_first,
    emb_second,
    readout,
    read_first,
    read_second,
    in_proj,
    in_first,
    in_second,
    out_proj,
    out_first,
    out_second,
    up_proj,
    up_first,
    up_second,
    down_proj,
    down_first,
    down_second,
    vectors,
    vec_first,
    vec_second,
    position,
    pos_first,
    pos_second,
):
    tensor_at = lax.axis_index("tensor")
    tensor_size = lax.axis_size("tensor")
    seqs, patches = token_codes.shape
    side = math.isqrt(patches)
    tokens = patches + 1
    lp = -(-tokens // 16) * 16
    slots = mask_slots.shape[1]
    mine = seqs // tensor_size
    layers = in_proj.shape[0]
    tail = vectors.shape[0] - 4
    half_vocab = embedding.shape[0]
    vocab_start = tensor_at * half_vocab
    d = vectors.shape[1]

    live_slot = jnp.arange(slots)[None, :] < mask_counts[:, None]
    hits = (mask_slots[:, :, None] == jnp.arange(patches)[None, None, :])
    masked = jnp.any(hits & live_slot[:, :, None], axis=1)
    targets = jnp.sum(jnp.where(hits, token_codes[:, None, :], 0), axis=2)
    count_here = jnp.sum(mask_counts.astype(F32))
    dp_size = lax.axis_size("dp")
    custom = dp_size == 16 and tensor_size == 2

    shards = [
        pack_layer(in_proj[l], out_proj[l], up_proj[l], down_proj[l]).astype(BF16)
        for l in range(layers)
    ]
    sources = [
        shards[0],
        jnp.full((8, 128), count_here),
        shards[1],
        embedding.T.astype(BF16),
        readout.T.astype(BF16),
    ]
    wide = (True, False, True, False, False)
    found = gather_all(sources, wide, 1) if custom else gather_plain(sources, wide)
    mask_total = jnp.sum(found[1][:, 0, 0])
    weights = [found[0].reshape(2, d, -1), found[2].reshape(2, d, -1)]
    emb_table = found[3].reshape(d, half_vocab)
    read_table = found[4].reshape(d, half_vocab)

    code_rows = jnp.where(masked, -1, token_codes - vocab_start)
    code_rows = jnp.pad(code_rows, ((0, 0), (1, lp - tokens)), constant_values=-1).reshape(-1)
    code_hot = (code_rows[:, None] == jnp.arange(half_vocab)[None, :]).astype(BF16)
    part = dot_nt(code_hot, emb_table).astype(BF16)
    summed = lax.psum_scatter(part, "tensor", scatter_dimension=0, tiled=True).astype(F32)
    my_masked = lax.dynamic_slice_in_dim(masked, tensor_at * mine, mine, 0)
    mask_flag = jnp.pad(my_masked.astype(F32), ((0, 0), (1, lp - tokens))).reshape(-1, 1)
    lead_flag = jnp.zeros((mine, lp), F32).at[:, 0].set(1.0).reshape(-1, 1)
    x = summed + lead_flag * vectors[tail] + mask_flag * vectors[tail + 1]

    biases = expand_bias(position, side, lp)
    kept = []
    for l in range(layers):
        x, saved = forward_layer(x, weights[l], vectors[14 * l : 14 * l + 14], biases[l], mine)
        kept.append(saved)

    my_slots = lax.dynamic_slice_in_dim(mask_slots, tensor_at * mine, mine, 0)
    pick = (jnp.arange(mine)[:, None] * lp + 1 + my_slots).reshape(-1)
    final_in = x[pick]
    unit, _ = norm_parts(final_in)
    u = (unit * vectors[tail + 2] + vectors[tail + 3]).astype(BF16)
    u_all = lax.all_gather(u, "tensor", axis=0, tiled=True)
    logits = dot_nn(u_all, read_table)
    is_target = jnp.arange(half_vocab)[None, :] == (targets.reshape(-1) - vocab_start)[:, None]
    peak = jnp.max(logits, axis=1)
    total = jnp.sum(jnp.exp(logits - peak[:, None]), axis=1)
    chosen = jnp.sum(jnp.where(is_target, logits, 0.0), axis=1)
    stats = lax.all_gather(jnp.stack([peak, total, chosen]), "tensor")
    top = jnp.maximum(stats[0, 0], stats[1, 0])
    log_total = top + jnp.log(
        stats[0, 1] * jnp.exp(stats[0, 0] - top) + stats[1, 1] * jnp.exp(stats[1, 0] - top)
    )
    weight_row = live_slot.reshape(-1).astype(F32)
    loss_here = jnp.sum((log_total - stats[0, 2] - stats[1, 2]) * weight_row)
    g_logits = (jnp.exp(logits - log_total[:, None]) - is_target.astype(F32)) * (
        weight_row / mask_total
    )[:, None]
    g_logits = g_logits.astype(BF16)
    grad_final = lax.psum_scatter(
        dot_nt(g_logits, read_table).astype(BF16), "tensor", scatter_dimension=0, tiled=True
    ).astype(F32)
    grad_read = dot_tn(u_all, g_logits)
    back, g_gain, g_shift = norm_back(grad_final, final_in, vectors[tail + 2])
    g = jnp.zeros_like(x).at[pick].add(back)

    mat_grads = [None] * layers
    vec_grads = [None] * layers
    rel_grads = [None] * layers
    for l in reversed(range(layers)):
        g, full, vec_grads[l], rel = backward_layer(
            g, kept[l], weights[l], vectors[14 * l : 14 * l + 14], biases[l], mine
        )
        mat_grads[l] = full
        rel_grads[l] = rel

    g0 = g.astype(BF16)
    grad_lead = jnp.sum(g0.astype(F32) * lead_flag, axis=0)
    grad_mask = jnp.sum(g0.astype(F32) * mask_flag, axis=0)
    g0_all = lax.all_gather(g0, "tensor", axis=0, tiled=True)
    grad_emb = dot_tn(g0_all, code_hot)
    vec_local = jnp.concatenate(
        vec_grads + [jnp.stack([grad_lead, grad_mask, g_gain, g_shift])], axis=0
    )
    small_parts = [vec_local, fold_bias(jnp.stack(rel_grads), side), loss_here / tensor_size]
    flat = jnp.concatenate([p.reshape(-1) for p in small_parts])
    flat = jnp.pad(flat, (0, -flat.size % 1024)).reshape(-1, 128)
    if custom:
        lead = (4, 2, 2, d // 16)
        reduced = reduce_all(
            [m.reshape((2,) + lead + m.shape[-1:]) for layer in mat_grads for m in layer],
            [m.astype(BF16).reshape(lead + m.shape[-1:]) for m in (grad_read, grad_emb)],
            flat,
            2,
        )
    else:
        lead = (dp_size, d // dp_size)
        reduced = reduce_plain(
            [m.reshape((2,) + lead + m.shape[-1:]) for layer in mat_grads for m in layer],
            [m.astype(BF16).reshape(lead + m.shape[-1:]) for m in (grad_read, grad_emb)],
            flat,
        )
    grad_read, grad_emb, flat = reduced[3 * layers :]
    flat = flat.reshape(-1)
    vec_all = flat[: vectors.size].reshape(vectors.shape)
    rel_all = flat[vectors.size : vectors.size + position.size].reshape(position.shape)
    loss_sum = flat[vectors.size + position.size]

    half = d // 2
    in_g, out_g, up_g, down_g = [], [], [], []
    for l in range(layers):
        attn, up, down = reduced[3 * l : 3 * l + 3]
        in_g.append(attn[:, : 3 * half].reshape(-1, 3, half))
        out_g.append(attn[:, 3 * half :])
        up_g.append(up)
        down_g.append(down)
    emb_new = adamw_update(
        embedding, grad_emb.astype(F32).T, emb_first, emb_second, rate_table, decay_matrix
    )
    read_new = adamw_update(
        readout, grad_read.astype(F32).T, read_first, read_second, rate_matrix, decay_matrix
    )
    in_new = adamw_update(in_proj, jnp.stack(in_g), in_first, in_second, rate_matrix, decay_matrix)
    out_new = adamw_update(
        out_proj, jnp.stack(out_g), out_first, out_second, rate_matrix, decay_matrix
    )
    up_new = adamw_update(up_proj, jnp.stack(up_g), up_first, up_second, rate_matrix, decay_matrix)
    down_new = adamw_update(
        down_proj, jnp.stack(down_g), down_first, down_second, rate_matrix, decay_matrix
    )
    vec_new = adamw_update(vectors, vec_all, vec_first, vec_second, rate_vector, 0.0)
    pos_new = adamw_update(position, rel_all, pos_first, pos_second, rate_vector, 0.0)
    return (
        (loss_sum, mask_total)
        + emb_new
        + read_new
        + in_new
        + out_new
        + up_new
        + down_new
        + vec_new
        + pos_new
        + tuple(n[0].astype(BF16) for n in (in_new, out_new, up_new, down_new))
    )


def solution(mesh):
    table = P("tensor", "dp")
    in_spec = P(None, "dp", None, "tensor")
    mat = P(None, "dp", "tensor")
    return jax.shard_map(
        local,
        mesh=mesh,
        in_specs=(P("dp", None), P("dp", None), P("dp"))
        + (table,) * 6
        + (in_spec,) * 3
        + (mat,) * 9
        + (P(),) * 6,
        out_specs=(P(), P())
        + (table,) * 6
        + (in_spec,) * 3
        + (mat,) * 9
        + (P(),) * 6
        + (in_spec, mat, mat, mat),
        check_vma=False,
    )
```

```python
import functools
import math

import jax
import jax.numpy as jnp
import numpy as np
from jax import lax
from jax.experimental import pallas as pl
from jax.experimental.pallas import tpu as pltpu
from jax.sharding import PartitionSpec as P

HEADS = 12
HD = 64
STEP = 5

beta_one = 0.5
beta_two = 0.5
adam_eps = 1e-08
rate_matrix = 0.05
rate_vector = 0.3
rate_table = 0.5
decay_matrix = 0.05
norm_eps = 1e-06
F32 = jnp.float32
BF16 = jnp.bfloat16
BIG = -1e30
ROOT_HALF = 0.5**0.5


def dot_nn(a, b):
    return lax.dot_general(a, b, (((1,), (0,)), ((), ())), preferred_element_type=F32)


def dot_nt(a, b):
    return lax.dot_general(a, b, (((1,), (1,)), ((), ())), preferred_element_type=F32)


def dot_tn(a, b):
    return lax.dot_general(a, b, (((0,), (0,)), ((), ())), preferred_element_type=F32)


def norm_parts(values):
    center = values - jnp.mean(values, axis=-1, keepdims=True)
    spread_sq = jnp.mean(center * center, axis=-1, keepdims=True)
    scale = lax.rsqrt(spread_sq + norm_eps)
    return center * scale, scale


def norm_back(grad, values, gain):
    unit, scale = norm_parts(values)
    inner = grad * gain
    back = scale * (
        inner
        - jnp.mean(inner, axis=-1, keepdims=True)
        - unit * jnp.mean(inner * unit, axis=-1, keepdims=True)
    )
    return back, jnp.sum(grad * unit, axis=0), jnp.sum(grad, axis=0)


def norm_back(grad, values, gain):
    unit, scale = norm_parts(values)
    inner = grad * gain
    back = scale * (
        inner
        - jnp.mean(inner, axis=-1, keepdims=True)
        - unit * jnp.mean(inner * unit, axis=-1, keepdims=True)
    )
    return back, jnp.sum(grad * unit, axis=0), jnp.sum(grad, axis=0)


ROWS = 48


def row_loop(rows, body):
    def step(i, _):
        body(pl.ds(pl.multiple_of(i * ROWS, ROWS), ROWS))
        return 0

    lax.fori_loop(0, rows // ROWS, step, 0)


def lane_low():
    return lax.broadcasted_iota(jnp.int32, (1, 2 * HD), 1) < HD


def halves(pair):
    low = lane_low()
    zero = jnp.zeros_like(pair)
    return jnp.where(low, pair, zero), jnp.where(low, zero, pair)


def softmax_rows(scores):
    e = jnp.exp(scores - jnp.max(scores, axis=-1, keepdims=True))
    return e * (1.0 / jnp.sum(e, axis=-1, keepdims=True))


def attention_loop(seqs, lp, half, body):
    pairs = half // (2 * HD)

    def step(s, _):
        rows = pl.ds(pl.multiple_of(s * lp, 16), lp)
        for hp in range(pairs):
            body(s, rows, hp * 2 * HD, 2 * hp)
        return 0

    lax.fori_loop(0, seqs, step, 0)


def attn_kernel(seqs, x, w, vec, bias, y1, qkv, att, r, middle, y2):
    rows, d = x.shape
    half = d // 2
    lp = rows // seqs
    t = pl.program_id(0)
    mine = pl.ds(pl.multiple_of(t * half, 128), half)

    def first_norm(at):
        unit, _ = norm_parts(x[at, :])
        y1[at, :] = (unit * vec[0:1, :] + vec[1:2, :]).astype(BF16)

    pl.when(t == 0)(lambda: row_loop(rows, first_norm))
    for k in range(3):
        mixed = dot_nn(y1[...], w[0, :, k * half : (k + 1) * half])
        if k != 1:
            row = 2 if k == 0 else 3
            mixed = mixed + vec[row : row + 1, mine]
        qkv[0, :, k * half : (k + 1) * half] = mixed.astype(BF16)

    def attend(s, at, col, head):
        q = qkv[0, at, pl.ds(col, 2 * HD)]
        k = qkv[0, at, pl.ds(half + col, 2 * HD)]
        v = qkv[0, at, pl.ds(2 * half + col, 2 * HD)]
        found = []
        for i, part in enumerate(halves(q)):
            scores = dot_nt(part, k) * HD**-0.5 + bias[head + i]
            found.append(dot_nn(softmax_rows(scores).astype(BF16), v))
        att[0, at, pl.ds(col, 2 * HD)] = jnp.where(lane_low(), found[0], found[1]).astype(BF16)

    attention_loop(seqs, lp, half, attend)
    part = dot_nt(att[0], w[0, :, 3 * half :])

    @pl.when(t == 0)
    def _():
        r[...] = part

    def second_norm(at):
        here = x[at, :] + vec[5:6, :] * (r[at, :] + vec[4:5, :])
        middle[at, :] = here
        unit, _ = norm_parts(here)
        y2[at, :] = (unit * vec[6:7, :] + vec[7:8, :]).astype(BF16)

    @pl.when(t == 1)
    def _():
        r[...] += part
        row_loop(rows, second_norm)


def feed_kernel(middle, y2, w_up, w_down, shift, vec, pre, hid, z, out):
    rows = middle.shape[0]
    i = pl.program_id(0)
    a = dot_nn(y2[...], w_up[0]) + shift[0]
    pre[0] = a
    h = (0.5 * a * (1.0 + lax.erf(a * ROOT_HALF))).astype(BF16)
    hid[0] = h
    part = dot_nt(h, w_down[0])

    @pl.when(i == 0)
    def _():
        z[...] = part

    @pl.when(i > 0)
    def _():
        z[...] += part

    def finish(at):
        out[at, :] = middle[at, :] + vec[9:10, :] * (z[at, :] + vec[8:9, :])

    pl.when(i == pl.num_programs(0) - 1)(lambda: row_loop(rows, finish))


def full(shape):
    return pl.BlockSpec(shape, functools.partial(lambda n, *_: (0,) * n, len(shape)))


def lead(shape):
    return pl.BlockSpec((1,) + tuple(shape[1:]), lambda i: (i,) + (0,) * (len(shape) - 1))


def heads_of(shape):
    return pl.BlockSpec((shape[0] // 2,) + tuple(shape[1:]), lambda i: (i, 0, 0))


def tiles(rows, cols, first=0):
    return pl.BlockSpec((1, rows, cols), lambda i: (i // 3, 0, first + i % 3))


def call(kernel, steps, ins, in_specs, outs, out_specs, scratch, name, flops):
    return pl.pallas_call(
        kernel,
        out_shape=outs,
        grid=(steps,),
        in_specs=in_specs,
        out_specs=out_specs,
        scratch_shapes=scratch,
        compiler_params=pltpu.CompilerParams(vmem_limit_bytes=60 * 2**20),
        cost_estimate=pl.CostEstimate(flops=flops, bytes_accessed=3 * 10**7, transcendentals=0),
        name=name,
    )(*ins)


def attn_spec(weights):
    return pl.BlockSpec((1, weights.shape[1], weights.shape[2] // 3), lambda i: (i, 0, 0))


def forward_layer(x, weights, vec, bias, seqs):
    rows, d = x.shape
    half, ff = d // 2, weights.shape[2] // 3
    tile = ff // 3
    s = jax.ShapeDtypeStruct
    wide, slim = s((rows, d), F32), s((rows, d), BF16)
    qkv, att = s((2, rows, 3 * half), BF16), s((2, rows, half), BF16)
    y1, qkv, att, r, middle, y2 = call(
        functools.partial(attn_kernel, seqs),
        2,
        [x, weights, vec, bias],
        [full(x.shape), attn_spec(weights), full(vec.shape), heads_of(bias.shape)],
        [slim, qkv, att, wide, wide, slim],
        [full(slim.shape), lead(qkv.shape), lead(att.shape)] + [full(wide.shape)] * 3,
        [],
        "attn",
        4 * 10**9,
    )
    shift = vec[10:14].reshape(6, 1, tile)
    pre, hid, z, out = call(
        feed_kernel,
        6,
        [middle, y2, weights, weights, shift, vec],
        [
            full(wide.shape),
            full(wide.shape),
            tiles(d, tile, 3),
            tiles(d, tile, 6),
            lead(shift.shape),
            full(vec.shape),
        ],
        [s((2, rows, ff), F32), s((2, rows, ff), BF16), wide, wide],
        [tiles(rows, tile), tiles(rows, tile), full(wide.shape), full(wide.shape)],
        [],
        "feed",
        6 * 10**9,
    )
    return out, (x, y1, qkv, att, r, middle, y2, pre, hid, z)


def norm_back_rows(grad, values, gain):
    unit, scale = norm_parts(values)
    inner = grad * gain
    back = scale * (
        inner
        - jnp.mean(inner, axis=-1, keepdims=True)
        - unit * jnp.mean(inner * unit, axis=-1, keepdims=True)
    )
    return back, unit


def col_sum(v):
    return jnp.sum(v, axis=0, keepdims=True)


def feed_back_kernel(
    g, z, hid, pre, middle, y2, vec, w_up, w_down, gm, g_up, g_down, sums, upb, dz, dy2
):
    rows = g.shape[0]
    i = pl.program_id(0)

    def first(at):
        here = g[at, :]
        scaled = here * vec[9:10, :]
        dz[at, :] = scaled.astype(BF16)
        sums[0:1, :] += col_sum(scaled)
        sums[1:2, :] += col_sum(here * (z[at, :] + vec[8:9, :]))

    @pl.when(i == 0)
    def _():
        sums[...] = jnp.zeros_like(sums)
        row_loop(rows, first)

    dh = dot_nn(dz[...], w_down[0])
    a = pre[0]
    slope = 0.5 * (1.0 + lax.erf(a * ROOT_HALF))
    slope = slope + a * (jnp.exp(-0.5 * a * a) * (2 * math.pi) ** -0.5)
    da = (dh * slope).astype(BF16)
    upb[0] = col_sum(da.astype(F32))
    g_down[0] = dot_tn(dz[...], hid[0]).astype(BF16)
    g_up[0] = dot_tn(y2[...], da).astype(BF16)
    part = dot_nt(da, w_up[0])

    @pl.when(i == 0)
    def _():
        dy2[...] = part

    @pl.when(i > 0)
    def _():
        dy2[...] += part

    def last(at):
        grad = dy2[at, :]
        back, unit = norm_back_rows(grad, middle[at, :], vec[6:7, :])
        gm[at, :] = g[at, :] + back
        sums[2:3, :] += col_sum(grad * unit)
        sums[3:4, :] += col_sum(grad)

    pl.when(i == pl.num_programs(0) - 1)(lambda: row_loop(rows, last))


def attn_back_kernel(
    seqs, gm, r, x, y1, qkv, att, bias, vec, w, g, g_attn, sums, rel, dr, do, dqkv, dy1
):
    rows, d = gm.shape
    half = d // 2
    lp = rows // seqs
    t = pl.program_id(0)
    mine = pl.ds(pl.multiple_of(t * half, 128), half)

    def first(at):
        here = gm[at, :]
        scaled = here * vec[5:6, :]
        dr[at, :] = scaled.astype(BF16)
        sums[0:1, :] += col_sum(scaled)
        sums[1:2, :] += col_sum(here * (r[at, :] + vec[4:5, :]))

    @pl.when(t == 0)
    def _():
        sums[...] = jnp.zeros_like(sums)
        row_loop(rows, first)

    g_attn[0, :, 3 * half :] = dot_tn(dr[...], att[0]).astype(BF16)
    do[...] = dot_nn(dr[...], w[0, :, 3 * half :]).astype(BF16)

    def attend(s, at, col, head):
        q = qkv[0, at, pl.ds(col, 2 * HD)]
        k = qkv[0, at, pl.ds(half + col, 2 * HD)]
        v = qkv[0, at, pl.ds(2 * half + col, 2 * HD)]
        o = do[at, pl.ds(col, 2 * HD)]
        dq, dk, dv = [], [], []
        for i, (q_part, o_part) in enumerate(zip(halves(q), halves(o))):
            p = softmax_rows(dot_nt(q_part, k) * HD**-0.5 + bias[head + i])
            dp = dot_nt(o_part, v)
            ds = (p * (dp - jnp.sum(p * dp, axis=-1, keepdims=True))).astype(BF16)
            more = ds.astype(F32)
            rel[head + i] = jnp.where(s == 0, more, rel[head + i] + more)
            dq.append(dot_nn(ds, k))
            dk.append(dot_tn(ds, q))
            dv.append(dot_tn(p.astype(BF16), o))
        low = lane_low()
        for k, pair in enumerate((dq, dk, dv)):
            value = jnp.where(low, pair[0], pair[1])
            if k < 2:
                value = value * HD**-0.5
            dqkv[at, pl.ds(k * half + col, 2 * HD)] = value.astype(BF16)

    attention_loop(seqs, lp, half, attend)
    total = 0.0
    for k in range(3):
        cols = slice(k * half, (k + 1) * half)
        part = dqkv[:, cols]
        if k != 1:
            row = 2 if k == 0 else 3
            sums[row : row + 1, mine] = col_sum(part.astype(F32))
        g_attn[0, :, cols] = dot_tn(y1[...], part).astype(BF16)
        total = total + dot_nt(part, w[0, :, cols])

    @pl.when(t == 0)
    def _():
        dy1[...] = total

    def last(at):
        grad = dy1[at, :]
        back, unit = norm_back_rows(grad, x[at, :], vec[0:1, :])
        g[at, :] = gm[at, :] + back
        sums[4:5, :] += col_sum(grad * unit)
        sums[5:6, :] += col_sum(grad)

    @pl.when(t == 1)
    def _():
        dy1[...] += total
        row_loop(rows, last)


def backward_layer(g, saved, weights, vec, bias, seqs):
    x, y1, qkv, att, r, middle, y2, pre, hid, z = saved
    rows, d = x.shape
    half, ff = d // 2, weights.shape[2] // 3
    tile = ff // 3
    s = jax.ShapeDtypeStruct
    part = s((2, d, ff), BF16)
    wide = full((rows, d))
    gm, g_up, g_down, low_sums, upb = call(
        feed_back_kernel,
        6,
        [g, z, hid, pre, middle, y2, vec, weights, weights],
        [wide, wide, tiles(rows, tile), tiles(rows, tile), wide, wide, full(vec.shape)]
        + [tiles(d, tile, 3), tiles(d, tile, 6)],
        [s((rows, d), F32), part, part, s((8, d), F32), s((6, 1, tile), F32)],
        [wide, tiles(d, tile), tiles(d, tile), full((8, d)), lead((6, 1, tile))],
        [pltpu.VMEM((rows, d), BF16), pltpu.VMEM((rows, d), F32)],
        "feed_back",
        12 * 10**9,
    )
    g, g_attn, top_sums, rel = call(
        functools.partial(attn_back_kernel, seqs),
        2,
        [gm, r, x, y1, qkv, att, bias, vec, weights],
        [wide, wide, wide, wide, lead(qkv.shape), lead(att.shape)]
        + [heads_of(bias.shape), full(vec.shape), attn_spec(weights)],
        [s((rows, d), F32), part, s((8, d), F32), s(bias.shape, F32)],
        [wide, lead(part.shape), full((8, d)), heads_of(bias.shape)],
        [
            pltpu.VMEM((rows, d), BF16),
            pltpu.VMEM((rows, half), BF16),
            pltpu.VMEM((rows, 3 * half), BF16),
            pltpu.VMEM((rows, d), F32),
        ],
        "attn_back",
        6 * 10**9,
    )
    vec_grad = jnp.concatenate(
        [
            top_sums[4:6],
            top_sums[2:4],
            top_sums[0:2],
            low_sums[2:4],
            low_sums[0:2],
            upb.reshape(4, d),
        ],
        axis=0,
    )
    return g, (g_attn, g_up, g_down), vec_grad, rel


def strip_constant(side):
    width = 2 * side - 1
    wide = -(-(width * side) // 128) * 128
    out = np.zeros((width * width, 16, wide), np.float32)
    for c in range(side):
        for k in range(width):
            for e in range(side):
                out[width * k + side - 1 - c + e, c, k * side + e] = 1.0
    return out.reshape(width * width, 16 * wide), wide


def split_three(v):
    high = lax.reduce_precision(v, 8, 7)
    rest = v - high
    mid = lax.reduce_precision(rest, 8, 7)
    return jnp.concatenate([high, mid, rest - mid], axis=0).astype(BF16)


def add_three(v):
    n = v.shape[0] // 3
    return v[:n] + v[n : 2 * n] + v[2 * n :]


def expand_kernel(side, strips, ends, out):
    def head(h, _):
        expand_head(side, strips, ends, out, h)
        return 0

    lax.fori_loop(0, out.shape[0], head, 0)


def expand_head(side, strips, ends, out, h):
    lp = out.shape[1]
    wide = strips.shape[2]
    tokens = side * side + 1
    a = strips[h]
    lane = lax.broadcasted_iota(jnp.int32, (1, lp), 1)
    row_end, col_end, corner = ends[h, 0:1, 0:1], ends[h, 0:1, 1:2], ends[h, 0:1, 2:3]
    top = jnp.where(lane == 0, corner, row_end)
    out[h, 0:1, :] = jnp.where(lane < tokens, top, BIG)
    for r in range(side):
        shift = (side - 1 - r) * side - 1
        moved = pltpu.roll(a, (wide - shift) % wide, 1)[:side, :lp]
        moved = jnp.where(lane == 0, col_end, moved)
        out[h, 1 + r * side : 1 + (r + 1) * side, :] = jnp.where(lane < tokens, moved, BIG)
    tail = jnp.where(lane < tokens, 0.0, BIG)
    out[h, tokens:, :] = jnp.broadcast_to(tail, (lp - tokens, lp))


def expand_bias(position, side, lp):
    layers, heads, entries = position.shape
    flat = position.reshape(layers * heads, entries)
    hot, wide = strip_constant(side)
    cells = hot.shape[0]
    strips = add_three(dot_nn(split_three(flat[:, :cells][:, ::-1]), jnp.asarray(hot, BF16)))
    strips = strips.reshape(layers * heads, 16, wide)
    ends = jnp.pad(flat[:, cells:], ((0, 0), (0, 125)))[:, None, :]
    out = pl.pallas_call(
        functools.partial(expand_kernel, side),
        out_shape=jax.ShapeDtypeStruct((layers * heads, lp, lp), F32),
        grid=(layers * heads // 6,),
        in_specs=[
            pl.BlockSpec((6, 16, wide), lambda i: (i, 0, 0)),
            pl.BlockSpec((6, 1, 128), lambda i: (i, 0, 0)),
        ],
        out_specs=pl.BlockSpec((6, lp, lp), lambda i: (i, 0, 0)),
        name="expand",
    )(strips, ends)
    return out.reshape(layers, heads, lp, lp)


def fold_kernel(side, grads, strips, ends):
    def head(h, _):
        fold_head(side, grads, strips, ends, h)
        return 0

    lax.fori_loop(0, grads.shape[0], head, 0)


def fold_head(side, grads, strips, ends, h):
    lp = grads.shape[1]
    wide = strips.shape[2]
    tokens = side * side + 1
    lane = lax.broadcasted_iota(jnp.int32, (1, lp), 1)
    total = jnp.zeros((16, wide), F32)
    for r in range(side):
        shift = (side - 1 - r) * side - 1
        part = jnp.where(lane == 0, 0.0, grads[h, 1 + r * side : 1 + (r + 1) * side, :])
        part = jnp.concatenate([part, jnp.zeros((16 - side, lp), F32)], axis=0)
        part = jnp.concatenate([part, jnp.zeros((16, wide - lp), F32)], axis=1)
        total = total + pltpu.roll(part, shift % wide, 1)
    strips[h] = total
    corner = grads[h, 0:1, 0:1]
    row_end = jnp.sum(grads[h, 0:1, :], axis=1, keepdims=True) - corner
    col_end = jnp.sum(grads[h, 1:tokens, 0:1], axis=0, keepdims=True)
    out_lane = lax.broadcasted_iota(jnp.int32, (1, 128), 1)
    ends[h] = jnp.where(
        out_lane == 0, row_end, jnp.where(out_lane == 1, col_end, jnp.where(out_lane == 2, corner, 0.0))
    )


def fold_bias(grads, side):
    layers, heads, lp, _ = grads.shape
    hot, wide = strip_constant(side)
    n = layers * heads
    strips, ends = pl.pallas_call(
        functools.partial(fold_kernel, side),
        out_shape=[
            jax.ShapeDtypeStruct((n, 16, wide), F32),
            jax.ShapeDtypeStruct((n, 1, 128), F32),
        ],
        grid=(n // 6,),
        in_specs=[pl.BlockSpec((6, lp, lp), lambda i: (i, 0, 0))],
        out_specs=[
            pl.BlockSpec((6, 16, wide), lambda i: (i, 0, 0)),
            pl.BlockSpec((6, 1, 128), lambda i: (i, 0, 0)),
        ],
        name="fold",
    )(grads.reshape(n, lp, lp))
    cells = add_three(dot_nt(split_three(strips.reshape(n, 16 * wide)), jnp.asarray(hot, BF16)))
    flat = jnp.concatenate([cells[:, ::-1], ends[:, 0, :3]], axis=1)
    return flat.reshape(layers, heads, -1)


def adamw_update(master, gradient, first_mom, second_mom, step_rate, decay_rate):
    first_mom = beta_one * first_mom + (1.0 - beta_one) * gradient
    second_mom = beta_two * second_mom + (1.0 - beta_two) * gradient * gradient
    step_dir = (
        first_mom
        / (1.0 - beta_one**STEP)
        / (jnp.sqrt(second_mom / (1.0 - beta_two**STEP)) + adam_eps)
    )
    return (master - step_rate * (step_dir + decay_rate * master), first_mom, second_mom)


def pack_layer(in_proj, out_proj, up_proj, down_proj):
    return jnp.concatenate(
        [in_proj[:, 0], in_proj[:, 1], in_proj[:, 2], out_proj, up_proj, down_proj], axis=1
    )


MESH = pl.DeviceIdType.MESH


def place():
    dp = lax.axis_index("dp")
    return lax.axis_index("tensor"), dp // 4, lax.rem(dp // 2, 2), lax.rem(dp, 2)


def at(x, z, y, c):
    return ((z * 2 + y) * 2 + c, x)


def near(v, step, size):
    return lax.rem(v + step, size)


def greet(peers):
    barrier = pltpu.get_barrier_semaphore()
    for peer in peers:
        pl.semaphore_signal(barrier, inc=1, device_id=peer, device_id_type=MESH)
    pl.semaphore_wait(barrier, len(peers))


def gather_kernel(wide, *refs):
    n = len(wide)
    srcs, dsts = refs[:n], refs[n : 2 * n]
    own_sem, send_sem, recv_sem = refs[2 * n :]
    x, z, y, c = place()
    peer_x, peer_y, peer_c = at(1 - x, z, y, c), at(x, z, 1 - y, c), at(x, z, y, 1 - c)
    up, down = at(x, jnp.minimum(z + 1, 3), y, c), at(x, jnp.maximum(z - 1, 0), y, c)
    barrier = pltpu.get_barrier_semaphore()
    for peer in (peer_x, peer_y, peer_c):
        pl.semaphore_signal(barrier, inc=1, device_id=peer, device_id_type=MESH)

    @pl.when(z < 3)
    def _():
        pl.semaphore_signal(barrier, inc=1, device_id=up, device_id_type=MESH)

    @pl.when(z > 0)
    def _():
        pl.semaphore_signal(barrier, inc=1, device_id=down, device_id_type=MESH)

    pl.semaphore_wait(barrier, 3 + jnp.where(z < 3, 1, 0) + jnp.where(z > 0, 1, 0))

    def slot(i, ox, oz, oy, oc):
        ref = dsts[i]
        dp = (oz * 2 + oy) * 2 + oc
        return ref.at[ox, dp] if wide[i] else ref.at[dp]

    Z, Y, X, C, Z2 = 0, 4, 8, 16, 32

    def make(i, src, origin, way, peer, two=False):
        ox, oz, oy, oc = origin
        if way == Z:
            k = Z + oz
        elif way == Y:
            k = Y + oz
        elif way == X:
            k = X + oy * 4 + oz
        else:
            k = C + (ox * 2 + oy) * 4 + oz
        return pltpu.make_async_remote_copy(
            src_ref=src,
            dst_ref=slot(i, *origin),
            send_sem=send_sem.at[i, Z2 if two else k],
            recv_sem=recv_sem.at[i, k],
            device_id=peer,
            device_id_type=MESH,
        )

    own = (x, z, y, c)
    locals_ = []
    for i in range(n):
        copy = pltpu.make_async_copy(srcs[i], slot(i, *own), own_sem.at[i])
        copy.start()
        locals_.append(copy)

    def spread(i, src, origin, ways):
        for way, peer in ((Y, peer_y), (X, peer_x), (C, peer_c)):
            if way in ways and (wide[i] or way != X):
                make(i, src, origin, way, peer).start()

    def begin(i):
        src = srcs[i]

        @pl.when(z < 3)
        def _():
            make(i, src, own, Z, up).start()

        @pl.when(z > 0)
        def _():
            make(i, src, own, Z, down, True).start()

        spread(i, src, own, (Y, X, C))

    def each_z(fn):
        for k in (1, 2, 3):
            pl.when(z - k >= 0)(functools.partial(fn, z - k, True))
            pl.when(z + k <= 3)(functools.partial(fn, z + k, False))

    def landed(i, origin, way, peer):
        ref = slot(i, *origin)
        make(i, ref, origin, way, peer).wait_recv()
        return ref

    def after_z(i):
        def one(oz, rising):
            origin = (x, oz, y, c)
            ref = landed(i, origin, Z, up)
            if rising:

                @pl.when(z < 3)
                def _():
                    make(i, ref, origin, Z, up).start()
            else:

                @pl.when(z > 0)
                def _():
                    make(i, ref, origin, Z, down).start()

            spread(i, ref, origin, (Y, X, C))

        each_z(one)

    def after_y(i):
        def one(oz, rising):
            origin = (x, oz, 1 - y, c)
            spread(i, landed(i, origin, Y, peer_y), origin, (X, C))

        one(z, True)
        each_z(one)

    def after_x(i):
        for oy in (y, 1 - y):

            def one(oz, rising):
                origin = (1 - x, oz, oy, c)
                spread(i, landed(i, origin, X, peer_x), origin, (C,))

            one(z, True)
            each_z(one)

    AHEAD = 1
    for i in range(min(AHEAD, n)):
        begin(i)
    for i in range(n + 2):
        if i + AHEAD < n:
            begin(i + AHEAD)
        if i < n:
            after_z(i)
        if 0 <= i - 1 < n:
            after_y(i - 1)
        if 0 <= i - 2 < n and wide[i - 2]:
            after_x(i - 2)
    for i in range(n):
        for ox in (0, 1) if wide[i] else (x,):
            for oy in (0, 1):
                for oz in range(4):
                    landed(i, (ox, oz, oy, 1 - c), C, peer_c)
                    make(i, slot(i, ox, oz, oy, c), (ox, oz, oy, c), C, peer_c).wait_send()
        for oz in range(4):
            make(i, slot(i, x, oz, y, c), (x, oz, y, c), Y, peer_y).wait_send()
        if wide[i]:
            for oy in (0, 1):
                for oz in range(4):
                    make(i, slot(i, x, oz, oy, c), (x, oz, oy, c), X, peer_x).wait_send()

        def sent(oz, rising):
            origin = (x, oz, y, c)
            pl.when(z < 3 if rising else z > 0)(
                lambda: make(i, slot(i, *origin), origin, Z, up).wait_send()
            )

        each_z(sent)
        pl.when(z < 3)(lambda: make(i, srcs[i], own, Z, up).wait_send())
        pl.when(z > 0)(lambda: make(i, srcs[i], own, Z, down, True).wait_send())
        locals_[i].wait()


def gather_all(shards, wide, cid):
    n = len(shards)
    outs = [
        jax.ShapeDtypeStruct(((2, 16) if w else (16,)) + s.shape, s.dtype)
        for s, w in zip(shards, wide)
    ]
    any_ = pl.BlockSpec(memory_space=pl.ANY)
    return pl.pallas_call(
        functools.partial(gather_kernel, wide),
        out_shape=outs,
        in_specs=[any_] * n,
        out_specs=[any_] * n,
        scratch_shapes=[
            pltpu.SemaphoreType.DMA((n,)),
            pltpu.SemaphoreType.DMA((n, 33)),
            pltpu.SemaphoreType.DMA((n, 33)),
        ],
        compiler_params=pltpu.CompilerParams(collective_id=cid, has_side_effects=True),
        name="gather",
    )(*shards)


RING = 3


def reduce_kernel(nw, nt, *refs):
    srcs, small = refs[: nw + nt], refs[nw + nt]
    outs, small_out = refs[nw + nt + 1 : 2 * (nw + nt) + 1], refs[2 * (nw + nt) + 1]
    accw, rcw, rxw, ryw, rzw, acct, rct, ryt, rzt, tot, rsm = refs[2 * (nw + nt) + 2 : -3]
    send_sem, recv_sem, free_sem = refs[-3:]
    x, z, y, c = place()
    zs = [near(z, k, 4) for k in (1, 2, 3)]
    peer_x, peer_y, peer_c = at(1 - x, z, y, c), at(x, z, 1 - y, c), at(x, z, y, 1 - c)
    greet([at(x, k, y, c) for k in zs] + [peer_x, peer_y, peer_c])
    counts = [0]

    def remote(src, dst, peer):
        k = counts[0]
        counts[0] += 1
        copy = pltpu.make_async_remote_copy(
            src_ref=src,
            dst_ref=dst,
            send_sem=send_sem.at[k],
            recv_sem=recv_sem.at[k],
            device_id=peer,
            device_id_type=MESH,
        )
        copy.start()
        return copy

    def local(src, dst):
        k = counts[0]
        counts[0] += 1
        copy = pltpu.make_async_copy(src, dst, send_sem.at[k])
        copy.start()
        return copy

    rw, rt = accw.shape[-2], acct.shape[-2]
    wide = [(i, j) for i in range(nw) for j in range(0, srcs[0].shape[-2], rw)]
    slim = [(nw + i, j) for i in range(nt) for j in range(0, srcs[nw].shape[-2], rt)]

    def group(kind, chunk, gx, gy, gc):
        i, j = chunk
        rows = pl.ds(j, rw if kind == "w" else rt)
        if kind == "w":
            return srcs[i].at[gx, :, gy, gc, rows, :]
        return srcs[i].at[:, gy, gc, rows, :]

    def groups(kind):
        if kind == "w":
            return [(1 - x, 1 - y), (1 - x, y), (x, 1 - y), (x, y)]
        return [(0, 1 - y), (0, y)]

    bufs = {"w": (accw, rcw, rxw, ryw, rzw), "t": (acct, rct, None, ryt, rzt)}
    chunks = {"w": wide, "t": slim}
    state = {}
    pending = []

    def add_into(dst, other):
        def body(k, _):
            dst[k] = dst[k] + other[k]
            return 0

        lax.fori_loop(0, dst.shape[0], body, 0)

    def fetch(kind, k):
        acc, rc = bufs[kind][:2]
        items = []
        if k >= RING:
            pl.semaphore_wait(free_sem.at[0 if kind == "w" else 1], 1)
        for g, (gx, gy) in enumerate(groups(kind)):
            mine = local(group(kind, chunks[kind][k], gx, gy, c), acc.at[k, g])
            other = remote(group(kind, chunks[kind][k], gx, gy, 1 - c), rc.at[k % RING, g], peer_c)
            items.append((mine, other))
        state[kind, k] = items

    def core_sum(kind, k):
        acc, rc, rx, ry, _ = bufs[kind]
        sent = []
        for g, (mine, other) in enumerate(state[kind, k]):
            mine.wait()
            other.wait_recv()
            pending.append(other)
            add_into(acc.at[k, g], rc.at[k % RING, g])
            if kind == "w" and g < 2:
                sent.append(remote(acc.at[k, g], rx.at[k, g], peer_x))
            if kind == "t" and g == 0:
                sent.append(remote(acc.at[k, g], ry.at[k], peer_y))
        if k + RING < len(chunks[kind]):
            pl.semaphore_signal(
                free_sem.at[0 if kind == "w" else 1], inc=1, device_id=peer_c, device_id_type=MESH
            )
        state[kind, k] = sent

    def after_x(k):
        sent = state["w", k]
        for g in range(2):
            sent[g].wait_recv()
            pending.append(sent[g])
            add_into(accw.at[k, 2 + g], rxw.at[k, g])
            if g == 0:
                state["w", k] = [remote(accw.at[k, 2], ryw.at[k], peer_y)]

    def after_y(kind, k):
        acc, _, _, ry, rz = bufs[kind]
        last = 3 if kind == "w" else 1
        copy = state[kind, k][0]
        copy.wait_recv()
        pending.append(copy)
        add_into(acc.at[k, last], ry.at[k])
        state[kind, k] = [
            remote(acc.at[k, last, zs[s]], rz.at[k, 2 - s], at(x, zs[s], y, c)) for s in range(3)
        ]

    def after_z(kind, k):
        acc, _, _, _, rz = bufs[kind]
        last = 3 if kind == "w" else 1
        total = acc[k, last, z].astype(F32)
        for s in range(3):
            state[kind, k][s].wait_recv()
            pending.append(state[kind, k][s])
        for s in range(3):
            total = total + rz[k, s].astype(F32)
        i, j = chunks[kind][k]
        outs[i][j : j + total.shape[0], :] = total

    tot[0] = small[...]
    flips = [peer_c, peer_x, peer_y]
    flips += [at(x, z + 1 - 2 * lax.rem(z, 2), y, c), at(x, lax.rem(z + 2, 4), y, c)]
    small_state = []

    def small_step(s):
        if s > 0:
            copy = small_state[-1]
            copy.wait_recv()
            pending.append(copy)
            tot[s] = tot[s - 1] + rsm[s - 1]
        if s < len(flips):
            small_state.append(remote(tot.at[s], rsm.at[s], flips[s]))

    n, m = len(wide), len(slim)
    fetch("w", 0)
    fetch("t", 0)
    for k in range(max(n, m) + 4):
        if k + 1 < n:
            fetch("w", k + 1)
        if k < n:
            core_sum("w", k)
        if k + 1 < m:
            fetch("t", k + 1)
        if k < m:
            core_sum("t", k)
        if k <= len(flips):
            small_step(k)
        if 0 <= k - 1 < n:
            after_x(k - 1)
        if 0 <= k - 1 < m:
            after_y("t", k - 1)
        if 0 <= k - 2 < n:
            after_y("w", k - 2)
        if 0 <= k - 2 < m:
            after_z("t", k - 2)
        if 0 <= k - 3 < n:
            after_z("w", k - 3)
    small_out[...] = tot[len(flips)]
    for copy in pending:
        copy.wait_send()


def reduce_all(wide, slim, small, cid):
    nw, nt = len(wide), len(slim)
    rows, cw = wide[0].shape[-2:]
    ct = slim[0].shape[-1]
    kw, kt = nw, nt * rows // 16
    outs = [jax.ShapeDtypeStruct((rows, a.shape[-1]), F32) for a in wide + slim]
    outs.append(jax.ShapeDtypeStruct(small.shape, F32))
    copies = kw * (8 + 2 + 1 + 3) + kt * (4 + 1 + 3) + 5
    any_ = pl.BlockSpec(memory_space=pl.ANY)
    vm = pl.BlockSpec(memory_space=pltpu.VMEM)
    return pl.pallas_call(
        functools.partial(reduce_kernel, nw, nt),
        out_shape=outs,
        in_specs=[any_] * (nw + nt) + [vm],
        out_specs=[vm] * (nw + nt + 1),
        scratch_shapes=[
            pltpu.VMEM((kw, 4, 4, rows, cw), BF16),
            pltpu.VMEM((RING, 4, 4, rows, cw), BF16),
            pltpu.VMEM((kw, 2, 4, rows, cw), BF16),
            pltpu.VMEM((kw, 4, rows, cw), BF16),
            pltpu.VMEM((kw, 3, rows, cw), BF16),
            pltpu.VMEM((kt, 2, 4, 16, ct), BF16),
            pltpu.VMEM((RING, 2, 4, 16, ct), BF16),
            pltpu.VMEM((kt, 4, 16, ct), BF16),
            pltpu.VMEM((kt, 3, 16, ct), BF16),
            pltpu.VMEM((6,) + small.shape, F32),
            pltpu.VMEM((5,) + small.shape, F32),
            pltpu.SemaphoreType.DMA((copies,)),
            pltpu.SemaphoreType.DMA((copies,)),
            pltpu.SemaphoreType.REGULAR((2,)),
        ],
        compiler_params=pltpu.CompilerParams(
            collective_id=cid, has_side_effects=True, vmem_limit_bytes=62 * 2**20
        ),
        name="reduce",
    )(*wide, *slim, small)


def gather_plain(shards, wide):
    full = [lax.all_gather(s, "dp") for s in shards]
    return [lax.all_gather(f, "tensor") if w else f for f, w in zip(full, wide)]


def reduce_plain(wide, slim, small):
    outs = []
    for grads in wide:
        part = lax.psum_scatter(grads, "tensor", scatter_dimension=0, tiled=False)
        outs.append(lax.psum_scatter(part, "dp", scatter_dimension=0, tiled=False).astype(F32))
    for grads in slim:
        outs.append(lax.psum_scatter(grads, "dp", scatter_dimension=0, tiled=False).astype(F32))
    outs.append(lax.psum(small, ("dp", "tensor")))
    return outs


def local(
    token_codes,
    mask_slots,
    mask_counts,
    embedding,
    emb_first,
    emb_second,
    readout,
    read_first,
    read_second,
    in_proj,
    in_first,
    in_second,
    out_proj,
    out_first,
    out_second,
    up_proj,
    up_first,
    up_second,
    down_proj,
    down_first,
    down_second,
    vectors,
    vec_first,
    vec_second,
    position,
    pos_first,
    pos_second,
):
    tensor_at = lax.axis_index("tensor")
    tensor_size = lax.axis_size("tensor")
    seqs, patches = token_codes.shape
    side = math.isqrt(patches)
    tokens = patches + 1
    lp = -(-tokens // 16) * 16
    slots = mask_slots.shape[1]
    mine = seqs // tensor_size
    layers = in_proj.shape[0]
    tail = vectors.shape[0] - 4
    half_vocab = embedding.shape[0]
    vocab_start = tensor_at * half_vocab
    d = vectors.shape[1]

    live_slot = jnp.arange(slots)[None, :] < mask_counts[:, None]
    hits = (mask_slots[:, :, None] == jnp.arange(patches)[None, None, :])
    masked = jnp.any(hits & live_slot[:, :, None], axis=1)
    targets = jnp.sum(jnp.where(hits, token_codes[:, None, :], 0), axis=2)
    count_here = jnp.sum(mask_counts.astype(F32))
    dp_size = lax.axis_size("dp")
    custom = dp_size == 16 and tensor_size == 2

    shards = [
        pack_layer(in_proj[l], out_proj[l], up_proj[l], down_proj[l]).astype(BF16)
        for l in range(layers)
    ]
    sources = [shards[0], jnp.full((8, 128), count_here), embedding.T.astype(BF16)]
    wide = (True, False, False)
    found = gather_all(sources, wide, 1) if custom else gather_plain(sources, wide)
    mask_total = jnp.sum(found[1][:, 0, 0])
    weights = [found[0].reshape(2, d, -1)]
    emb_table = found[2].reshape(d, half_vocab)
    weights.append(lax.all_gather(shards[1], ("tensor", "dp")).reshape(2, d, -1))
    read_table = lax.all_gather(readout.T.astype(BF16), "dp").reshape(d, half_vocab)

    peer_at = 1 - tensor_at

    def swap(value):
        return lax.ppermute(value, "tensor", [(0, 1), (1, 0)])

    def side_of(value, where):
        return lax.dynamic_slice_in_dim(value, where * mine, mine, 0)

    code_rows = jnp.where(masked, -1, token_codes - vocab_start)
    code_rows = jnp.pad(code_rows, ((0, 0), (1, lp - tokens)), constant_values=-1)
    codes = jnp.arange(half_vocab)[None, :]
    peer_hot = (side_of(code_rows, peer_at).reshape(-1, 1) == codes).astype(BF16)
    own_hot = (side_of(code_rows, tensor_at).reshape(-1, 1) == codes).astype(BF16)
    came = swap(dot_nt(peer_hot, emb_table).astype(BF16))
    summed = dot_nt(own_hot, emb_table).astype(BF16).astype(F32) + came.astype(F32)
    my_masked = side_of(masked, tensor_at)
    mask_flag = jnp.pad(my_masked.astype(F32), ((0, 0), (1, lp - tokens))).reshape(-1, 1)
    lead_flag = jnp.zeros((mine, lp), F32).at[:, 0].set(1.0).reshape(-1, 1)
    x = summed + lead_flag * vectors[tail] + mask_flag * vectors[tail + 1]

    biases = expand_bias(position, side, lp)
    kept = []
    for l in range(layers):
        x, saved = forward_layer(x, weights[l], vectors[14 * l : 14 * l + 14], biases[l], mine)
        kept.append(saved)

    my_slots = side_of(mask_slots, tensor_at)
    pick = (jnp.arange(mine)[:, None] * lp + 1 + my_slots).reshape(-1)
    final_in = x[pick]
    unit, _ = norm_parts(final_in)
    u = (unit * vectors[tail + 2] + vectors[tail + 3]).astype(BF16)
    u_peer = swap(u)
    places = [tensor_at, peer_at]
    logits, stats, target_hot = [], [], []
    for rows, where in zip((u, u_peer), places):
        lg = dot_nn(rows, read_table)
        hot = codes == (side_of(targets, where).reshape(-1) - vocab_start)[:, None]
        peak = jnp.max(lg, axis=1)
        total = jnp.sum(jnp.exp(lg - peak[:, None]), axis=1)
        chosen = jnp.sum(jnp.where(hot, lg, 0.0), axis=1)
        logits.append(lg)
        target_hot.append(hot)
        stats.append(jnp.stack([peak, total, chosen]))
    both = jnp.stack(stats)
    other = swap(both)[::-1]
    top = jnp.maximum(both[:, 0], other[:, 0])
    log_total = top + jnp.log(
        both[:, 1] * jnp.exp(both[:, 0] - top) + other[:, 1] * jnp.exp(other[:, 0] - top)
    )
    weight_row = live_slot.astype(F32)
    weights_of = [side_of(weight_row, where).reshape(-1) for where in places]
    losses = log_total - both[:, 2] - other[:, 2]
    loss_here = jnp.sum(losses * jnp.stack(weights_of))
    g_logits = [
        ((jnp.exp(logits[i] - log_total[i][:, None]) - target_hot[i].astype(F32)) * (weights_of[i] / mask_total)[:, None]).astype(BF16)
        for i in range(2)
    ]
    came = swap(dot_nt(g_logits[1], read_table).astype(BF16))
    grad_read = dot_tn(jnp.concatenate([u, u_peer]), jnp.concatenate(g_logits))
    grad_final = dot_nt(g_logits[0], read_table).astype(BF16).astype(F32) + came.astype(F32)
    back, g_gain, g_shift = norm_back(grad_final, final_in, vectors[tail + 2])
    g = jnp.zeros_like(x).at[pick].add(back)

    mat_grads = [None] * layers
    vec_grads = [None] * layers
    rel_grads = [None] * layers
    for l in reversed(range(layers)):
        g, full, vec_grads[l], rel = backward_layer(
            g, kept[l], weights[l], vectors[14 * l : 14 * l + 14], biases[l], mine
        )
        mat_grads[l] = full
        rel_grads[l] = rel

    g0 = g.astype(BF16)
    grad_lead = jnp.sum(g0.astype(F32) * lead_flag, axis=0)
    grad_mask = jnp.sum(g0.astype(F32) * mask_flag, axis=0)
    g0_peer = swap(g0)
    grad_emb = dot_tn(
        jnp.concatenate([g0, g0_peer]), jnp.concatenate([own_hot, peer_hot])
    )
    vec_local = jnp.concatenate(
        vec_grads + [jnp.stack([grad_lead, grad_mask, g_gain, g_shift])], axis=0
    )
    small_parts = [vec_local, fold_bias(jnp.stack(rel_grads), side), loss_here / tensor_size]
    flat = jnp.concatenate([p.reshape(-1) for p in small_parts])
    flat = jnp.pad(flat, (0, -flat.size % 1024)).reshape(-1, 128)
    if custom:
        lead = (4, 2, 2, d // 16)
        reduced = reduce_all(
            [m.reshape((2,) + lead + m.shape[-1:]) for layer in mat_grads for m in layer],
            [m.astype(BF16).reshape(lead + m.shape[-1:]) for m in (grad_read, grad_emb)],
            flat,
            2,
        )
    else:
        lead = (dp_size, d // dp_size)
        reduced = reduce_plain(
            [m.reshape((2,) + lead + m.shape[-1:]) for layer in mat_grads for m in layer],
            [m.astype(BF16).reshape(lead + m.shape[-1:]) for m in (grad_read, grad_emb)],
            flat,
        )
    grad_read, grad_emb, flat = reduced[3 * layers :]
    flat = flat.reshape(-1)
    vec_all = flat[: vectors.size].reshape(vectors.shape)
    rel_all = flat[vectors.size : vectors.size + position.size].reshape(position.shape)
    loss_sum = flat[vectors.size + position.size]

    half = d // 2
    in_g, out_g, up_g, down_g = [], [], [], []
    for l in range(layers):
        attn, up, down = reduced[3 * l : 3 * l + 3]
        in_g.append(attn[:, : 3 * half].reshape(-1, 3, half))
        out_g.append(attn[:, 3 * half :])
        up_g.append(up)
        down_g.append(down)
    emb_new = adamw_update(
        embedding, grad_emb.astype(F32).T, emb_first, emb_second, rate_table, decay_matrix
    )
    read_new = adamw_update(
        readout, grad_read.astype(F32).T, read_first, read_second, rate_matrix, decay_matrix
    )
    in_new = adamw_update(in_proj, jnp.stack(in_g), in_first, in_second, rate_matrix, decay_matrix)
    out_new = adamw_update(
        out_proj, jnp.stack(out_g), out_first, out_second, rate_matrix, decay_matrix
    )
    up_new = adamw_update(up_proj, jnp.stack(up_g), up_first, up_second, rate_matrix, decay_matrix)
    down_new = adamw_update(
        down_proj, jnp.stack(down_g), down_first, down_second, rate_matrix, decay_matrix
    )
    vec_new = adamw_update(vectors, vec_all, vec_first, vec_second, rate_vector, 0.0)
    pos_new = adamw_update(position, rel_all, pos_first, pos_second, rate_vector, 0.0)
    return (
        (loss_sum, mask_total)
        + emb_new
        + read_new
        + in_new
        + out_new
        + up_new
        + down_new
        + vec_new
        + pos_new
        + tuple(n[0].astype(BF16) for n in (in_new, out_new, up_new, down_new))
    )


def solution(mesh):
    table = P("tensor", "dp")
    in_spec = P(None, "dp", None, "tensor")
    mat = P(None, "dp", "tensor")
    return jax.shard_map(
        local,
        mesh=mesh,
        in_specs=(P("dp", None), P("dp", None), P("dp"))
        + (table,) * 6
        + (in_spec,) * 3
        + (mat,) * 9
        + (P(),) * 6,
        out_specs=(P(), P())
        + (table,) * 6
        + (in_spec,) * 3
        + (mat,) * 9
        + (P(),) * 6
        + (in_spec, mat, mat, mat),
        check_vma=False,
    )
```

```python
import functools
import math

import jax
import jax.numpy as jnp
import numpy as np
from jax import lax
from jax.experimental import pallas as pl
from jax.experimental.pallas import tpu as pltpu
from jax.sharding import PartitionSpec as P

HEADS = 12
HD = 64
STEP = 5

beta_one = 0.5
beta_two = 0.5
adam_eps = 1e-08
rate_matrix = 0.05
rate_vector = 0.3
rate_table = 0.5
decay_matrix = 0.05
norm_eps = 1e-06
F32 = jnp.float32
BF16 = jnp.bfloat16
BIG = -1e30
ROOT_HALF = 0.5**0.5


def dot_nn(a, b):
    return lax.dot_general(a, b, (((1,), (0,)), ((), ())), preferred_element_type=F32)


def dot_nt(a, b):
    return lax.dot_general(a, b, (((1,), (1,)), ((), ())), preferred_element_type=F32)


def dot_tn(a, b):
    return lax.dot_general(a, b, (((0,), (0,)), ((), ())), preferred_element_type=F32)


def norm_parts(values):
    center = values - jnp.mean(values, axis=-1, keepdims=True)
    spread_sq = jnp.mean(center * center, axis=-1, keepdims=True)
    scale = lax.rsqrt(spread_sq + norm_eps)
    return center * scale, scale


def norm_back(grad, values, gain):
    unit, scale = norm_parts(values)
    inner = grad * gain
    back = scale * (
        inner
        - jnp.mean(inner, axis=-1, keepdims=True)
        - unit * jnp.mean(inner * unit, axis=-1, keepdims=True)
    )
    return back, jnp.sum(grad * unit, axis=0), jnp.sum(grad, axis=0)


def norm_back(grad, values, gain):
    unit, scale = norm_parts(values)
    inner = grad * gain
    back = scale * (
        inner
        - jnp.mean(inner, axis=-1, keepdims=True)
        - unit * jnp.mean(inner * unit, axis=-1, keepdims=True)
    )
    return back, jnp.sum(grad * unit, axis=0), jnp.sum(grad, axis=0)


ROWS = 48


def row_loop(rows, body):
    def step(i, _):
        body(pl.ds(pl.multiple_of(i * ROWS, ROWS), ROWS))
        return 0

    lax.fori_loop(0, rows // ROWS, step, 0)


def lane_low():
    return lax.broadcasted_iota(jnp.int32, (1, 2 * HD), 1) < HD


def halves(pair):
    low = lane_low()
    zero = jnp.zeros_like(pair)
    return jnp.where(low, pair, zero), jnp.where(low, zero, pair)


def softmax_rows(scores):
    e = jnp.exp(scores - jnp.max(scores, axis=-1, keepdims=True))
    return e * (1.0 / jnp.sum(e, axis=-1, keepdims=True))


def attention_loop(seqs, lp, half, body):
    pairs = half // (2 * HD)

    def step(s, _):
        rows = pl.ds(pl.multiple_of(s * lp, 16), lp)
        for hp in range(pairs):
            body(s, rows, hp * 2 * HD, 2 * hp)
        return 0

    lax.fori_loop(0, seqs, step, 0)


def attn_kernel(seqs, x, w, vec, bias, y1, qkv, att, r, middle, y2):
    rows, d = x.shape
    half = d // 2
    lp = rows // seqs
    t = pl.program_id(0)
    mine = pl.ds(pl.multiple_of(t * half, 128), half)

    def first_norm(at):
        unit, _ = norm_parts(x[at, :])
        y1[at, :] = (unit * vec[0:1, :] + vec[1:2, :]).astype(BF16)

    pl.when(t == 0)(lambda: row_loop(rows, first_norm))
    for k in range(3):
        mixed = dot_nn(y1[...], w[0, :, k * half : (k + 1) * half])
        if k != 1:
            row = 2 if k == 0 else 3
            mixed = mixed + vec[row : row + 1, mine]
        qkv[0, :, k * half : (k + 1) * half] = mixed.astype(BF16)

    def attend(s, at, col, head):
        q = qkv[0, at, pl.ds(col, 2 * HD)]
        k = qkv[0, at, pl.ds(half + col, 2 * HD)]
        v = qkv[0, at, pl.ds(2 * half + col, 2 * HD)]
        found = []
        for i, part in enumerate(halves(q)):
            scores = dot_nt(part, k) * HD**-0.5 + bias[head + i]
            found.append(dot_nn(softmax_rows(scores).astype(BF16), v))
        att[0, at, pl.ds(col, 2 * HD)] = jnp.where(lane_low(), found[0], found[1]).astype(BF16)

    attention_loop(seqs, lp, half, attend)
    part = dot_nt(att[0], w[0, :, 3 * half :])

    @pl.when(t == 0)
    def _():
        r[...] = part

    def second_norm(at):
        here = x[at, :] + vec[5:6, :] * (r[at, :] + vec[4:5, :])
        middle[at, :] = here
        unit, _ = norm_parts(here)
        y2[at, :] = (unit * vec[6:7, :] + vec[7:8, :]).astype(BF16)

    @pl.when(t == 1)
    def _():
        r[...] += part
        row_loop(rows, second_norm)


def feed_kernel(middle, y2, w_up, w_down, shift, vec, pre, hid, z, out):
    rows = middle.shape[0]
    i = pl.program_id(0)
    a = dot_nn(y2[...], w_up[0]) + shift[0]
    pre[0] = a
    h = (0.5 * a * (1.0 + lax.erf(a * ROOT_HALF))).astype(BF16)
    hid[0] = h
    part = dot_nt(h, w_down[0])

    @pl.when(i == 0)
    def _():
        z[...] = part

    @pl.when(i > 0)
    def _():
        z[...] += part

    def finish(at):
        out[at, :] = middle[at, :] + vec[9:10, :] * (z[at, :] + vec[8:9, :])

    pl.when(i == pl.num_programs(0) - 1)(lambda: row_loop(rows, finish))


def full(shape):
    return pl.BlockSpec(shape, functools.partial(lambda n, *_: (0,) * n, len(shape)))


def lead(shape):
    return pl.BlockSpec((1,) + tuple(shape[1:]), lambda i: (i,) + (0,) * (len(shape) - 1))


def heads_of(shape):
    return pl.BlockSpec((shape[0] // 2,) + tuple(shape[1:]), lambda i: (i, 0, 0))


def tiles(rows, cols, first=0):
    return pl.BlockSpec((1, rows, cols), lambda i: (i // 3, 0, first + i % 3))


def call(kernel, steps, ins, in_specs, outs, out_specs, scratch, name, flops):
    return pl.pallas_call(
        kernel,
        out_shape=outs,
        grid=(steps,),
        in_specs=in_specs,
        out_specs=out_specs,
        scratch_shapes=scratch,
        compiler_params=pltpu.CompilerParams(vmem_limit_bytes=60 * 2**20),
        cost_estimate=pl.CostEstimate(flops=flops, bytes_accessed=3 * 10**7, transcendentals=0),
        name=name,
    )(*ins)


def attn_spec(weights):
    return pl.BlockSpec((1, weights.shape[1], weights.shape[2] // 3), lambda i: (i, 0, 0))


def forward_layer(x, weights, vec, bias, seqs):
    rows, d = x.shape
    half, ff = d // 2, weights.shape[2] // 3
    tile = ff // 3
    s = jax.ShapeDtypeStruct
    wide, slim = s((rows, d), F32), s((rows, d), BF16)
    qkv, att = s((2, rows, 3 * half), BF16), s((2, rows, half), BF16)
    y1, qkv, att, r, middle, y2 = call(
        functools.partial(attn_kernel, seqs),
        2,
        [x, weights, vec, bias],
        [full(x.shape), attn_spec(weights), full(vec.shape), heads_of(bias.shape)],
        [slim, qkv, att, wide, wide, slim],
        [full(slim.shape), lead(qkv.shape), lead(att.shape)] + [full(wide.shape)] * 3,
        [],
        "attn",
        4 * 10**9,
    )
    shift = vec[10:14].reshape(6, 1, tile)
    pre, hid, z, out = call(
        feed_kernel,
        6,
        [middle, y2, weights, weights, shift, vec],
        [
            full(wide.shape),
            full(wide.shape),
            tiles(d, tile, 3),
            tiles(d, tile, 6),
            lead(shift.shape),
            full(vec.shape),
        ],
        [s((2, rows, ff), F32), s((2, rows, ff), BF16), wide, wide],
        [tiles(rows, tile), tiles(rows, tile), full(wide.shape), full(wide.shape)],
        [],
        "feed",
        6 * 10**9,
    )
    return out, (x, y1, qkv, att, r, middle, y2, pre, hid, z)


def norm_back_rows(grad, values, gain):
    unit, scale = norm_parts(values)
    inner = grad * gain
    back = scale * (
        inner
        - jnp.mean(inner, axis=-1, keepdims=True)
        - unit * jnp.mean(inner * unit, axis=-1, keepdims=True)
    )
    return back, unit


def col_sum(v):
    return jnp.sum(v, axis=0, keepdims=True)


def feed_back_kernel(
    g, z, hid, pre, middle, y2, vec, w_up, w_down, gm, g_up, g_down, sums, upb, dz, dy2
):
    rows = g.shape[0]
    i = pl.program_id(0)

    def first(at):
        here = g[at, :]
        scaled = here * vec[9:10, :]
        dz[at, :] = scaled.astype(BF16)
        sums[0:1, :] += col_sum(scaled)
        sums[1:2, :] += col_sum(here * (z[at, :] + vec[8:9, :]))

    @pl.when(i == 0)
    def _():
        sums[...] = jnp.zeros_like(sums)
        row_loop(rows, first)

    dh = dot_nn(dz[...], w_down[0])
    a = pre[0]
    slope = 0.5 * (1.0 + lax.erf(a * ROOT_HALF))
    slope = slope + a * (jnp.exp(-0.5 * a * a) * (2 * math.pi) ** -0.5)
    da = (dh * slope).astype(BF16)
    upb[0] = col_sum(da.astype(F32))
    g_down[0] = dot_tn(dz[...], hid[0]).astype(BF16)
    g_up[0] = dot_tn(y2[...], da).astype(BF16)
    part = dot_nt(da, w_up[0])

    @pl.when(i == 0)
    def _():
        dy2[...] = part

    @pl.when(i > 0)
    def _():
        dy2[...] += part

    def last(at):
        grad = dy2[at, :]
        back, unit = norm_back_rows(grad, middle[at, :], vec[6:7, :])
        gm[at, :] = g[at, :] + back
        sums[2:3, :] += col_sum(grad * unit)
        sums[3:4, :] += col_sum(grad)

    pl.when(i == pl.num_programs(0) - 1)(lambda: row_loop(rows, last))


def attn_back_kernel(
    seqs, gm, r, x, y1, qkv, att, bias, vec, w, g, g_attn, sums, rel, dr, do, dqkv, dy1
):
    rows, d = gm.shape
    half = d // 2
    lp = rows // seqs
    t = pl.program_id(0)
    mine = pl.ds(pl.multiple_of(t * half, 128), half)

    def first(at):
        here = gm[at, :]
        scaled = here * vec[5:6, :]
        dr[at, :] = scaled.astype(BF16)
        sums[0:1, :] += col_sum(scaled)
        sums[1:2, :] += col_sum(here * (r[at, :] + vec[4:5, :]))

    @pl.when(t == 0)
    def _():
        sums[...] = jnp.zeros_like(sums)
        row_loop(rows, first)

    g_attn[0, :, 3 * half :] = dot_tn(dr[...], att[0]).astype(BF16)
    do[...] = dot_nn(dr[...], w[0, :, 3 * half :]).astype(BF16)

    def attend(s, at, col, head):
        q = qkv[0, at, pl.ds(col, 2 * HD)]
        k = qkv[0, at, pl.ds(half + col, 2 * HD)]
        v = qkv[0, at, pl.ds(2 * half + col, 2 * HD)]
        o = do[at, pl.ds(col, 2 * HD)]
        dq, dk, dv = [], [], []
        for i, (q_part, o_part) in enumerate(zip(halves(q), halves(o))):
            p = softmax_rows(dot_nt(q_part, k) * HD**-0.5 + bias[head + i])
            dp = dot_nt(o_part, v)
            ds = (p * (dp - jnp.sum(p * dp, axis=-1, keepdims=True))).astype(BF16)
            more = ds.astype(F32)
            rel[head + i] = jnp.where(s == 0, more, rel[head + i] + more)
            dq.append(dot_nn(ds, k))
            dk.append(dot_tn(ds, q))
            dv.append(dot_tn(p.astype(BF16), o))
        low = lane_low()
        for k, pair in enumerate((dq, dk, dv)):
            value = jnp.where(low, pair[0], pair[1])
            if k < 2:
                value = value * HD**-0.5
            dqkv[at, pl.ds(k * half + col, 2 * HD)] = value.astype(BF16)

    attention_loop(seqs, lp, half, attend)
    total = 0.0
    for k in range(3):
        cols = slice(k * half, (k + 1) * half)
        part = dqkv[:, cols]
        if k != 1:
            row = 2 if k == 0 else 3
            sums[row : row + 1, mine] = col_sum(part.astype(F32))
        g_attn[0, :, cols] = dot_tn(y1[...], part).astype(BF16)
        total = total + dot_nt(part, w[0, :, cols])

    @pl.when(t == 0)
    def _():
        dy1[...] = total

    def last(at):
        grad = dy1[at, :]
        back, unit = norm_back_rows(grad, x[at, :], vec[0:1, :])
        g[at, :] = gm[at, :] + back
        sums[4:5, :] += col_sum(grad * unit)
        sums[5:6, :] += col_sum(grad)

    @pl.when(t == 1)
    def _():
        dy1[...] += total
        row_loop(rows, last)


def backward_layer(g, saved, weights, vec, bias, seqs):
    x, y1, qkv, att, r, middle, y2, pre, hid, z = saved
    rows, d = x.shape
    half, ff = d // 2, weights.shape[2] // 3
    tile = ff // 3
    s = jax.ShapeDtypeStruct
    part = s((2, d, ff), BF16)
    wide = full((rows, d))
    gm, g_up, g_down, low_sums, upb = call(
        feed_back_kernel,
        6,
        [g, z, hid, pre, middle, y2, vec, weights, weights],
        [wide, wide, tiles(rows, tile), tiles(rows, tile), wide, wide, full(vec.shape)]
        + [tiles(d, tile, 3), tiles(d, tile, 6)],
        [s((rows, d), F32), part, part, s((8, d), F32), s((6, 1, tile), F32)],
        [wide, tiles(d, tile), tiles(d, tile), full((8, d)), lead((6, 1, tile))],
        [pltpu.VMEM((rows, d), BF16), pltpu.VMEM((rows, d), F32)],
        "feed_back",
        12 * 10**9,
    )
    g, g_attn, top_sums, rel = call(
        functools.partial(attn_back_kernel, seqs),
        2,
        [gm, r, x, y1, qkv, att, bias, vec, weights],
        [wide, wide, wide, wide, lead(qkv.shape), lead(att.shape)]
        + [heads_of(bias.shape), full(vec.shape), attn_spec(weights)],
        [s((rows, d), F32), part, s((8, d), F32), s(bias.shape, F32)],
        [wide, lead(part.shape), full((8, d)), heads_of(bias.shape)],
        [
            pltpu.VMEM((rows, d), BF16),
            pltpu.VMEM((rows, half), BF16),
            pltpu.VMEM((rows, 3 * half), BF16),
            pltpu.VMEM((rows, d), F32),
        ],
        "attn_back",
        6 * 10**9,
    )
    vec_grad = jnp.concatenate(
        [
            top_sums[4:6],
            top_sums[2:4],
            top_sums[0:2],
            low_sums[2:4],
            low_sums[0:2],
            upb.reshape(4, d),
        ],
        axis=0,
    )
    return g, (g_attn, g_up, g_down), vec_grad, rel


def strip_constant(side):
    width = 2 * side - 1
    wide = -(-(width * side) // 128) * 128
    out = np.zeros((width * width, 16, wide), np.float32)
    for c in range(side):
        for k in range(width):
            for e in range(side):
                out[width * k + side - 1 - c + e, c, k * side + e] = 1.0
    return out.reshape(width * width, 16 * wide), wide


def split_three(v):
    high = lax.reduce_precision(v, 8, 7)
    rest = v - high
    mid = lax.reduce_precision(rest, 8, 7)
    return jnp.concatenate([high, mid, rest - mid], axis=0).astype(BF16)


def add_three(v):
    n = v.shape[0] // 3
    return v[:n] + v[n : 2 * n] + v[2 * n :]


def expand_kernel(side, strips, ends, out):
    def head(h, _):
        expand_head(side, strips, ends, out, h)
        return 0

    lax.fori_loop(0, out.shape[0], head, 0)


def expand_head(side, strips, ends, out, h):
    lp = out.shape[1]
    wide = strips.shape[2]
    tokens = side * side + 1
    a = strips[h]
    lane = lax.broadcasted_iota(jnp.int32, (1, lp), 1)
    row_end, col_end, corner = ends[h, 0:1, 0:1], ends[h, 0:1, 1:2], ends[h, 0:1, 2:3]
    top = jnp.where(lane == 0, corner, row_end)
    out[h, 0:1, :] = jnp.where(lane < tokens, top, BIG)
    for r in range(side):
        shift = (side - 1 - r) * side - 1
        moved = pltpu.roll(a, (wide - shift) % wide, 1)[:side, :lp]
        moved = jnp.where(lane == 0, col_end, moved)
        out[h, 1 + r * side : 1 + (r + 1) * side, :] = jnp.where(lane < tokens, moved, BIG)
    tail = jnp.where(lane < tokens, 0.0, BIG)
    out[h, tokens:, :] = jnp.broadcast_to(tail, (lp - tokens, lp))


def expand_bias(position, side, lp):
    layers, heads, entries = position.shape
    flat = position.reshape(layers * heads, entries)
    hot, wide = strip_constant(side)
    cells = hot.shape[0]
    strips = add_three(dot_nn(split_three(flat[:, :cells][:, ::-1]), jnp.asarray(hot, BF16)))
    strips = strips.reshape(layers * heads, 16, wide)
    ends = jnp.pad(flat[:, cells:], ((0, 0), (0, 125)))[:, None, :]
    found = []
    for l in range(layers):
        own = slice(l * heads, (l + 1) * heads)
        found.append(
            pl.pallas_call(
                functools.partial(expand_kernel, side),
                out_shape=jax.ShapeDtypeStruct((heads, lp, lp), F32),
                grid=(heads // 6,),
                in_specs=[
                    pl.BlockSpec((6, 16, wide), lambda i: (i, 0, 0)),
                    pl.BlockSpec((6, 1, 128), lambda i: (i, 0, 0)),
                ],
                out_specs=pl.BlockSpec((6, lp, lp), lambda i: (i, 0, 0)),
                name="expand",
            )(strips[own], ends[own])
        )
    return found


def fold_kernel(side, grads, strips, ends):
    def head(h, _):
        fold_head(side, grads, strips, ends, h)
        return 0

    lax.fori_loop(0, grads.shape[0], head, 0)


def fold_head(side, grads, strips, ends, h):
    lp = grads.shape[1]
    wide = strips.shape[2]
    tokens = side * side + 1
    lane = lax.broadcasted_iota(jnp.int32, (1, lp), 1)
    total = jnp.zeros((16, wide), F32)
    for r in range(side):
        shift = (side - 1 - r) * side - 1
        part = jnp.where(lane == 0, 0.0, grads[h, 1 + r * side : 1 + (r + 1) * side, :])
        part = jnp.concatenate([part, jnp.zeros((16 - side, lp), F32)], axis=0)
        part = jnp.concatenate([part, jnp.zeros((16, wide - lp), F32)], axis=1)
        total = total + pltpu.roll(part, shift % wide, 1)
    strips[h] = total
    corner = grads[h, 0:1, 0:1]
    row_end = jnp.sum(grads[h, 0:1, :], axis=1, keepdims=True) - corner
    col_end = jnp.sum(grads[h, 1:tokens, 0:1], axis=0, keepdims=True)
    out_lane = lax.broadcasted_iota(jnp.int32, (1, 128), 1)
    ends[h] = jnp.where(
        out_lane == 0, row_end, jnp.where(out_lane == 1, col_end, jnp.where(out_lane == 2, corner, 0.0))
    )


def fold_bias(layers, side):
    hot, wide = strip_constant(side)
    found = []
    for grads in layers:
        n, lp, _ = grads.shape
        found.append(
            pl.pallas_call(
                functools.partial(fold_kernel, side),
                out_shape=[
                    jax.ShapeDtypeStruct((n, 16, wide), F32),
                    jax.ShapeDtypeStruct((n, 1, 128), F32),
                ],
                grid=(n // 6,),
                in_specs=[pl.BlockSpec((6, lp, lp), lambda i: (i, 0, 0))],
                out_specs=[
                    pl.BlockSpec((6, 16, wide), lambda i: (i, 0, 0)),
                    pl.BlockSpec((6, 1, 128), lambda i: (i, 0, 0)),
                ],
                name="fold",
            )(grads)
        )
    strips = jnp.concatenate([f[0].reshape(-1, 16 * wide) for f in found], axis=0)
    ends = jnp.concatenate([f[1][:, 0, :3] for f in found], axis=0)
    cells = add_three(dot_nt(split_three(strips), jnp.asarray(hot, BF16)))
    flat = jnp.concatenate([cells[:, ::-1], ends], axis=1)
    return flat.reshape(len(layers), -1, flat.shape[1])


def adamw_update(master, gradient, first_mom, second_mom, step_rate, decay_rate):
    first_mom = beta_one * first_mom + (1.0 - beta_one) * gradient
    second_mom = beta_two * second_mom + (1.0 - beta_two) * gradient * gradient
    step_dir = (
        first_mom
        / (1.0 - beta_one**STEP)
        / (jnp.sqrt(second_mom / (1.0 - beta_two**STEP)) + adam_eps)
    )
    return (master - step_rate * (step_dir + decay_rate * master), first_mom, second_mom)


def update_kernel(layers, *refs):
    grads, refs = refs[: 3 * layers + 2], refs[3 * layers + 2 :]
    olds, news, copies = refs[:18], refs[18:36], refs[36:]

    def put(item, index, gradient, rate):
        old = [olds[3 * item + k][index] for k in range(3)]
        found = adamw_update(old[0], gradient, old[1], old[2], rate, decay_matrix)
        for k in range(3):
            news[3 * item + k][index] = found[k]
        if item >= 2:
            copies[item - 2][index] = found[0].astype(BF16)

    put(0, slice(None), grads[3 * layers + 1][...], rate_table)
    put(1, slice(None), grads[3 * layers][...], rate_matrix)
    for l in range(layers):
        attn, up, down = grads[3 * l : 3 * l + 3]
        half = attn.shape[1] // 4
        for k in range(3):
            put(2, (l, k), attn[:, k * half : (k + 1) * half], rate_matrix)
        put(3, l, attn[:, 3 * half :], rate_matrix)
        put(4, l, up[...], rate_matrix)
        put(5, l, down[...], rate_matrix)


def update_all(grads, olds):
    layers = (len(grads) - 2) // 3
    rows = grads[0].shape[0]
    block = 16 if rows % 16 == 0 else rows

    def spec(a):
        n = len(a.shape)
        return pl.BlockSpec(
            tuple(a.shape[:-2]) + (block, a.shape[-1]), lambda i: (0,) * (n - 2) + (i, 0)
        )

    outs = [jax.ShapeDtypeStruct(a.shape, F32) for a in olds]
    outs += [jax.ShapeDtypeStruct(olds[3 * k].shape, BF16) for k in range(2, 6)]
    return pl.pallas_call(
        functools.partial(update_kernel, layers),
        out_shape=outs,
        grid=(rows // block,),
        in_specs=[spec(a) for a in list(grads) + list(olds)],
        out_specs=[spec(a) for a in outs],
        compiler_params=pltpu.CompilerParams(vmem_limit_bytes=56 * 2**20),
        name="update",
    )(*grads, *olds)


def pack_layer(in_proj, out_proj, up_proj, down_proj):
    return jnp.concatenate(
        [in_proj[:, 0], in_proj[:, 1], in_proj[:, 2], out_proj, up_proj, down_proj], axis=1
    )


MESH = pl.DeviceIdType.MESH


def place():
    dp = lax.axis_index("dp")
    return lax.axis_index("tensor"), dp // 4, lax.rem(dp // 2, 2), lax.rem(dp, 2)


def at(x, z, y, c):
    return ((z * 2 + y) * 2 + c, x)


def near(v, step, size):
    return lax.rem(v + step, size)


def greet(peers):
    barrier = pltpu.get_barrier_semaphore()
    for peer in peers:
        pl.semaphore_signal(barrier, inc=1, device_id=peer, device_id_type=MESH)
    pl.semaphore_wait(barrier, len(peers))


def gather_kernel(wide, *refs):
    n = len(wide)
    srcs, dsts = refs[:n], refs[n : 2 * n]
    own_sem, send_sem, recv_sem = refs[2 * n :]
    x, z, y, c = place()
    peer_x, peer_y, peer_c = at(1 - x, z, y, c), at(x, z, 1 - y, c), at(x, z, y, 1 - c)
    up, down = at(x, jnp.minimum(z + 1, 3), y, c), at(x, jnp.maximum(z - 1, 0), y, c)
    barrier = pltpu.get_barrier_semaphore()
    for peer in (peer_x, peer_y, peer_c):
        pl.semaphore_signal(barrier, inc=1, device_id=peer, device_id_type=MESH)

    @pl.when(z < 3)
    def _():
        pl.semaphore_signal(barrier, inc=1, device_id=up, device_id_type=MESH)

    @pl.when(z > 0)
    def _():
        pl.semaphore_signal(barrier, inc=1, device_id=down, device_id_type=MESH)

    pl.semaphore_wait(barrier, 3 + jnp.where(z < 3, 1, 0) + jnp.where(z > 0, 1, 0))

    def slot(i, ox, oz, oy, oc):
        ref = dsts[i]
        dp = (oz * 2 + oy) * 2 + oc
        return ref.at[ox, dp] if wide[i] else ref.at[dp]

    Z, Y, X, C, Z2 = 0, 4, 8, 16, 32

    def make(i, src, origin, way, peer, two=False):
        ox, oz, oy, oc = origin
        if way == Z:
            k = Z + oz
        elif way == Y:
            k = Y + oz
        elif way == X:
            k = X + oy * 4 + oz
        else:
            k = C + (ox * 2 + oy) * 4 + oz
        return pltpu.make_async_remote_copy(
            src_ref=src,
            dst_ref=slot(i, *origin),
            send_sem=send_sem.at[i, Z2 if two else k],
            recv_sem=recv_sem.at[i, k],
            device_id=peer,
            device_id_type=MESH,
        )

    own = (x, z, y, c)
    locals_ = []
    for i in range(n):
        copy = pltpu.make_async_copy(srcs[i], slot(i, *own), own_sem.at[i])
        copy.start()
        locals_.append(copy)

    def spread(i, src, origin, ways):
        for way, peer in ((Y, peer_y), (X, peer_x), (C, peer_c)):
            if way in ways and (wide[i] or way != X):
                make(i, src, origin, way, peer).start()

    def begin(i):
        src = srcs[i]

        @pl.when(z < 3)
        def _():
            make(i, src, own, Z, up).start()

        @pl.when(z > 0)
        def _():
            make(i, src, own, Z, down, True).start()

        spread(i, src, own, (Y, X, C))

    def each_z(fn):
        for k in (1, 2, 3):
            pl.when(z - k >= 0)(functools.partial(fn, z - k, True))
            pl.when(z + k <= 3)(functools.partial(fn, z + k, False))

    def landed(i, origin, way, peer):
        ref = slot(i, *origin)
        make(i, ref, origin, way, peer).wait_recv()
        return ref

    def after_z(i):
        def one(oz, rising):
            origin = (x, oz, y, c)
            ref = landed(i, origin, Z, up)
            if rising:

                @pl.when(z < 3)
                def _():
                    make(i, ref, origin, Z, up).start()
            else:

                @pl.when(z > 0)
                def _():
                    make(i, ref, origin, Z, down).start()

            spread(i, ref, origin, (Y, X, C))

        each_z(one)

    def after_y(i):
        def one(oz, rising):
            origin = (x, oz, 1 - y, c)
            spread(i, landed(i, origin, Y, peer_y), origin, (X, C))

        one(z, True)
        each_z(one)

    def after_x(i):
        for oy in (y, 1 - y):

            def one(oz, rising):
                origin = (1 - x, oz, oy, c)
                spread(i, landed(i, origin, X, peer_x), origin, (C,))

            one(z, True)
            each_z(one)

    AHEAD = 1
    for i in range(min(AHEAD, n)):
        begin(i)
    for i in range(n + 2):
        if i + AHEAD < n:
            begin(i + AHEAD)
        if i < n:
            after_z(i)
        if 0 <= i - 1 < n:
            after_y(i - 1)
        if 0 <= i - 2 < n and wide[i - 2]:
            after_x(i - 2)
    for i in range(n):
        for ox in (0, 1) if wide[i] else (x,):
            for oy in (0, 1):
                for oz in range(4):
                    landed(i, (ox, oz, oy, 1 - c), C, peer_c)
                    make(i, slot(i, ox, oz, oy, c), (ox, oz, oy, c), C, peer_c).wait_send()
        for oz in range(4):
            make(i, slot(i, x, oz, y, c), (x, oz, y, c), Y, peer_y).wait_send()
        if wide[i]:
            for oy in (0, 1):
                for oz in range(4):
                    make(i, slot(i, x, oz, oy, c), (x, oz, oy, c), X, peer_x).wait_send()

        def sent(oz, rising):
            origin = (x, oz, y, c)
            pl.when(z < 3 if rising else z > 0)(
                lambda: make(i, slot(i, *origin), origin, Z, up).wait_send()
            )

        each_z(sent)
        pl.when(z < 3)(lambda: make(i, srcs[i], own, Z, up).wait_send())
        pl.when(z > 0)(lambda: make(i, srcs[i], own, Z, down, True).wait_send())
        locals_[i].wait()


def gather_all(shards, wide, cid):
    n = len(shards)
    outs = [
        jax.ShapeDtypeStruct(((2, 16) if w else (16,)) + s.shape, s.dtype)
        for s, w in zip(shards, wide)
    ]
    any_ = pl.BlockSpec(memory_space=pl.ANY)
    return pl.pallas_call(
        functools.partial(gather_kernel, wide),
        out_shape=outs,
        in_specs=[any_] * n,
        out_specs=[any_] * n,
        scratch_shapes=[
            pltpu.SemaphoreType.DMA((n,)),
            pltpu.SemaphoreType.DMA((n, 33)),
            pltpu.SemaphoreType.DMA((n, 33)),
        ],
        compiler_params=pltpu.CompilerParams(collective_id=cid, has_side_effects=True),
        name="gather",
    )(*shards)


RING = 3


def reduce_kernel(nw, nt, *refs):
    srcs, small = refs[: nw + nt], refs[nw + nt]
    outs, small_out = refs[nw + nt + 1 : 2 * (nw + nt) + 1], refs[2 * (nw + nt) + 1]
    accw, rcw, rxw, ryw, rzw, acct, rct, ryt, rzt, tot, rsm = refs[2 * (nw + nt) + 2 : -3]
    send_sem, recv_sem, free_sem = refs[-3:]
    x, z, y, c = place()
    zs = [near(z, k, 4) for k in (1, 2, 3)]
    peer_x, peer_y, peer_c = at(1 - x, z, y, c), at(x, z, 1 - y, c), at(x, z, y, 1 - c)
    greet([at(x, k, y, c) for k in zs] + [peer_x, peer_y, peer_c])
    counts = [0]

    def remote(src, dst, peer):
        k = counts[0]
        counts[0] += 1
        copy = pltpu.make_async_remote_copy(
            src_ref=src,
            dst_ref=dst,
            send_sem=send_sem.at[k],
            recv_sem=recv_sem.at[k],
            device_id=peer,
            device_id_type=MESH,
        )
        copy.start()
        return copy

    def local(src, dst):
        k = counts[0]
        counts[0] += 1
        copy = pltpu.make_async_copy(src, dst, send_sem.at[k])
        copy.start()
        return copy

    rw, rt = accw.shape[-2], acct.shape[-2]
    wide = [(i, j) for i in range(nw) for j in range(0, srcs[0].shape[-2], rw)]
    slim = [(nw + i, j) for i in range(nt) for j in range(0, srcs[nw].shape[-2], rt)]

    def group(kind, chunk, gx, gy, gc):
        i, j = chunk
        rows = pl.ds(j, rw if kind == "w" else rt)
        if kind == "w":
            return srcs[i].at[gx, :, gy, gc, rows, :]
        return srcs[i].at[:, gy, gc, rows, :]

    def groups(kind):
        if kind == "w":
            return [(1 - x, 1 - y), (1 - x, y), (x, 1 - y), (x, y)]
        return [(0, 1 - y), (0, y)]

    bufs = {"w": (accw, rcw, rxw, ryw, rzw), "t": (acct, rct, None, ryt, rzt)}
    chunks = {"w": wide, "t": slim}
    state = {}
    pending = []

    def add_into(dst, other):
        def body(k, _):
            dst[k] = dst[k] + other[k]
            return 0

        lax.fori_loop(0, dst.shape[0], body, 0)

    def fetch(kind, k):
        acc, rc = bufs[kind][:2]
        items = []
        if k >= RING:
            pl.semaphore_wait(free_sem.at[0 if kind == "w" else 1], 1)
        for g, (gx, gy) in enumerate(groups(kind)):
            mine = local(group(kind, chunks[kind][k], gx, gy, c), acc.at[k, g])
            other = remote(group(kind, chunks[kind][k], gx, gy, 1 - c), rc.at[k % RING, g], peer_c)
            items.append((mine, other))
        state[kind, k] = items

    def core_sum(kind, k):
        acc, rc, rx, ry, _ = bufs[kind]
        sent = []
        for g, (mine, other) in enumerate(state[kind, k]):
            mine.wait()
            other.wait_recv()
            pending.append(other)
            add_into(acc.at[k, g], rc.at[k % RING, g])
            if kind == "w" and g < 2:
                sent.append(remote(acc.at[k, g], rx.at[k, g], peer_x))
            if kind == "t" and g == 0:
                sent.append(remote(acc.at[k, g], ry.at[k], peer_y))
        if k + RING < len(chunks[kind]):
            pl.semaphore_signal(
                free_sem.at[0 if kind == "w" else 1], inc=1, device_id=peer_c, device_id_type=MESH
            )
        state[kind, k] = sent

    def after_x(k):
        sent = state["w", k]
        for g in range(2):
            sent[g].wait_recv()
            pending.append(sent[g])
            add_into(accw.at[k, 2 + g], rxw.at[k, g])
            if g == 0:
                state["w", k] = [remote(accw.at[k, 2], ryw.at[k], peer_y)]

    def after_y(kind, k):
        acc, _, _, ry, rz = bufs[kind]
        last = 3 if kind == "w" else 1
        copy = state[kind, k][0]
        copy.wait_recv()
        pending.append(copy)
        add_into(acc.at[k, last], ry.at[k])
        state[kind, k] = [
            remote(acc.at[k, last, zs[s]], rz.at[k, 2 - s], at(x, zs[s], y, c)) for s in range(3)
        ]

    def after_z(kind, k):
        acc, _, _, _, rz = bufs[kind]
        last = 3 if kind == "w" else 1
        total = acc[k, last, z].astype(F32)
        for s in range(3):
            state[kind, k][s].wait_recv()
            pending.append(state[kind, k][s])
        for s in range(3):
            total = total + rz[k, s].astype(F32)
        i, j = chunks[kind][k]
        outs[i][j : j + total.shape[0], :] = total

    tot[0] = small[...]
    flips = [peer_c, peer_x, peer_y]
    flips += [at(x, z + 1 - 2 * lax.rem(z, 2), y, c), at(x, lax.rem(z + 2, 4), y, c)]
    small_state = []

    def small_step(s):
        if s > 0:
            copy = small_state[-1]
            copy.wait_recv()
            pending.append(copy)
            tot[s] = tot[s - 1] + rsm[s - 1]
        if s < len(flips):
            small_state.append(remote(tot.at[s], rsm.at[s], flips[s]))

    n, m = len(wide), len(slim)
    fetch("w", 0)
    fetch("t", 0)
    for k in range(max(n, m) + 4):
        if k + 1 < n:
            fetch("w", k + 1)
        if k < n:
            core_sum("w", k)
        if k + 1 < m:
            fetch("t", k + 1)
        if k < m:
            core_sum("t", k)
        if k <= len(flips):
            small_step(k)
        if 0 <= k - 1 < n:
            after_x(k - 1)
        if 0 <= k - 1 < m:
            after_y("t", k - 1)
        if 0 <= k - 2 < n:
            after_y("w", k - 2)
        if 0 <= k - 2 < m:
            after_z("t", k - 2)
        if 0 <= k - 3 < n:
            after_z("w", k - 3)
    small_out[...] = tot[len(flips)]
    for copy in pending:
        copy.wait_send()


def reduce_all(wide, slim, small, cid):
    nw, nt = len(wide), len(slim)
    rows, cw = wide[0].shape[-2:]
    ct = slim[0].shape[-1]
    kw, kt = nw, nt * rows // 16
    outs = [jax.ShapeDtypeStruct((rows, a.shape[-1]), F32) for a in wide + slim]
    outs.append(jax.ShapeDtypeStruct(small.shape, F32))
    copies = kw * (8 + 2 + 1 + 3) + kt * (4 + 1 + 3) + 5
    any_ = pl.BlockSpec(memory_space=pl.ANY)
    vm = pl.BlockSpec(memory_space=pltpu.VMEM)
    return pl.pallas_call(
        functools.partial(reduce_kernel, nw, nt),
        out_shape=outs,
        in_specs=[any_] * (nw + nt) + [vm],
        out_specs=[vm] * (nw + nt + 1),
        scratch_shapes=[
            pltpu.VMEM((kw, 4, 4, rows, cw), BF16),
            pltpu.VMEM((RING, 4, 4, rows, cw), BF16),
            pltpu.VMEM((kw, 2, 4, rows, cw), BF16),
            pltpu.VMEM((kw, 4, rows, cw), BF16),
            pltpu.VMEM((kw, 3, rows, cw), BF16),
            pltpu.VMEM((kt, 2, 4, 16, ct), BF16),
            pltpu.VMEM((RING, 2, 4, 16, ct), BF16),
            pltpu.VMEM((kt, 4, 16, ct), BF16),
            pltpu.VMEM((kt, 3, 16, ct), BF16),
            pltpu.VMEM((6,) + small.shape, F32),
            pltpu.VMEM((5,) + small.shape, F32),
            pltpu.SemaphoreType.DMA((copies,)),
            pltpu.SemaphoreType.DMA((copies,)),
            pltpu.SemaphoreType.REGULAR((2,)),
        ],
        compiler_params=pltpu.CompilerParams(
            collective_id=cid, has_side_effects=True, vmem_limit_bytes=62 * 2**20
        ),
        name="reduce",
    )(*wide, *slim, small)


def gather_plain(shards, wide):
    full = [lax.all_gather(s, "dp") for s in shards]
    return [lax.all_gather(f, "tensor") if w else f for f, w in zip(full, wide)]


def reduce_plain(wide, slim, small):
    outs = []
    for grads in wide:
        part = lax.psum_scatter(grads, "tensor", scatter_dimension=0, tiled=False)
        outs.append(lax.psum_scatter(part, "dp", scatter_dimension=0, tiled=False).astype(F32))
    for grads in slim:
        outs.append(lax.psum_scatter(grads, "dp", scatter_dimension=0, tiled=False).astype(F32))
    outs.append(lax.psum(small, ("dp", "tensor")))
    return outs


def local(
    token_codes,
    mask_slots,
    mask_counts,
    embedding,
    emb_first,
    emb_second,
    readout,
    read_first,
    read_second,
    in_proj,
    in_first,
    in_second,
    out_proj,
    out_first,
    out_second,
    up_proj,
    up_first,
    up_second,
    down_proj,
    down_first,
    down_second,
    vectors,
    vec_first,
    vec_second,
    position,
    pos_first,
    pos_second,
):
    tensor_at = lax.axis_index("tensor")
    tensor_size = lax.axis_size("tensor")
    seqs, patches = token_codes.shape
    side = math.isqrt(patches)
    tokens = patches + 1
    lp = -(-tokens // 16) * 16
    slots = mask_slots.shape[1]
    mine = seqs // tensor_size
    layers = in_proj.shape[0]
    tail = vectors.shape[0] - 4
    half_vocab = embedding.shape[0]
    vocab_start = tensor_at * half_vocab
    d = vectors.shape[1]

    live_slot = jnp.arange(slots)[None, :] < mask_counts[:, None]
    hits = (mask_slots[:, :, None] == jnp.arange(patches)[None, None, :])
    masked = jnp.any(hits & live_slot[:, :, None], axis=1)
    targets = jnp.sum(jnp.where(hits, token_codes[:, None, :], 0), axis=2)
    count_here = jnp.sum(mask_counts.astype(F32))
    dp_size = lax.axis_size("dp")
    custom = dp_size == 16 and tensor_size == 2

    shards = [
        pack_layer(in_proj[l], out_proj[l], up_proj[l], down_proj[l]).astype(BF16)
        for l in range(layers)
    ]
    peer_at = 1 - tensor_at

    def swap(value):
        return lax.ppermute(value, "tensor", [(0, 1), (1, 0)])

    def side_of(value, where):
        return lax.dynamic_slice_in_dim(value, where * mine, mine, 0)

    code_rows = jnp.where(masked, -1, token_codes - vocab_start)
    code_rows = jnp.pad(code_rows, ((0, 0), (1, lp - tokens)), constant_values=-1)
    codes = jnp.arange(half_vocab)[None, :]
    peer_hot = (side_of(code_rows, peer_at).reshape(-1, 1) == codes).astype(BF16)
    own_hot = (side_of(code_rows, tensor_at).reshape(-1, 1) == codes).astype(BF16)
    biases = expand_bias(position, side, lp)
    first_shard, biases, peer_hot, own_hot = lax.optimization_barrier(
        (shards[0], biases, peer_hot, own_hot)
    )
    sources = [first_shard, jnp.full((8, 128), count_here), embedding.T.astype(BF16)]
    wide = (True, False, False)
    found = gather_all(sources, wide, 1) if custom else gather_plain(sources, wide)
    mask_total = jnp.sum(found[1][:, 0, 0])
    weights = [found[0].reshape(2, d, -1)]
    emb_table = found[2].reshape(d, half_vocab)
    weights.append(lax.all_gather(shards[1], ("tensor", "dp")).reshape(2, d, -1))
    read_table = lax.all_gather(readout.T.astype(BF16), "dp").reshape(d, half_vocab)

    came = swap(dot_nt(peer_hot, emb_table).astype(BF16))
    own_part = lax.optimization_barrier(dot_nt(own_hot, emb_table).astype(BF16))
    summed = own_part.astype(F32) + came.astype(F32)
    my_masked = side_of(masked, tensor_at)
    mask_flag = jnp.pad(my_masked.astype(F32), ((0, 0), (1, lp - tokens))).reshape(-1, 1)
    lead_flag = jnp.zeros((mine, lp), F32).at[:, 0].set(1.0).reshape(-1, 1)
    x = summed + lead_flag * vectors[tail] + mask_flag * vectors[tail + 1]

    kept = []
    for l in range(layers):
        x, saved = forward_layer(x, weights[l], vectors[14 * l : 14 * l + 14], biases[l], mine)
        kept.append(saved)

    my_slots = side_of(mask_slots, tensor_at)
    pick = (jnp.arange(mine)[:, None] * lp + 1 + my_slots).reshape(-1)
    final_in = x[pick]
    unit, _ = norm_parts(final_in)
    u = (unit * vectors[tail + 2] + vectors[tail + 3]).astype(BF16)
    u_peer = swap(u)
    places = [tensor_at, peer_at]
    logits, stats, target_hot = [], [], []
    for rows, where in zip((u, u_peer), places):
        lg = dot_nn(rows, read_table)
        hot = codes == (side_of(targets, where).reshape(-1) - vocab_start)[:, None]
        peak = jnp.max(lg, axis=1)
        total = jnp.sum(jnp.exp(lg - peak[:, None]), axis=1)
        chosen = jnp.sum(jnp.where(hot, lg, 0.0), axis=1)
        logits.append(lg)
        target_hot.append(hot)
        stats.append(jnp.stack([peak, total, chosen]))
    both = jnp.stack(stats)
    other = swap(both)[::-1]
    top = jnp.maximum(both[:, 0], other[:, 0])
    log_total = top + jnp.log(
        both[:, 1] * jnp.exp(both[:, 0] - top) + other[:, 1] * jnp.exp(other[:, 0] - top)
    )
    weight_row = live_slot.astype(F32)
    weights_of = [side_of(weight_row, where).reshape(-1) for where in places]
    losses = log_total - both[:, 2] - other[:, 2]
    loss_here = jnp.sum(losses * jnp.stack(weights_of))
    g_logits = [
        ((jnp.exp(logits[i] - log_total[i][:, None]) - target_hot[i].astype(F32)) * (weights_of[i] / mask_total)[:, None]).astype(BF16)
        for i in range(2)
    ]
    came = swap(dot_nt(g_logits[1], read_table).astype(BF16))
    grad_read = dot_tn(jnp.concatenate([u, u_peer]), jnp.concatenate(g_logits))
    grad_final = dot_nt(g_logits[0], read_table).astype(BF16).astype(F32) + came.astype(F32)
    back, g_gain, g_shift = norm_back(grad_final, final_in, vectors[tail + 2])
    g = jnp.zeros_like(x).at[pick].add(back)

    mat_grads = [None] * layers
    vec_grads = [None] * layers
    rel_grads = [None] * layers
    for l in reversed(range(layers)):
        g, full, vec_grads[l], rel = backward_layer(
            g, kept[l], weights[l], vectors[14 * l : 14 * l + 14], biases[l], mine
        )
        mat_grads[l] = full
        rel_grads[l] = rel

    g0 = g.astype(BF16)
    g0, rel_grads[0], rel_grads[1] = lax.optimization_barrier((g0, rel_grads[0], rel_grads[1]))
    grad_lead = jnp.sum(g0.astype(F32) * lead_flag, axis=0)
    grad_mask = jnp.sum(g0.astype(F32) * mask_flag, axis=0)
    g0_peer = swap(g0)
    grad_emb = dot_tn(
        jnp.concatenate([g0, g0_peer]), jnp.concatenate([own_hot, peer_hot])
    )
    vec_local = jnp.concatenate(
        vec_grads + [jnp.stack([grad_lead, grad_mask, g_gain, g_shift])], axis=0
    )
    small_parts = [vec_local, fold_bias(rel_grads, side), loss_here / tensor_size]
    flat = jnp.concatenate([p.reshape(-1) for p in small_parts])
    flat = jnp.pad(flat, (0, -flat.size % 1024)).reshape(-1, 128)
    if custom:
        lead = (4, 2, 2, d // 16)
        reduced = reduce_all(
            [m.reshape((2,) + lead + m.shape[-1:]) for layer in mat_grads for m in layer],
            [m.astype(BF16).reshape(lead + m.shape[-1:]) for m in (grad_read, grad_emb)],
            flat,
            2,
        )
    else:
        lead = (dp_size, d // dp_size)
        reduced = reduce_plain(
            [m.reshape((2,) + lead + m.shape[-1:]) for layer in mat_grads for m in layer],
            [m.astype(BF16).reshape(lead + m.shape[-1:]) for m in (grad_read, grad_emb)],
            flat,
        )
    flat = reduced[-1]
    flat = flat.reshape(-1)
    vec_all = flat[: vectors.size].reshape(vectors.shape)
    rel_all = flat[vectors.size : vectors.size + position.size].reshape(position.shape)
    loss_sum = flat[vectors.size + position.size]

    tables = [a.T for a in (embedding, emb_first, emb_second, readout, read_first, read_second)]
    ins = [a.transpose(0, 2, 1, 3) for a in (in_proj, in_first, in_second)]
    others = [
        out_proj,
        out_first,
        out_second,
        up_proj,
        up_first,
        up_second,
        down_proj,
        down_first,
        down_second,
    ]
    new = update_all(list(reduced[:-1]), tables + ins + others)
    tables = tuple(a.T for a in new[:6])
    ins = tuple(a.transpose(0, 2, 1, 3) for a in new[6:9])
    copies = (new[18].transpose(0, 2, 1, 3),) + tuple(new[19:])
    vec_new = adamw_update(vectors, vec_all, vec_first, vec_second, rate_vector, 0.0)
    pos_new = adamw_update(position, rel_all, pos_first, pos_second, rate_vector, 0.0)
    return (
        (loss_sum, mask_total) + tables + ins + tuple(new[9:18]) + vec_new + pos_new + copies
    )


def solution(mesh):
    table = P("tensor", "dp")
    in_spec = P(None, "dp", None, "tensor")
    mat = P(None, "dp", "tensor")
    return jax.shard_map(
        local,
        mesh=mesh,
        in_specs=(P("dp", None), P("dp", None), P("dp"))
        + (table,) * 6
        + (in_spec,) * 3
        + (mat,) * 9
        + (P(),) * 6,
        out_specs=(P(), P())
        + (table,) * 6
        + (in_spec,) * 3
        + (mat,) * 9
        + (P(),) * 6
        + (in_spec, mat, mat, mat),
        check_vma=False,
    )
```

```python
import functools
import math

import jax
import jax.numpy as jnp
import numpy as np
from jax import lax
from jax.experimental import pallas as pl
from jax.experimental.pallas import tpu as pltpu
from jax.sharding import PartitionSpec as P

HEADS = 12
HD = 64
STEP = 5

beta_one = 0.5
beta_two = 0.5
adam_eps = 1e-08
rate_matrix = 0.05
rate_vector = 0.3
rate_table = 0.5
decay_matrix = 0.05
norm_eps = 1e-06
F32 = jnp.float32
BF16 = jnp.bfloat16
BIG = -1e30
ROOT_HALF = 0.5**0.5


def dot_nn(a, b):
    return lax.dot_general(a, b, (((1,), (0,)), ((), ())), preferred_element_type=F32)


def dot_nt(a, b):
    return lax.dot_general(a, b, (((1,), (1,)), ((), ())), preferred_element_type=F32)


def dot_tn(a, b):
    return lax.dot_general(a, b, (((0,), (0,)), ((), ())), preferred_element_type=F32)


def norm_parts(values):
    center = values - jnp.mean(values, axis=-1, keepdims=True)
    spread_sq = jnp.mean(center * center, axis=-1, keepdims=True)
    scale = lax.rsqrt(spread_sq + norm_eps)
    return center * scale, scale


def norm_back(grad, values, gain):
    unit, scale = norm_parts(values)
    inner = grad * gain
    back = scale * (
        inner
        - jnp.mean(inner, axis=-1, keepdims=True)
        - unit * jnp.mean(inner * unit, axis=-1, keepdims=True)
    )
    return back, jnp.sum(grad * unit, axis=0), jnp.sum(grad, axis=0)


def norm_back(grad, values, gain):
    unit, scale = norm_parts(values)
    inner = grad * gain
    back = scale * (
        inner
        - jnp.mean(inner, axis=-1, keepdims=True)
        - unit * jnp.mean(inner * unit, axis=-1, keepdims=True)
    )
    return back, jnp.sum(grad * unit, axis=0), jnp.sum(grad, axis=0)


ROWS = 48


def row_loop(rows, body):
    def step(i, _):
        body(pl.ds(pl.multiple_of(i * ROWS, ROWS), ROWS))
        return 0

    lax.fori_loop(0, rows // ROWS, step, 0)


def lane_low():
    return lax.broadcasted_iota(jnp.int32, (1, 2 * HD), 1) < HD


def halves(pair):
    low = lane_low()
    zero = jnp.zeros_like(pair)
    return jnp.where(low, pair, zero), jnp.where(low, zero, pair)


def softmax_rows(scores):
    e = jnp.exp(scores - jnp.max(scores, axis=-1, keepdims=True))
    return e * (1.0 / jnp.sum(e, axis=-1, keepdims=True))


def attention_loop(seqs, lp, half, body):
    pairs = half // (2 * HD)

    def step(s, _):
        rows = pl.ds(pl.multiple_of(s * lp, 16), lp)
        for hp in range(pairs):
            body(s, rows, hp * 2 * HD, 2 * hp)
        return 0

    lax.fori_loop(0, seqs, step, 0)


def attn_kernel(seqs, x, w, vec, bias, y1, qkv, att, r, middle, y2):
    rows, d = x.shape
    half = d // 2
    lp = rows // seqs
    t = pl.program_id(0)
    mine = pl.ds(pl.multiple_of(t * half, 128), half)

    def first_norm(at):
        unit, _ = norm_parts(x[at, :])
        y1[at, :] = (unit * vec[0:1, :] + vec[1:2, :]).astype(BF16)

    pl.when(t == 0)(lambda: row_loop(rows, first_norm))
    for k in range(3):
        mixed = dot_nn(y1[...], w[0, :, k * half : (k + 1) * half])
        if k != 1:
            row = 2 if k == 0 else 3
            mixed = mixed + vec[row : row + 1, mine]
        qkv[0, :, k * half : (k + 1) * half] = mixed.astype(BF16)

    def attend(s, at, col, head):
        q = qkv[0, at, pl.ds(col, 2 * HD)]
        k = qkv[0, at, pl.ds(half + col, 2 * HD)]
        v = qkv[0, at, pl.ds(2 * half + col, 2 * HD)]
        found = []
        for i, part in enumerate(halves(q)):
            scores = dot_nt(part, k) * HD**-0.5 + bias[head + i]
            found.append(dot_nn(softmax_rows(scores).astype(BF16), v))
        att[0, at, pl.ds(col, 2 * HD)] = jnp.where(lane_low(), found[0], found[1]).astype(BF16)

    attention_loop(seqs, lp, half, attend)
    part = dot_nt(att[0], w[0, :, 3 * half :])

    @pl.when(t == 0)
    def _():
        r[...] = part

    def second_norm(at):
        here = x[at, :] + vec[5:6, :] * (r[at, :] + vec[4:5, :])
        middle[at, :] = here
        unit, _ = norm_parts(here)
        y2[at, :] = (unit * vec[6:7, :] + vec[7:8, :]).astype(BF16)

    @pl.when(t == 1)
    def _():
        r[...] += part
        row_loop(rows, second_norm)


def feed_kernel(middle, y2, w_up, w_down, shift, vec, pre, hid, z, out):
    rows = middle.shape[0]
    i = pl.program_id(0)
    a = dot_nn(y2[...], w_up[0]) + shift[0]
    pre[0] = a
    h = (0.5 * a * (1.0 + lax.erf(a * ROOT_HALF))).astype(BF16)
    hid[0] = h
    part = dot_nt(h, w_down[0])

    @pl.when(i == 0)
    def _():
        z[...] = part

    @pl.when(i > 0)
    def _():
        z[...] += part

    def finish(at):
        out[at, :] = middle[at, :] + vec[9:10, :] * (z[at, :] + vec[8:9, :])

    pl.when(i == pl.num_programs(0) - 1)(lambda: row_loop(rows, finish))


def full(shape):
    return pl.BlockSpec(shape, functools.partial(lambda n, *_: (0,) * n, len(shape)))


def lead(shape):
    return pl.BlockSpec((1,) + tuple(shape[1:]), lambda i: (i,) + (0,) * (len(shape) - 1))


def heads_of(shape):
    return pl.BlockSpec((shape[0] // 2,) + tuple(shape[1:]), lambda i: (i, 0, 0))


def tiles(rows, cols, first=0):
    return pl.BlockSpec((1, rows, cols), lambda i: (i // 3, 0, first + i % 3))


def call(kernel, steps, ins, in_specs, outs, out_specs, scratch, name, flops):
    return pl.pallas_call(
        kernel,
        out_shape=outs,
        grid=(steps,),
        in_specs=in_specs,
        out_specs=out_specs,
        scratch_shapes=scratch,
        compiler_params=pltpu.CompilerParams(vmem_limit_bytes=60 * 2**20),
        cost_estimate=pl.CostEstimate(flops=flops, bytes_accessed=3 * 10**7, transcendentals=0),
        name=name,
    )(*ins)


def attn_spec(weights):
    return pl.BlockSpec((1, weights.shape[1], weights.shape[2] // 3), lambda i: (i, 0, 0))


def forward_layer(x, weights, vec, bias, seqs):
    rows, d = x.shape
    half, ff = d // 2, weights.shape[2] // 3
    tile = ff // 3
    s = jax.ShapeDtypeStruct
    wide, slim = s((rows, d), F32), s((rows, d), BF16)
    qkv, att = s((2, rows, 3 * half), BF16), s((2, rows, half), BF16)
    y1, qkv, att, r, middle, y2 = call(
        functools.partial(attn_kernel, seqs),
        2,
        [x, weights, vec, bias],
        [full(x.shape), attn_spec(weights), full(vec.shape), heads_of(bias.shape)],
        [slim, qkv, att, wide, wide, slim],
        [full(slim.shape), lead(qkv.shape), lead(att.shape)] + [full(wide.shape)] * 3,
        [],
        "attn",
        4 * 10**9,
    )
    shift = vec[10:14].reshape(6, 1, tile)
    pre, hid, z, out = call(
        feed_kernel,
        6,
        [middle, y2, weights, weights, shift, vec],
        [
            full(wide.shape),
            full(wide.shape),
            tiles(d, tile, 3),
            tiles(d, tile, 6),
            lead(shift.shape),
            full(vec.shape),
        ],
        [s((2, rows, ff), F32), s((2, rows, ff), BF16), wide, wide],
        [tiles(rows, tile), tiles(rows, tile), full(wide.shape), full(wide.shape)],
        [],
        "feed",
        6 * 10**9,
    )
    return out, (x, y1, qkv, att, r, middle, y2, pre, hid, z)


def norm_back_rows(grad, values, gain):
    unit, scale = norm_parts(values)
    inner = grad * gain
    back = scale * (
        inner
        - jnp.mean(inner, axis=-1, keepdims=True)
        - unit * jnp.mean(inner * unit, axis=-1, keepdims=True)
    )
    return back, unit


def col_sum(v):
    return jnp.sum(v, axis=0, keepdims=True)


def feed_back_kernel(
    g, z, hid, pre, middle, y2, vec, w_up, w_down, gm, g_up, g_down, sums, upb, dz, dy2
):
    rows = g.shape[0]
    i = pl.program_id(0)

    def first(at):
        here = g[at, :]
        scaled = here * vec[9:10, :]
        dz[at, :] = scaled.astype(BF16)
        sums[0:1, :] += col_sum(scaled)
        sums[1:2, :] += col_sum(here * (z[at, :] + vec[8:9, :]))

    @pl.when(i == 0)
    def _():
        sums[...] = jnp.zeros_like(sums)
        row_loop(rows, first)

    dh = dot_nn(dz[...], w_down[0])
    a = pre[0]
    slope = 0.5 * (1.0 + lax.erf(a * ROOT_HALF))
    slope = slope + a * (jnp.exp(-0.5 * a * a) * (2 * math.pi) ** -0.5)
    da = (dh * slope).astype(BF16)
    upb[0] = col_sum(da.astype(F32))
    g_down[0] = dot_tn(dz[...], hid[0]).astype(BF16)
    g_up[0] = dot_tn(y2[...], da).astype(BF16)
    part = dot_nt(da, w_up[0])

    @pl.when(i == 0)
    def _():
        dy2[...] = part

    @pl.when(i > 0)
    def _():
        dy2[...] += part

    def last(at):
        grad = dy2[at, :]
        back, unit = norm_back_rows(grad, middle[at, :], vec[6:7, :])
        gm[at, :] = g[at, :] + back
        sums[2:3, :] += col_sum(grad * unit)
        sums[3:4, :] += col_sum(grad)

    pl.when(i == pl.num_programs(0) - 1)(lambda: row_loop(rows, last))


def attn_back_kernel(
    seqs, gm, r, x, y1, qkv, att, bias, vec, w, g, g_attn, sums, rel, dr, do, dqkv, dy1
):
    rows, d = gm.shape
    half = d // 2
    lp = rows // seqs
    t = pl.program_id(0)
    mine = pl.ds(pl.multiple_of(t * half, 128), half)

    def first(at):
        here = gm[at, :]
        scaled = here * vec[5:6, :]
        dr[at, :] = scaled.astype(BF16)
        sums[0:1, :] += col_sum(scaled)
        sums[1:2, :] += col_sum(here * (r[at, :] + vec[4:5, :]))

    @pl.when(t == 0)
    def _():
        sums[...] = jnp.zeros_like(sums)
        row_loop(rows, first)

    g_attn[0, :, 3 * half :] = dot_tn(dr[...], att[0]).astype(BF16)
    do[...] = dot_nn(dr[...], w[0, :, 3 * half :]).astype(BF16)

    def attend(s, at, col, head):
        q = qkv[0, at, pl.ds(col, 2 * HD)]
        k = qkv[0, at, pl.ds(half + col, 2 * HD)]
        v = qkv[0, at, pl.ds(2 * half + col, 2 * HD)]
        o = do[at, pl.ds(col, 2 * HD)]
        dq, dk, dv = [], [], []
        for i, (q_part, o_part) in enumerate(zip(halves(q), halves(o))):
            p = softmax_rows(dot_nt(q_part, k) * HD**-0.5 + bias[head + i])
            dp = dot_nt(o_part, v)
            ds = (p * (dp - jnp.sum(p * dp, axis=-1, keepdims=True))).astype(BF16)
            more = ds.astype(F32)
            rel[head + i] = jnp.where(s == 0, more, rel[head + i] + more)
            dq.append(dot_nn(ds, k))
            dk.append(dot_tn(ds, q))
            dv.append(dot_tn(p.astype(BF16), o))
        low = lane_low()
        for k, pair in enumerate((dq, dk, dv)):
            value = jnp.where(low, pair[0], pair[1])
            if k < 2:
                value = value * HD**-0.5
            dqkv[at, pl.ds(k * half + col, 2 * HD)] = value.astype(BF16)

    attention_loop(seqs, lp, half, attend)
    total = 0.0
    for k in range(3):
        cols = slice(k * half, (k + 1) * half)
        part = dqkv[:, cols]
        if k != 1:
            row = 2 if k == 0 else 3
            sums[row : row + 1, mine] = col_sum(part.astype(F32))
        g_attn[0, :, cols] = dot_tn(y1[...], part).astype(BF16)
        total = total + dot_nt(part, w[0, :, cols])

    @pl.when(t == 0)
    def _():
        dy1[...] = total

    def last(at):
        grad = dy1[at, :]
        back, unit = norm_back_rows(grad, x[at, :], vec[0:1, :])
        g[at, :] = gm[at, :] + back
        sums[4:5, :] += col_sum(grad * unit)
        sums[5:6, :] += col_sum(grad)

    @pl.when(t == 1)
    def _():
        dy1[...] += total
        row_loop(rows, last)


def backward_layer(g, saved, weights, vec, bias, seqs):
    x, y1, qkv, att, r, middle, y2, pre, hid, z = saved
    rows, d = x.shape
    half, ff = d // 2, weights.shape[2] // 3
    tile = ff // 3
    s = jax.ShapeDtypeStruct
    part = s((2, d, ff), BF16)
    wide = full((rows, d))
    gm, g_up, g_down, low_sums, upb = call(
        feed_back_kernel,
        6,
        [g, z, hid, pre, middle, y2, vec, weights, weights],
        [wide, wide, tiles(rows, tile), tiles(rows, tile), wide, wide, full(vec.shape)]
        + [tiles(d, tile, 3), tiles(d, tile, 6)],
        [s((rows, d), F32), part, part, s((8, d), F32), s((6, 1, tile), F32)],
        [wide, tiles(d, tile), tiles(d, tile), full((8, d)), lead((6, 1, tile))],
        [pltpu.VMEM((rows, d), BF16), pltpu.VMEM((rows, d), F32)],
        "feed_back",
        12 * 10**9,
    )
    g, g_attn, top_sums, rel = call(
        functools.partial(attn_back_kernel, seqs),
        2,
        [gm, r, x, y1, qkv, att, bias, vec, weights],
        [wide, wide, wide, wide, lead(qkv.shape), lead(att.shape)]
        + [heads_of(bias.shape), full(vec.shape), attn_spec(weights)],
        [s((rows, d), F32), part, s((8, d), F32), s(bias.shape, F32)],
        [wide, lead(part.shape), full((8, d)), heads_of(bias.shape)],
        [
            pltpu.VMEM((rows, d), BF16),
            pltpu.VMEM((rows, half), BF16),
            pltpu.VMEM((rows, 3 * half), BF16),
            pltpu.VMEM((rows, d), F32),
        ],
        "attn_back",
        6 * 10**9,
    )
    vec_grad = jnp.concatenate(
        [
            top_sums[4:6],
            top_sums[2:4],
            top_sums[0:2],
            low_sums[2:4],
            low_sums[0:2],
            upb.reshape(4, d),
        ],
        axis=0,
    )
    return g, (g_attn, g_up, g_down), vec_grad, rel


def strip_constant(side):
    width = 2 * side - 1
    wide = -(-(width * side) // 128) * 128
    out = np.zeros((width * width, 16, wide), np.float32)
    for c in range(side):
        for k in range(width):
            for e in range(side):
                out[width * k + side - 1 - c + e, c, k * side + e] = 1.0
    return out.reshape(width * width, 16 * wide), wide


def split_three(v):
    high = lax.reduce_precision(v, 8, 7)
    rest = v - high
    mid = lax.reduce_precision(rest, 8, 7)
    return jnp.concatenate([high, mid, rest - mid], axis=0).astype(BF16)


def add_three(v):
    n = v.shape[0] // 3
    return v[:n] + v[n : 2 * n] + v[2 * n :]


def expand_kernel(side, strips, ends, out):
    def head(h, _):
        expand_head(side, strips, ends, out, h)
        return 0

    lax.fori_loop(0, out.shape[0], head, 0)


def expand_head(side, strips, ends, out, h):
    lp = out.shape[1]
    wide = strips.shape[2]
    tokens = side * side + 1
    a = strips[h]
    lane = lax.broadcasted_iota(jnp.int32, (1, lp), 1)
    row_end, col_end, corner = ends[h, 0:1, 0:1], ends[h, 0:1, 1:2], ends[h, 0:1, 2:3]
    top = jnp.where(lane == 0, corner, row_end)
    out[h, 0:1, :] = jnp.where(lane < tokens, top, BIG)
    for r in range(side):
        shift = (side - 1 - r) * side - 1
        moved = pltpu.roll(a, (wide - shift) % wide, 1)[:side, :lp]
        moved = jnp.where(lane == 0, col_end, moved)
        out[h, 1 + r * side : 1 + (r + 1) * side, :] = jnp.where(lane < tokens, moved, BIG)
    tail = jnp.where(lane < tokens, 0.0, BIG)
    out[h, tokens:, :] = jnp.broadcast_to(tail, (lp - tokens, lp))


def expand_bias(position, side, lp):
    layers, heads, entries = position.shape
    flat = position.reshape(layers * heads, entries)
    hot, wide = strip_constant(side)
    cells = hot.shape[0]
    strips = add_three(dot_nn(split_three(flat[:, :cells][:, ::-1]), jnp.asarray(hot, BF16)))
    strips = strips.reshape(layers * heads, 16, wide)
    ends = jnp.pad(flat[:, cells:], ((0, 0), (0, 125)))[:, None, :]
    found = []
    for l in range(layers):
        own = slice(l * heads, (l + 1) * heads)
        found.append(
            pl.pallas_call(
                functools.partial(expand_kernel, side),
                out_shape=jax.ShapeDtypeStruct((heads, lp, lp), F32),
                grid=(heads // 6,),
                in_specs=[
                    pl.BlockSpec((6, 16, wide), lambda i: (i, 0, 0)),
                    pl.BlockSpec((6, 1, 128), lambda i: (i, 0, 0)),
                ],
                out_specs=pl.BlockSpec((6, lp, lp), lambda i: (i, 0, 0)),
                name="expand",
            )(strips[own], ends[own])
        )
    return found


def fold_kernel(side, grads, strips, ends):
    def head(h, _):
        fold_head(side, grads, strips, ends, h)
        return 0

    lax.fori_loop(0, grads.shape[0], head, 0)


def fold_head(side, grads, strips, ends, h):
    lp = grads.shape[1]
    wide = strips.shape[2]
    tokens = side * side + 1
    lane = lax.broadcasted_iota(jnp.int32, (1, lp), 1)
    total = jnp.zeros((16, wide), F32)
    for r in range(side):
        shift = (side - 1 - r) * side - 1
        part = jnp.where(lane == 0, 0.0, grads[h, 1 + r * side : 1 + (r + 1) * side, :])
        part = jnp.concatenate([part, jnp.zeros((16 - side, lp), F32)], axis=0)
        part = jnp.concatenate([part, jnp.zeros((16, wide - lp), F32)], axis=1)
        total = total + pltpu.roll(part, shift % wide, 1)
    strips[h] = total
    corner = grads[h, 0:1, 0:1]
    row_end = jnp.sum(grads[h, 0:1, :], axis=1, keepdims=True) - corner
    col_end = jnp.sum(grads[h, 1:tokens, 0:1], axis=0, keepdims=True)
    out_lane = lax.broadcasted_iota(jnp.int32, (1, 128), 1)
    ends[h] = jnp.where(
        out_lane == 0, row_end, jnp.where(out_lane == 1, col_end, jnp.where(out_lane == 2, corner, 0.0))
    )


def fold_bias(layers, side):
    hot, wide = strip_constant(side)
    found = []
    for grads in layers:
        n, lp, _ = grads.shape
        found.append(
            pl.pallas_call(
                functools.partial(fold_kernel, side),
                out_shape=[
                    jax.ShapeDtypeStruct((n, 16, wide), F32),
                    jax.ShapeDtypeStruct((n, 1, 128), F32),
                ],
                grid=(n // 6,),
                in_specs=[pl.BlockSpec((6, lp, lp), lambda i: (i, 0, 0))],
                out_specs=[
                    pl.BlockSpec((6, 16, wide), lambda i: (i, 0, 0)),
                    pl.BlockSpec((6, 1, 128), lambda i: (i, 0, 0)),
                ],
                name="fold",
            )(grads)
        )
    strips = jnp.concatenate([f[0].reshape(-1, 16 * wide) for f in found], axis=0)
    ends = jnp.concatenate([f[1][:, 0, :3] for f in found], axis=0)
    cells = add_three(dot_nt(split_three(strips), jnp.asarray(hot, BF16)))
    flat = jnp.concatenate([cells[:, ::-1], ends], axis=1)
    return flat.reshape(len(layers), -1, flat.shape[1])


def adamw_update(master, gradient, first_mom, second_mom, step_rate, decay_rate):
    first_mom = beta_one * first_mom + (1.0 - beta_one) * gradient
    second_mom = beta_two * second_mom + (1.0 - beta_two) * gradient * gradient
    step_dir = (
        first_mom
        / (1.0 - beta_one**STEP)
        / (jnp.sqrt(second_mom / (1.0 - beta_two**STEP)) + adam_eps)
    )
    return (master - step_rate * (step_dir + decay_rate * master), first_mom, second_mom)


def update_kernel(layers, *refs):
    grads, refs = refs[: 3 * layers + 2], refs[3 * layers + 2 :]
    olds, news, copies = refs[:18], refs[18:36], refs[36:]

    def put(item, index, gradient, rate):
        old = [olds[3 * item + k][index] for k in range(3)]
        found = adamw_update(old[0], gradient, old[1], old[2], rate, decay_matrix)
        for k in range(3):
            news[3 * item + k][index] = found[k]
        if item >= 2:
            copies[item - 2][index] = found[0].astype(BF16)

    put(0, slice(None), grads[3 * layers + 1][...], rate_table)
    put(1, slice(None), grads[3 * layers][...], rate_matrix)
    for l in range(layers):
        attn, up, down = grads[3 * l : 3 * l + 3]
        half = attn.shape[1] // 4
        for k in range(3):
            put(2, (l, k), attn[:, k * half : (k + 1) * half], rate_matrix)
        put(3, l, attn[:, 3 * half :], rate_matrix)
        put(4, l, up[...], rate_matrix)
        put(5, l, down[...], rate_matrix)


def update_all(grads, olds):
    layers = (len(grads) - 2) // 3
    rows = grads[0].shape[0]
    block = 16 if rows % 16 == 0 else rows

    def spec(a):
        n = len(a.shape)
        return pl.BlockSpec(
            tuple(a.shape[:-2]) + (block, a.shape[-1]), lambda i: (0,) * (n - 2) + (i, 0)
        )

    outs = [jax.ShapeDtypeStruct(a.shape, F32) for a in olds]
    outs += [jax.ShapeDtypeStruct(olds[3 * k].shape, BF16) for k in range(2, 6)]
    return pl.pallas_call(
        functools.partial(update_kernel, layers),
        out_shape=outs,
        grid=(rows // block,),
        in_specs=[spec(a) for a in list(grads) + list(olds)],
        out_specs=[spec(a) for a in outs],
        compiler_params=pltpu.CompilerParams(vmem_limit_bytes=56 * 2**20),
        name="update",
    )(*grads, *olds)


def pack_layer(in_proj, out_proj, up_proj, down_proj):
    return jnp.concatenate(
        [in_proj[:, 0], in_proj[:, 1], in_proj[:, 2], out_proj, up_proj, down_proj], axis=1
    )


MESH = pl.DeviceIdType.MESH


def place():
    dp = lax.axis_index("dp")
    return lax.axis_index("tensor"), dp // 4, lax.rem(dp // 2, 2), lax.rem(dp, 2)


def at(x, z, y, c):
    return ((z * 2 + y) * 2 + c, x)


def near(v, step, size):
    return lax.rem(v + step, size)


def greet(peers):
    barrier = pltpu.get_barrier_semaphore()
    for peer in peers:
        pl.semaphore_signal(barrier, inc=1, device_id=peer, device_id_type=MESH)
    pl.semaphore_wait(barrier, len(peers))


def gather_kernel(wide, *refs):
    n = len(wide)
    srcs, dsts = refs[:n], refs[n : 2 * n]
    own_sem, send_sem, recv_sem = refs[2 * n :]
    x, z, y, c = place()
    peer_x, peer_y, peer_c = at(1 - x, z, y, c), at(x, z, 1 - y, c), at(x, z, y, 1 - c)
    up, down = at(x, jnp.minimum(z + 1, 3), y, c), at(x, jnp.maximum(z - 1, 0), y, c)
    barrier = pltpu.get_barrier_semaphore()
    for peer in (peer_x, peer_y, peer_c):
        pl.semaphore_signal(barrier, inc=1, device_id=peer, device_id_type=MESH)

    @pl.when(z < 3)
    def _():
        pl.semaphore_signal(barrier, inc=1, device_id=up, device_id_type=MESH)

    @pl.when(z > 0)
    def _():
        pl.semaphore_signal(barrier, inc=1, device_id=down, device_id_type=MESH)

    pl.semaphore_wait(barrier, 3 + jnp.where(z < 3, 1, 0) + jnp.where(z > 0, 1, 0))

    def slot(i, ox, oz, oy, oc):
        ref = dsts[i]
        dp = (oz * 2 + oy) * 2 + oc
        return ref.at[ox, dp] if wide[i] else ref.at[dp]

    Z, Y, X, C, Z2 = 0, 4, 8, 16, 32

    def make(i, src, origin, way, peer, two=False):
        ox, oz, oy, oc = origin
        if way == Z:
            k = Z + oz
        elif way == Y:
            k = Y + oz
        elif way == X:
            k = X + oy * 4 + oz
        else:
            k = C + (ox * 2 + oy) * 4 + oz
        return pltpu.make_async_remote_copy(
            src_ref=src,
            dst_ref=slot(i, *origin),
            send_sem=send_sem.at[i, Z2 if two else k],
            recv_sem=recv_sem.at[i, k],
            device_id=peer,
            device_id_type=MESH,
        )

    own = (x, z, y, c)
    locals_ = []
    for i in range(n):
        copy = pltpu.make_async_copy(srcs[i], slot(i, *own), own_sem.at[i])
        copy.start()
        locals_.append(copy)

    def spread(i, src, origin, ways):
        for way, peer in ((Y, peer_y), (X, peer_x), (C, peer_c)):
            if way in ways and (wide[i] or way != X):
                make(i, src, origin, way, peer).start()

    def begin(i):
        src = srcs[i]

        @pl.when(z < 3)
        def _():
            make(i, src, own, Z, up).start()

        @pl.when(z > 0)
        def _():
            make(i, src, own, Z, down, True).start()

        spread(i, src, own, (Y, X, C))

    def each_z(fn):
        for k in (1, 2, 3):
            pl.when(z - k >= 0)(functools.partial(fn, z - k, True))
            pl.when(z + k <= 3)(functools.partial(fn, z + k, False))

    def landed(i, origin, way, peer):
        ref = slot(i, *origin)
        make(i, ref, origin, way, peer).wait_recv()
        return ref

    def after_z(i):
        def one(oz, rising):
            origin = (x, oz, y, c)
            ref = landed(i, origin, Z, up)
            if rising:

                @pl.when(z < 3)
                def _():
                    make(i, ref, origin, Z, up).start()
            else:

                @pl.when(z > 0)
                def _():
                    make(i, ref, origin, Z, down).start()

            spread(i, ref, origin, (Y, X, C))

        each_z(one)

    def after_y(i):
        def one(oz, rising):
            origin = (x, oz, 1 - y, c)
            spread(i, landed(i, origin, Y, peer_y), origin, (X, C))

        one(z, True)
        each_z(one)

    def after_x(i):
        for oy in (y, 1 - y):

            def one(oz, rising):
                origin = (1 - x, oz, oy, c)
                spread(i, landed(i, origin, X, peer_x), origin, (C,))

            one(z, True)
            each_z(one)

    AHEAD = 1
    for i in range(min(AHEAD, n)):
        begin(i)
    for i in range(n + 2):
        if i + AHEAD < n:
            begin(i + AHEAD)
        if i < n:
            after_z(i)
        if 0 <= i - 1 < n:
            after_y(i - 1)
        if 0 <= i - 2 < n and wide[i - 2]:
            after_x(i - 2)
    for i in range(n):
        for ox in (0, 1) if wide[i] else (x,):
            for oy in (0, 1):
                for oz in range(4):
                    landed(i, (ox, oz, oy, 1 - c), C, peer_c)
                    make(i, slot(i, ox, oz, oy, c), (ox, oz, oy, c), C, peer_c).wait_send()
        for oz in range(4):
            make(i, slot(i, x, oz, y, c), (x, oz, y, c), Y, peer_y).wait_send()
        if wide[i]:
            for oy in (0, 1):
                for oz in range(4):
                    make(i, slot(i, x, oz, oy, c), (x, oz, oy, c), X, peer_x).wait_send()

        def sent(oz, rising):
            origin = (x, oz, y, c)
            pl.when(z < 3 if rising else z > 0)(
                lambda: make(i, slot(i, *origin), origin, Z, up).wait_send()
            )

        each_z(sent)
        pl.when(z < 3)(lambda: make(i, srcs[i], own, Z, up).wait_send())
        pl.when(z > 0)(lambda: make(i, srcs[i], own, Z, down, True).wait_send())
        locals_[i].wait()


def gather_all(shards, wide, cid):
    n = len(shards)
    outs = [
        jax.ShapeDtypeStruct(((2, 16) if w else (16,)) + s.shape, s.dtype)
        for s, w in zip(shards, wide)
    ]
    any_ = pl.BlockSpec(memory_space=pl.ANY)
    return pl.pallas_call(
        functools.partial(gather_kernel, wide),
        out_shape=outs,
        in_specs=[any_] * n,
        out_specs=[any_] * n,
        scratch_shapes=[
            pltpu.SemaphoreType.DMA((n,)),
            pltpu.SemaphoreType.DMA((n, 33)),
            pltpu.SemaphoreType.DMA((n, 33)),
        ],
        compiler_params=pltpu.CompilerParams(collective_id=cid, has_side_effects=True),
        name="gather",
    )(*shards)


RING = 3


def reduce_kernel(nw, nt, *refs):
    srcs, small = refs[: nw + nt], refs[nw + nt]
    outs, small_out = refs[nw + nt + 1 : 2 * (nw + nt) + 1], refs[2 * (nw + nt) + 1]
    accw, rcw, rxw, ryw, rzw, acct, rct, ryt, rzt, tot, rsm = refs[2 * (nw + nt) + 2 : -3]
    send_sem, recv_sem, free_sem = refs[-3:]
    x, z, y, c = place()
    zs = [near(z, k, 4) for k in (1, 2, 3)]
    peer_x, peer_y, peer_c = at(1 - x, z, y, c), at(x, z, 1 - y, c), at(x, z, y, 1 - c)
    greet([at(x, k, y, c) for k in zs] + [peer_x, peer_y, peer_c])
    counts = [0]

    def remote(src, dst, peer):
        k = counts[0]
        counts[0] += 1
        copy = pltpu.make_async_remote_copy(
            src_ref=src,
            dst_ref=dst,
            send_sem=send_sem.at[k],
            recv_sem=recv_sem.at[k],
            device_id=peer,
            device_id_type=MESH,
        )
        copy.start()
        return copy

    def local(src, dst):
        k = counts[0]
        counts[0] += 1
        copy = pltpu.make_async_copy(src, dst, send_sem.at[k])
        copy.start()
        return copy

    rw, rt = accw.shape[-2], acct.shape[-2]
    wide = [(i, j) for i in range(nw) for j in range(0, srcs[0].shape[-2], rw)]
    slim = [(nw + i, j) for i in range(nt) for j in range(0, srcs[nw].shape[-2], rt)]

    def group(kind, chunk, gx, gy, gc):
        i, j = chunk
        rows = pl.ds(j, rw if kind == "w" else rt)
        if kind == "w":
            return srcs[i].at[gx, :, gy, gc, rows, :]
        return srcs[i].at[:, gy, gc, rows, :]

    def groups(kind):
        if kind == "w":
            return [(1 - x, 1 - y), (1 - x, y), (x, 1 - y), (x, y)]
        return [(0, 1 - y), (0, y)]

    bufs = {"w": (accw, rcw, rxw, ryw, rzw), "t": (acct, rct, None, ryt, rzt)}
    chunks = {"w": wide, "t": slim}
    state = {}
    pending = []

    def add_into(dst, other):
        def body(k, _):
            dst[k] = dst[k] + other[k]
            return 0

        lax.fori_loop(0, dst.shape[0], body, 0)

    def fetch(kind, k):
        acc, rc = bufs[kind][:2]
        items = []
        if k >= RING:
            pl.semaphore_wait(free_sem.at[0 if kind == "w" else 1], 1)
        for g, (gx, gy) in enumerate(groups(kind)):
            mine = local(group(kind, chunks[kind][k], gx, gy, c), acc.at[k, g])
            other = remote(group(kind, chunks[kind][k], gx, gy, 1 - c), rc.at[k % RING, g], peer_c)
            items.append((mine, other))
        state[kind, k] = items

    def core_sum(kind, k):
        acc, rc, rx, ry, _ = bufs[kind]
        sent = []
        for g, (mine, other) in enumerate(state[kind, k]):
            mine.wait()
            other.wait_recv()
            pending.append(other)
            add_into(acc.at[k, g], rc.at[k % RING, g])
            if kind == "w" and g < 2:
                sent.append(remote(acc.at[k, g], rx.at[k, g], peer_x))
            if kind == "t" and g == 0:
                sent.append(remote(acc.at[k, g], ry.at[k], peer_y))
        if k + RING < len(chunks[kind]):
            pl.semaphore_signal(
                free_sem.at[0 if kind == "w" else 1], inc=1, device_id=peer_c, device_id_type=MESH
            )
        state[kind, k] = sent

    def after_x(k):
        sent = state["w", k]
        for g in range(2):
            sent[g].wait_recv()
            pending.append(sent[g])
            add_into(accw.at[k, 2 + g], rxw.at[k, g])
            if g == 0:
                state["w", k] = [remote(accw.at[k, 2], ryw.at[k], peer_y)]

    def after_y(kind, k):
        acc, _, _, ry, rz = bufs[kind]
        last = 3 if kind == "w" else 1
        copy = state[kind, k][0]
        copy.wait_recv()
        pending.append(copy)
        add_into(acc.at[k, last], ry.at[k])
        state[kind, k] = [
            remote(acc.at[k, last, zs[s]], rz.at[k, 2 - s], at(x, zs[s], y, c)) for s in range(3)
        ]

    def after_z(kind, k):
        acc, _, _, _, rz = bufs[kind]
        last = 3 if kind == "w" else 1
        total = acc[k, last, z].astype(F32)
        for s in range(3):
            state[kind, k][s].wait_recv()
            pending.append(state[kind, k][s])
        for s in range(3):
            total = total + rz[k, s].astype(F32)
        i, j = chunks[kind][k]
        outs[i][j : j + total.shape[0], :] = total

    tot[0] = small[...]
    flips = [peer_c, peer_x, peer_y]
    flips += [at(x, z + 1 - 2 * lax.rem(z, 2), y, c), at(x, lax.rem(z + 2, 4), y, c)]
    small_state = []

    def small_step(s):
        if s > 0:
            copy = small_state[-1]
            copy.wait_recv()
            pending.append(copy)
            tot[s] = tot[s - 1] + rsm[s - 1]
        if s < len(flips):
            small_state.append(remote(tot.at[s], rsm.at[s], flips[s]))

    n, m = len(wide), len(slim)
    fetch("w", 0)
    fetch("t", 0)
    for k in range(n + 5):
        if k + 1 < n:
            fetch("w", k + 1)
        if k < n:
            core_sum("w", k)
        for i in range(2 * k, min(2 * k + 2, m)):
            if i + 1 < m:
                fetch("t", i + 1)
            core_sum("t", i)
        if k <= len(flips):
            small_step(k)
        if 0 <= k - 1 < n:
            after_x(k - 1)
        for i in range(max(2 * k - 2, 0), min(2 * k, m)):
            after_y("t", i)
        if 0 <= k - 2 < n:
            after_y("w", k - 2)
        for i in range(max(2 * k - 4, 0), max(min(2 * k - 2, m), 0)):
            after_z("t", i)
        if 0 <= k - 3 < n:
            after_z("w", k - 3)
    small_out[...] = tot[len(flips)]
    for copy in pending:
        copy.wait_send()


def reduce_all(wide, slim, small, cid):
    nw, nt = len(wide), len(slim)
    rows, cw = wide[0].shape[-2:]
    ct = slim[0].shape[-1]
    kw, kt = nw, nt * rows // 16
    outs = [jax.ShapeDtypeStruct((rows, a.shape[-1]), F32) for a in wide + slim]
    outs.append(jax.ShapeDtypeStruct(small.shape, F32))
    copies = kw * (8 + 2 + 1 + 3) + kt * (4 + 1 + 3) + 5
    any_ = pl.BlockSpec(memory_space=pl.ANY)
    vm = pl.BlockSpec(memory_space=pltpu.VMEM)
    return pl.pallas_call(
        functools.partial(reduce_kernel, nw, nt),
        out_shape=outs,
        in_specs=[any_] * (nw + nt) + [vm],
        out_specs=[vm] * (nw + nt + 1),
        scratch_shapes=[
            pltpu.VMEM((kw, 4, 4, rows, cw), BF16),
            pltpu.VMEM((RING, 4, 4, rows, cw), BF16),
            pltpu.VMEM((kw, 2, 4, rows, cw), BF16),
            pltpu.VMEM((kw, 4, rows, cw), BF16),
            pltpu.VMEM((kw, 3, rows, cw), BF16),
            pltpu.VMEM((kt, 2, 4, 16, ct), BF16),
            pltpu.VMEM((RING, 2, 4, 16, ct), BF16),
            pltpu.VMEM((kt, 4, 16, ct), BF16),
            pltpu.VMEM((kt, 3, 16, ct), BF16),
            pltpu.VMEM((6,) + small.shape, F32),
            pltpu.VMEM((5,) + small.shape, F32),
            pltpu.SemaphoreType.DMA((copies,)),
            pltpu.SemaphoreType.DMA((copies,)),
            pltpu.SemaphoreType.REGULAR((2,)),
        ],
        compiler_params=pltpu.CompilerParams(
            collective_id=cid, has_side_effects=True, vmem_limit_bytes=62 * 2**20
        ),
        name="reduce",
    )(*wide, *slim, small)


def gather_plain(shards, wide):
    full = [lax.all_gather(s, "dp") for s in shards]
    return [lax.all_gather(f, "tensor") if w else f for f, w in zip(full, wide)]


def reduce_plain(wide, slim, small):
    outs = []
    for grads in wide:
        part = lax.psum_scatter(grads, "tensor", scatter_dimension=0, tiled=False)
        outs.append(lax.psum_scatter(part, "dp", scatter_dimension=0, tiled=False).astype(F32))
    for grads in slim:
        outs.append(lax.psum_scatter(grads, "dp", scatter_dimension=0, tiled=False).astype(F32))
    outs.append(lax.psum(small, ("dp", "tensor")))
    return outs


def local(
    token_codes,
    mask_slots,
    mask_counts,
    embedding,
    emb_first,
    emb_second,
    readout,
    read_first,
    read_second,
    in_proj,
    in_first,
    in_second,
    out_proj,
    out_first,
    out_second,
    up_proj,
    up_first,
    up_second,
    down_proj,
    down_first,
    down_second,
    vectors,
    vec_first,
    vec_second,
    position,
    pos_first,
    pos_second,
):
    tensor_at = lax.axis_index("tensor")
    tensor_size = lax.axis_size("tensor")
    seqs, patches = token_codes.shape
    side = math.isqrt(patches)
    tokens = patches + 1
    lp = -(-tokens // 16) * 16
    slots = mask_slots.shape[1]
    mine = seqs // tensor_size
    layers = in_proj.shape[0]
    tail = vectors.shape[0] - 4
    half_vocab = embedding.shape[0]
    vocab_start = tensor_at * half_vocab
    d = vectors.shape[1]

    live_slot = jnp.arange(slots)[None, :] < mask_counts[:, None]
    hits = (mask_slots[:, :, None] == jnp.arange(patches)[None, None, :])
    masked = jnp.any(hits & live_slot[:, :, None], axis=1)
    targets = jnp.sum(jnp.where(hits, token_codes[:, None, :], 0), axis=2)
    count_here = jnp.sum(mask_counts.astype(F32))
    dp_size = lax.axis_size("dp")
    custom = dp_size == 16 and tensor_size == 2

    shards = [
        pack_layer(in_proj[l], out_proj[l], up_proj[l], down_proj[l]).astype(BF16)
        for l in range(layers)
    ]
    peer_at = 1 - tensor_at

    def swap(value):
        return lax.ppermute(value, "tensor", [(0, 1), (1, 0)])

    def side_of(value, where):
        return lax.dynamic_slice_in_dim(value, where * mine, mine, 0)

    code_rows = jnp.where(masked, -1, token_codes - vocab_start)
    code_rows = jnp.pad(code_rows, ((0, 0), (1, lp - tokens)), constant_values=-1)
    codes = jnp.arange(half_vocab)[None, :]
    peer_hot = (side_of(code_rows, peer_at).reshape(-1, 1) == codes).astype(BF16)
    own_hot = (side_of(code_rows, tensor_at).reshape(-1, 1) == codes).astype(BF16)
    biases = expand_bias(position, side, lp)
    first_shard, biases, peer_hot, own_hot = lax.optimization_barrier(
        (shards[0], biases, peer_hot, own_hot)
    )
    sources = [first_shard, jnp.full((8, 128), count_here), embedding.T.astype(BF16)]
    wide = (True, False, False)
    found = gather_all(sources, wide, 1) if custom else gather_plain(sources, wide)
    mask_total = jnp.sum(found[1][:, 0, 0])
    weights = [found[0].reshape(2, d, -1)]
    emb_table = found[2].reshape(d, half_vocab)
    weights.append(lax.all_gather(shards[1], ("tensor", "dp")).reshape(2, d, -1))
    read_table = lax.all_gather(readout.T.astype(BF16), "dp").reshape(d, half_vocab)

    came = swap(dot_nt(peer_hot, emb_table).astype(BF16))
    own_part = lax.optimization_barrier(dot_nt(own_hot, emb_table).astype(BF16))
    summed = own_part.astype(F32) + came.astype(F32)
    my_masked = side_of(masked, tensor_at)
    mask_flag = jnp.pad(my_masked.astype(F32), ((0, 0), (1, lp - tokens))).reshape(-1, 1)
    lead_flag = jnp.zeros((mine, lp), F32).at[:, 0].set(1.0).reshape(-1, 1)
    x = summed + lead_flag * vectors[tail] + mask_flag * vectors[tail + 1]

    kept = []
    for l in range(layers):
        x, saved = forward_layer(x, weights[l], vectors[14 * l : 14 * l + 14], biases[l], mine)
        kept.append(saved)

    my_slots = side_of(mask_slots, tensor_at)
    pick = (jnp.arange(mine)[:, None] * lp + 1 + my_slots).reshape(-1)
    final_in = x[pick]
    unit, _ = norm_parts(final_in)
    u = (unit * vectors[tail + 2] + vectors[tail + 3]).astype(BF16)
    u_peer = swap(u)
    places = [tensor_at, peer_at]
    logits, stats, target_hot = [], [], []
    for rows, where in zip((u, u_peer), places):
        lg = dot_nn(rows, read_table)
        hot = codes == (side_of(targets, where).reshape(-1) - vocab_start)[:, None]
        peak = jnp.max(lg, axis=1)
        total = jnp.sum(jnp.exp(lg - peak[:, None]), axis=1)
        chosen = jnp.sum(jnp.where(hot, lg, 0.0), axis=1)
        logits.append(lg)
        target_hot.append(hot)
        stats.append(jnp.stack([peak, total, chosen]))
    both = jnp.stack(stats)
    other = swap(both)[::-1]
    top = jnp.maximum(both[:, 0], other[:, 0])
    log_total = top + jnp.log(
        both[:, 1] * jnp.exp(both[:, 0] - top) + other[:, 1] * jnp.exp(other[:, 0] - top)
    )
    weight_row = live_slot.astype(F32)
    weights_of = [side_of(weight_row, where).reshape(-1) for where in places]
    losses = log_total - both[:, 2] - other[:, 2]
    loss_here = jnp.sum(losses * jnp.stack(weights_of))
    g_logits = [
        ((jnp.exp(logits[i] - log_total[i][:, None]) - target_hot[i].astype(F32)) * (weights_of[i] / mask_total)[:, None]).astype(BF16)
        for i in range(2)
    ]
    came = swap(dot_nt(g_logits[1], read_table).astype(BF16))
    grad_read = dot_tn(jnp.concatenate([u, u_peer]), jnp.concatenate(g_logits))
    grad_final = dot_nt(g_logits[0], read_table).astype(BF16).astype(F32) + came.astype(F32)
    back, g_gain, g_shift = norm_back(grad_final, final_in, vectors[tail + 2])
    g = jnp.zeros_like(x).at[pick].add(back)

    mat_grads = [None] * layers
    vec_grads = [None] * layers
    rel_grads = [None] * layers
    for l in reversed(range(layers)):
        g, full, vec_grads[l], rel = backward_layer(
            g, kept[l], weights[l], vectors[14 * l : 14 * l + 14], biases[l], mine
        )
        mat_grads[l] = full
        rel_grads[l] = rel

    g0 = g.astype(BF16)
    g0, rel_grads[0], rel_grads[1] = lax.optimization_barrier((g0, rel_grads[0], rel_grads[1]))
    grad_lead = jnp.sum(g0.astype(F32) * lead_flag, axis=0)
    grad_mask = jnp.sum(g0.astype(F32) * mask_flag, axis=0)
    g0_peer = swap(g0)
    grad_emb = dot_tn(
        jnp.concatenate([g0, g0_peer]), jnp.concatenate([own_hot, peer_hot])
    )
    vec_local = jnp.concatenate(
        vec_grads + [jnp.stack([grad_lead, grad_mask, g_gain, g_shift])], axis=0
    )
    small_parts = [vec_local, fold_bias(rel_grads, side), loss_here / tensor_size]
    flat = jnp.concatenate([p.reshape(-1) for p in small_parts])
    flat = jnp.pad(flat, (0, -flat.size % 1024)).reshape(-1, 128)
    if custom:
        lead = (4, 2, 2, d // 16)
        reduced = reduce_all(
            [m.reshape((2,) + lead + m.shape[-1:]) for layer in mat_grads for m in layer],
            [m.astype(BF16).reshape(lead + m.shape[-1:]) for m in (grad_read, grad_emb)],
            flat,
            2,
        )
    else:
        lead = (dp_size, d // dp_size)
        reduced = reduce_plain(
            [m.reshape((2,) + lead + m.shape[-1:]) for layer in mat_grads for m in layer],
            [m.astype(BF16).reshape(lead + m.shape[-1:]) for m in (grad_read, grad_emb)],
            flat,
        )
    flat = reduced[-1]
    flat = flat.reshape(-1)
    vec_all = flat[: vectors.size].reshape(vectors.shape)
    rel_all = flat[vectors.size : vectors.size + position.size].reshape(position.shape)
    loss_sum = flat[vectors.size + position.size]

    tables = [a.T for a in (embedding, emb_first, emb_second, readout, read_first, read_second)]
    ins = [a.transpose(0, 2, 1, 3) for a in (in_proj, in_first, in_second)]
    others = [
        out_proj,
        out_first,
        out_second,
        up_proj,
        up_first,
        up_second,
        down_proj,
        down_first,
        down_second,
    ]
    new = update_all(list(reduced[:-1]), tables + ins + others)
    tables = tuple(a.T for a in new[:6])
    ins = tuple(a.transpose(0, 2, 1, 3) for a in new[6:9])
    copies = (new[18].transpose(0, 2, 1, 3),) + tuple(new[19:])
    vec_new = adamw_update(vectors, vec_all, vec_first, vec_second, rate_vector, 0.0)
    pos_new = adamw_update(position, rel_all, pos_first, pos_second, rate_vector, 0.0)
    return (
        (loss_sum, mask_total) + tables + ins + tuple(new[9:18]) + vec_new + pos_new + copies
    )


def solution(mesh):
    table = P("tensor", "dp")
    in_spec = P(None, "dp", None, "tensor")
    mat = P(None, "dp", "tensor")
    return jax.shard_map(
        local,
        mesh=mesh,
        in_specs=(P("dp", None), P("dp", None), P("dp"))
        + (table,) * 6
        + (in_spec,) * 3
        + (mat,) * 9
        + (P(),) * 6,
        out_specs=(P(), P())
        + (table,) * 6
        + (in_spec,) * 3
        + (mat,) * 9
        + (P(),) * 6
        + (in_spec, mat, mat, mat),
        check_vma=False,
    )
```
